128 devices in a mesh: dp: 32 (over z_hi, x, y), tensor: 4 (over z_lo, core).
Axes of the slice: x: 4, y: 4, z: 4 (z_hi: 2, z_lo: 2; z = z_hi * 2 + z_lo), core: 2. Of those that a mesh axis runs over, the one named last changes fastest.
Arguments:
- tokens: bfloat16 [16384, 1536], P(('dp', 'tensor')), may hold values from -6 to 6
- query_weight: bfloat16 [2, 1536, 1536], P(None, 'dp', 'tensor'), may hold values from -0.15625 to 0.15625
- key_weight: bfloat16 [2, 1536, 768], P(None, 'dp', 'tensor'), may hold values from -0.15625 to 0.15625
- value_weight: bfloat16 [2, 1536, 768], P(None, 'dp', 'tensor'), may hold values from -0.15625 to 0.15625
- out_weight: bfloat16 [2, 1536, 1536], P(None, 'tensor', 'dp'), may hold values from -1.25 to 1.25
- gate_weight: bfloat16 [2, 1536, 4096], P(None, 'dp', 'tensor'), may hold values from -0.15625 to 0.15625
- up_weight: bfloat16 [2, 1536, 4096], P(None, 'dp', 'tensor'), may hold values from -0.15625 to 0.15625
- down_weight: bfloat16 [2, 4096, 1536], P(None, 'tensor', 'dp'), may hold values from -0.09375 to 0.09375
- norm_gains: bfloat16 [2, 2, 1536], P(None, None, 'dp'), may hold values from 0.5 to 1.5
- grad_out: bfloat16 [16384, 1536], P(('dp', 'tensor')), may hold values from -6 to 6
Outputs:
- output: bfloat16 [16384, 1536], P(('dp', 'tensor'))
- input_grad: float32 [16384, 1536], P(('dp', 'tensor'))
- query_grad: float32 [2, 1536, 1536], P(None, 'dp', 'tensor')
- key_grad: float32 [2, 1536, 768], P(None, 'dp', 'tensor')
- value_grad: float32 [2, 1536, 768], P(None, 'dp', 'tensor')
- out_proj_grad: float32 [2, 1536, 1536], P(None, 'tensor', 'dp')
- gate_grad: float32 [2, 1536, 4096], P(None, 'dp', 'tensor')
- up_grad: float32 [2, 1536, 4096], P(None, 'dp', 'tensor')
- down_grad: float32 [2, 4096, 1536], P(None, 'tensor', 'dp')
- gains_grad: float32 [2, 2, 1536], P(None, None, 'dp')
The draws below stay inside these ranges and needn't reach their ends.
All inputs are finite; a program needn't handle non-finite values.
Results may differ from the reference program's by a relative error of at most 0.04.
Values may be sent and summed in bfloat16 or wider, within the bound.
A program may use at most 192 MiB of HBM per device.

```python
import math
import jax
import jax.numpy as jnp
from jax import lax

D = 1536
NH = 16
KV = 8
HD = 96
FF = 4096
LAYERS = 2
SEQ = 512
TOKENS = 16384
N_DP = 32


def block_scale(rng, extent, cuts, low, largest):
    def one(axis_at, blocks):
        draws = jax.random.uniform(jax.random.fold_in(jax.random.fold_in(rng, 6), axis_at), (blocks,), jnp.float32, low / len(cuts), largest / len(cuts))
        return jnp.repeat(jnp.exp(draws), extent[axis_at] // blocks).reshape((-1,) + (1,) * (len(extent) - axis_at - 1))

    loudness = one(*cuts[0])
    for cut in cuts[1:]:
        loudness = loudness * one(*cut)
    return loudness


def noise(own_key, dims, deviation, reach, shards=(), kind=jnp.bfloat16):
    values = deviation * jax.random.normal(own_key, dims, jnp.float32)
    if shards:
        values = values * block_scale(own_key, dims, shards, -0.22, 0.18)
    return jnp.clip(values, -reach, reach).astype(kind)


def setup_inputs(seed: int = 0) -> dict:
    key_list = jax.random.split(jax.random.key(seed), 11)
    tokens = noise(key_list[0], (TOKENS, D), 1.0, 6.0, ((0, 128),))
    query_weight = noise(key_list[1], (LAYERS, D, NH * HD), D ** -0.5, 0.15625, ((1, 32), (2, 4)))
    key_weight = noise(key_list[2], (LAYERS, D, KV * HD), D ** -0.5, 0.15625, ((1, 32), (2, 4)))
    value_weight = noise(key_list[3], (LAYERS, D, KV * HD), D ** -0.5, 0.15625, ((1, 32), (2, 4)))
    out_weight = noise(key_list[4], (LAYERS, NH * HD, D), (NH * HD // 64) ** -0.5, 1.25, ((1, 4), (2, 32)))
    gate_weight = noise(key_list[5], (LAYERS, D, FF), D ** -0.5, 0.15625, ((1, 32), (2, 4)))
    up_weight = noise(key_list[6], (LAYERS, D, FF), D ** -0.5, 0.15625, ((1, 32), (2, 4)))
    down_weight = noise(key_list[7], (LAYERS, FF, D), FF ** -0.5, 0.09375, ((1, 4), (2, 32)))
    norm_gains = jnp.clip(1.0 + 0.1 * jax.random.normal(key_list[8], (LAYERS, 2, D), jnp.float32), 0.5, 1.5).astype(jnp.bfloat16)
    grad_out = noise(key_list[9], (TOKENS, D), 1.0, 6.0, ((0, 128),))
    return {"tokens": tokens, "query_weight": query_weight, "key_weight": key_weight, "value_weight": value_weight, "out_weight": out_weight, "gate_weight": gate_weight, "up_weight": up_weight, "down_weight": down_weight, "norm_gains": norm_gains, "grad_out": grad_out}


norm_eps = 1e-05
rope_base = 100000.0
highest = lax.Precision.HIGHEST

@jax.custom_vjp
def low(v):
    return lax.optimization_barrier(v.astype(jnp.bfloat16)).astype(jnp.float32)

@jax.custom_vjp
def low_back(v):
    return v

def low_keep(v):
    return (low(v), None)

def low_pass(kept, grad):
    return (grad,)

def back_keep(v):
    return (v, None)

def back_low(kept, grad):
    return (low(grad),)
low.defvjp(low_keep, low_pass)
low_back.defvjp(back_keep, back_low)

def rope_tables(seq_rows, head_width):
    half_width = head_width // 2
    position = jnp.arange(seq_rows, dtype=jnp.float32)[:, None]
    exponent = 2.0 * jnp.arange(half_width, dtype=jnp.float32) / head_width
    angles = position * (rope_base ** (-exponent))[None, :]
    return (jnp.cos(angles), jnp.sin(angles))

def rotate(values, cosine_table, sine_table):
    half_width = values.shape[-1] // 2
    first_half = values[..., :half_width]
    second_half = values[..., half_width:]
    cosine_wide = cosine_table[:, None, :]
    sine_wide = sine_table[:, None, :]
    return jnp.concatenate([first_half * cosine_wide - second_half * sine_wide, second_half * cosine_wide + first_half * sine_wide], axis=-1)

def rms_scaled(values, gain):
    return values * lax.rsqrt(lax.optimization_barrier(jnp.mean(values * values, axis=-1, keepdims=True)) + norm_eps) * gain

def project(values, weight):
    return jnp.einsum('bsi,ij->bsj', values, weight, precision=highest)

def attention(query_rows, key_rows, value_rows):
    batch_size, seq_rows, head_count, head_width = query_rows.shape
    kv_count = key_rows.shape[2]
    group_size = head_count // kv_count
    block_rows = min(512, seq_rows)
    block_count = seq_rows // block_rows
    scaling = 1.0 / math.sqrt(head_width)
    query_blocks = jnp.moveaxis(query_rows.reshape(batch_size, block_count, block_rows, kv_count, group_size, head_width), 1, 0)
    block_starts = jnp.arange(block_count, dtype=jnp.int32) * block_rows
    key_places = jnp.arange(seq_rows, dtype=jnp.int32)

    def one_block(inputs):
        query_part, block_start = inputs
        raw_scores = jnp.einsum('bqkgd,bskd->bkgqs', query_part, key_rows, precision=highest)
        scores = low_back(raw_scores * scaling)
        row_places = block_start + jnp.arange(block_rows, dtype=jnp.int32)
        allowed = row_places[:, None] >= key_places[None, :]
        scores = jnp.where(allowed, scores, -1e+30)
        row_peak = lax.optimization_barrier(jnp.max(scores, axis=-1, keepdims=True))
        exponent = jnp.exp(scores - row_peak)
        attn_weights = exponent / lax.optimization_barrier(jnp.sum(exponent, axis=-1, keepdims=True))
        return jnp.einsum('bkgqs,bskd->bqkgd', low(attn_weights), value_rows, precision=highest)
    outputs = lax.map(jax.checkpoint(one_block), (query_blocks, block_starts))
    return jnp.moveaxis(outputs, 0, 1).reshape(batch_size, seq_rows, head_count * head_width)

def block_layer(values, query_weight, key_weight, value_weight, out_weight, gate_weight, up_weight, down_weight, layer_gains, cosine_table, sine_table):
    batch_size, seq_rows, model_width = values.shape
    normed_first = low(rms_scaled(values, layer_gains[0]))
    query_rows = low_back(project(normed_first, query_weight)).reshape(batch_size, seq_rows, -1, HD)
    key_rows = low_back(project(normed_first, key_weight)).reshape(batch_size, seq_rows, -1, HD)
    value_rows = low(low_back(project(normed_first, value_weight))).reshape(batch_size, seq_rows, -1, HD)
    query_turned = low(rotate(query_rows, cosine_table, sine_table))
    key_turned = low(rotate(key_rows, cosine_table, sine_table))
    attended = low(low_back(attention(query_turned, key_turned, value_rows)))
    middle = values + low_back(project(attended, out_weight))
    normed_second = low(rms_scaled(middle, layer_gains[1]))
    gate_rows = low_back(project(normed_second, gate_weight))
    upward = low_back(project(normed_second, up_weight))
    hidden = low(jax.nn.silu(gate_rows) * upward)
    return middle + low_back(project(hidden, down_weight))

def forward(values, query_weight, key_weight, value_weight, out_weight, gate_weight, up_weight, down_weight, norm_gains):
    cosine_table, sine_table = rope_tables(values.shape[1], HD)
    for layer_index in range(LAYERS):
        values = block_layer(values, query_weight[layer_index], key_weight[layer_index], value_weight[layer_index], out_weight[layer_index], gate_weight[layer_index], up_weight[layer_index], down_weight[layer_index], norm_gains[layer_index], cosine_table, sine_table)
    return values

def reference(tokens, query_weight, key_weight, value_weight, out_weight, gate_weight, up_weight, down_weight, norm_gains, grad_out):
    weights = tuple((weight.astype(jnp.float32) for weight in (query_weight, key_weight, value_weight, out_weight, gate_weight, up_weight, down_weight, norm_gains)))
    group_seqs = math.gcd(N_DP, max(1, 4096 // SEQ))
    group_count = N_DP // group_seqs
    inputs = tokens.astype(jnp.float32).reshape(group_count, group_seqs, SEQ, D)
    cotangents = grad_out.astype(jnp.float32).reshape(group_count, group_seqs, SEQ, D)

    def accumulate(totals, pair_now):
        inputs_now, cotangent_now = pair_now
        outputs, pullback = jax.vjp(forward, inputs_now, *weights)
        gradients = pullback(cotangent_now)
        totals = tuple((running + fresh for running, fresh in zip(totals, gradients[1:])))
        return (totals, (outputs, gradients[0]))
    zero_grads = tuple((jnp.zeros(weight.shape, jnp.float32) for weight in weights))
    totals, (outputs, input_grads) = lax.scan(accumulate, zero_grads, (inputs, cotangents))
    return (outputs.reshape(TOKENS, D).astype(jnp.bfloat16), input_grads.reshape(TOKENS, D), totals[0], totals[1], totals[2], totals[3], totals[4], totals[5], totals[6], totals[7])
```

```python
import functools
import math

import jax
import jax.numpy as jnp
from jax import lax
from jax.experimental import pallas as pl
from jax.experimental.pallas import tpu as pltpu
from jax.sharding import PartitionSpec as P

HD = 96
MESH_IDS = pl.DeviceIdType.MESH
SIDE = 4


COLS = (384, 192, 192, 384, 1024, 1024, 1024)
WIDTH = 4224
HALVES = (((0, 1024), (1024, 2048)), ((2048, 3072), (3072, 4224)))


def here():
    dp = lax.axis_index("dp")
    tensor = lax.axis_index("tensor")
    return dp // 16, (dp // 4) % 4, dp % 4, tensor


def device(z_hi, x, y, tensor):
    return (z_hi * 16 + x * 4 + y, tensor)


def shift(place, step):
    return lax.rem(place + step + 2 * SIDE, SIDE)


def greet(targets):
    barrier = pltpu.get_barrier_semaphore()
    for target in targets:
        pl.semaphore_signal(barrier, inc=1, device_id=target, device_id_type=MESH_IDS)
    pl.semaphore_wait(barrier, len(targets))


class Wire:
    def __init__(self, send_sems, recv_sems):
        self.send_sems, self.recv_sems = send_sems, recv_sems
        self.count = 0
        self.sent = []

    def slot(self):
        self.count += 1
        return self.count - 1

    def send(self, slot, source, target_ref, target):
        copy = pltpu.make_async_remote_copy(
            src_ref=source,
            dst_ref=target_ref,
            send_sem=self.send_sems.at[slot],
            recv_sem=self.recv_sems.at[slot],
            device_id=target,
            device_id_type=MESH_IDS,
        )
        copy.start()
        self.sent.append(copy)

    def arrive(self, slot, landed, target):
        pltpu.make_async_remote_copy(
            src_ref=landed,
            dst_ref=landed,
            send_sem=self.send_sems.at[slot],
            recv_sem=self.recv_sems.at[slot],
            device_id=target,
            device_id_type=MESH_IDS,
        ).wait_recv()

    def drain(self):
        for copy in self.sent:
            copy.wait_send()
        self.sent = []


class Place:
    def __init__(self):
        self.z_hi, self.x, self.y, self.tensor = here()

    def beside(self, axis, step):
        if axis == "x":
            return device(self.z_hi, shift(self.x, step), self.y, self.tensor)
        return device(self.z_hi, self.x, shift(self.y, step), self.tensor)

    def across(self):
        return device(1 - self.z_hi, self.x, self.y, self.tensor)

    def greeted(self):
        return [
            self.beside("x", 1),
            self.beside("x", -1),
            self.beside("y", 1),
            self.beside("y", -1),
            self.across(),
        ]


def gather_job(wire, at, full, layer, z_data, own):
    parts = []
    for first, second, (left, right) in (("y", "x", HALVES[0]), ("x", "y", HALVES[1])):

        def block(first_step, second_step, cols, first=first):
            steps = {first: first_step}
            steps["x" if first == "y" else "y"] = second_step
            return full.at[
                layer,
                z_data,
                shift(at.x, steps["x"]),
                shift(at.y, steps["y"]),
                :,
                pl.ds(cols[0], cols[1] - cols[0]),
            ]

        def source(first_step, second_step, cols, block=block):
            if own is not None and first_step == 0 and second_step == 0:
                return own.at[layer, :, pl.ds(cols[0], cols[1] - cols[0])]
            return block(first_step, second_step, cols)

        parts.append(
            dict(
                first=first,
                second=second,
                left=left,
                right=right,
                whole=(left[0], right[1]),
                block=block,
                source=source,
                one={s: wire.slot() for s in (1, -1)},
                two={s: wire.slot() for s in (1, -1)},
                side={(f, s): wire.slot() for f in (0, -1, 1, 2) for s in (1, -1)},
                far={(f, s): wire.slot() for f in (0, -1, 1, 2) for s in (1, -1)},
            )
        )

    def one_start(part, step):
        wire.send(
            part["one"][step],
            part["source"](0, 0, part["whole"]),
            part["block"](0, 0, part["whole"]),
            at.beside(part["first"], step),
        )

    def side_start(part, first_step):
        for step in (1, -1):
            wire.send(
                part["side"][first_step, step],
                part["source"](first_step, 0, part["whole"]),
                part["block"](first_step, 0, part["whole"]),
                at.beside(part["second"], step),
            )

    def half(part, step):
        return part["left"] if step == 1 else part["right"]

    def one_done(part, step):
        target = at.beside(part["first"], step)
        wire.arrive(part["one"][step], part["block"](-step, 0, part["whole"]), target)
        piece = part["block"](-step, 0, half(part, step))
        wire.send(part["two"][step], piece, piece, target)

    def two_done(part):
        for step in (1, -1):
            piece = part["block"](2, 0, half(part, step))
            wire.arrive(part["two"][step], piece, at.beside(part["first"], step))

    def side_done(part, first_step):
        for step in (1, -1):
            target = at.beside(part["second"], step)
            wire.arrive(
                part["side"][first_step, step],
                part["block"](first_step, -step, part["whole"]),
                target,
            )
            piece = part["block"](first_step, -step, half(part, step))
            wire.send(part["far"][first_step, step], piece, piece, target)

    def far_done(part, first_step):
        for step in (1, -1):
            piece = part["block"](first_step, 2, half(part, step))
            wire.arrive(part["far"][first_step, step], piece, at.beside(part["second"], step))

    for part in parts:
        for step in (1, -1):
            one_start(part, step)
    for part in parts:
        side_start(part, 0)
    yield
    for step in (1, -1):
        for part in parts:
            one_done(part, step)
    for first_step in (-1, 1):
        for part in parts:
            side_start(part, first_step)
    yield
    for part in parts:
        two_done(part)
    for part in parts:
        side_start(part, 2)
    for part in parts:
        side_done(part, 0)
    yield
    for first_step in (-1, 1):
        for part in parts:
            side_done(part, first_step)
    yield
    for part in parts:
        side_done(part, 2)
    yield
    for first_step in (0, -1, 1, 2):
        for part in parts:
            far_done(part, first_step)
    yield


def gather_kernel(shard, full, send_sems, recv_sems, own_sem):
    at = Place()
    greet(at.greeted())
    wire = Wire(send_sems, recv_sems)
    layers = shard.shape[0]
    own_copies = [
        pltpu.make_async_copy(
            shard.at[layer], full.at[layer, at.z_hi, at.x, at.y], own_sem.at[layer]
        )
        for layer in range(layers)
    ]
    for copy in own_copies:
        copy.start()
    across = [wire.slot() for _ in range(layers)]
    jobs = []
    for layer in range(layers):
        jobs.append((layer, gather_job(wire, at, full, layer, at.z_hi, shard)))
        jobs.append((layer, gather_job(wire, at, full, layer, 1 - at.z_hi, None)))
    for layer in range(layers):
        wire.send(
            across[layer], shard.at[layer], full.at[layer, at.z_hi, at.x, at.y], at.across()
        )

    def advance(index):
        if index < len(jobs):
            next(jobs[index][1])

    def begin(index):
        if index < len(jobs):
            layer = jobs[index][0]
            if index % 2:
                wire.arrive(
                    across[layer], full.at[layer, 1 - at.z_hi, at.x, at.y], at.across()
                )
            advance(index)

    begin(0)
    advance(0)
    for index in range(len(jobs)):
        advance(index)
        begin(index + 1)
        advance(index)
        advance(index)
        advance(index + 1)
        advance(index)
    for copy in own_copies:
        copy.wait()
    wire.drain()


def gather_weights(shard):
    layers = shard.shape[0]
    slots = layers * 81
    return pl.pallas_call(
        gather_kernel,
        out_shape=jax.ShapeDtypeStruct((layers, 2, SIDE, SIDE, 48, WIDTH), jnp.bfloat16),
        in_specs=[pl.BlockSpec(memory_space=pl.ANY)],
        out_specs=pl.BlockSpec(memory_space=pl.ANY),
        scratch_shapes=[
            pltpu.SemaphoreType.DMA((slots,)),
            pltpu.SemaphoreType.DMA((slots,)),
            pltpu.SemaphoreType.DMA((layers,)),
        ],
        compiler_params=pltpu.CompilerParams(collective_id=0, has_side_effects=True),
        name="gather_weights",
    )(shard)


def add_into(target, terms, rows_lead):
    def step(index, carry):
        lead, start = index // 3, pl.multiple_of((index % 3) * 16, 16)
        window = (lead, pl.ds(start, 16)) if rows_lead else (pl.ds(start, 16),)
        total = None
        for term in terms:
            value = term[window].astype(jnp.float32)
            total = value if total is None else total + value
        target[window] = total.astype(target.dtype)
        return carry

    lax.fori_loop(0, 3 * (SIDE if rows_lead else 1), step, 0)


def scatter_job(wire, at, grads, layer, z_data, job, bufs, finish):
    one, two_up, two_down, small_one, small_up, small_down = bufs

    def cut(cols):
        return pl.ds(cols[0], cols[1] - cols[0])

    parts = []
    for first, second, (left, right) in (("y", "x", HALVES[0]), ("x", "y", HALVES[1])):

        def region(step, cols, second=second):
            if second == "x":
                return grads.at[layer, z_data, shift(at.x, step), :, :, cut(cols)]
            return grads.at[layer, z_data, :, shift(at.y, step), :, cut(cols)]

        def mine(step, cols, first=first):
            place = at.y if first == "y" else at.x
            return two_up.at[job, shift(place, step), :, cut(cols)]

        parts.append(
            dict(
                first=first,
                second=second,
                left=left,
                right=right,
                whole=(left[0], right[1]),
                region=region,
                mine=mine,
                far={s: wire.slot() for s in (1, -1)},
                raw={s: wire.slot() for s in (1, -1)},
                sum={s: wire.slot() for s in (1, -1)},
                far2={s: wire.slot() for s in (1, -1)},
                raw2={s: wire.slot() for s in (1, -1)},
                sum2={s: wire.slot() for s in (1, -1)},
            )
        )

    def half(part, step):
        return part["left"] if step == 1 else part["right"]

    def other(part, step):
        return part["right"] if step == 1 else part["left"]

    def landing(step):
        return two_up if step == 1 else two_down

    def small_landing(step):
        return small_up if step == 1 else small_down

    for part in parts:
        for step in (1, -1):
            cols = half(part, step)
            wire.send(
                part["far"][step],
                part["region"](2, cols),
                one.at[job, :, :, cut(cols)],
                at.beside(part["second"], step),
            )
    for part in parts:
        for step in (1, -1):
            cols = other(part, step)
            wire.send(
                part["raw"][step],
                part["region"](step, cols),
                landing(step).at[job, :, :, cut(cols)],
                at.beside(part["second"], step),
            )
    yield
    for step in (1, -1):
        for part in parts:
            cols = half(part, step)
            target = at.beside(part["second"], step)
            piece = one.at[job, :, :, cut(cols)]
            wire.arrive(part["far"][step], piece, target)
            add_into(piece, (piece, part["region"](step, cols)), True)
            wire.send(part["sum"][step], piece, landing(step).at[job, :, :, cut(cols)], target)
    yield
    for part in parts:
        for step in (1, -1):
            target = at.beside(part["second"], step)
            cols = other(part, step)
            wire.arrive(part["raw"][step], landing(step).at[job, :, :, cut(cols)], target)
            cols = half(part, step)
            wire.arrive(part["sum"][step], landing(step).at[job, :, :, cut(cols)], target)
        cols = part["whole"]
        piece = two_up.at[job, :, :, cut(cols)]
        add_into(
            piece,
            (part["region"](0, cols), piece, two_down.at[job, :, :, cut(cols)]),
            True,
        )
        for step in (1, -1):
            cols = half(part, step)
            target = at.beside(part["first"], step)
            wire.send(
                part["far2"][step], part["mine"](2, cols), small_one.at[job, :, cut(cols)], target
            )
            cols = other(part, step)
            wire.send(
                part["raw2"][step],
                part["mine"](step, cols),
                small_landing(step).at[job, :, cut(cols)],
                target,
            )
    yield
    for step in (1, -1):
        for part in parts:
            cols = half(part, step)
            target = at.beside(part["first"], step)
            piece = small_one.at[job, :, cut(cols)]
            wire.arrive(part["far2"][step], piece, target)
            add_into(piece, (piece, part["mine"](step, cols)), False)
            wire.send(
                part["sum2"][step], piece, small_landing(step).at[job, :, cut(cols)], target
            )
    yield
    for part in parts:
        for step in (1, -1):
            target = at.beside(part["first"], step)
            cols = other(part, step)
            wire.arrive(part["raw2"][step], small_landing(step).at[job, :, cut(cols)], target)
            cols = half(part, step)
            wire.arrive(part["sum2"][step], small_landing(step).at[job, :, cut(cols)], target)
        cols = part["whole"]
        finish(
            cut(cols),
            (
                part["mine"](0, cols),
                small_up.at[job, :, cut(cols)],
                small_down.at[job, :, cut(cols)],
            ),
        )
    yield


def scatter_kernel(
    grads,
    out,
    one,
    two_up,
    two_down,
    small_one,
    small_up,
    small_down,
    leaving,
    landed,
    send_sems,
    recv_sems,
):
    at = Place()
    greet(at.greeted())
    wire = Wire(send_sems, recv_sems)
    layers = grads.shape[0]
    bufs = (one, two_up, two_down, small_one, small_up, small_down)
    jobs = []
    for layer in range(layers):
        across = [wire.slot() for _ in range(2)]
        places = (pl.ds(0, 2048), pl.ds(2048, WIDTH - 2048))
        turn = iter(range(2))

        def finish_other(cols, terms, layer=layer, across=across, turn=turn):
            piece = leaving.at[layer, :, cols]
            add_into(piece, terms, False)
            wire.send(
                across[next(turn)], piece, landed.at[layer, :, cols], at.across()
            )

        turn_own = iter(range(2))

        def finish_own(cols, terms, layer=layer, across=across, turn=turn_own):
            piece = landed.at[layer, :, cols]
            wire.arrive(across[next(turn)], piece, at.across())
            add_into(out.at[layer, :, cols], terms + (piece,), False)

        jobs.append(
            scatter_job(
                wire, at, grads, layer, 1 - at.z_hi, 2 * layer, bufs, finish_other
            )
        )
        jobs.append(
            scatter_job(wire, at, grads, layer, at.z_hi, 2 * layer + 1, bufs, finish_own)
        )

    def advance(index):
        if index < len(jobs):
            next(jobs[index])

    advance(0)
    advance(0)
    for index in range(len(jobs)):
        advance(index + 1)
        advance(index)
        advance(index)
        advance(index + 1)
        advance(index)
    wire.drain()


def scatter_grads(grads):
    layers = grads.shape[0]
    slots = layers * 50
    jobs = 2 * layers
    return pl.pallas_call(
        scatter_kernel,
        out_shape=jax.ShapeDtypeStruct((layers, 48, WIDTH), jnp.float32),
        in_specs=[pl.BlockSpec(memory_space=pltpu.VMEM)],
        out_specs=pl.BlockSpec(memory_space=pltpu.VMEM),
        scratch_shapes=[
            pltpu.VMEM((jobs, SIDE, 48, WIDTH), jnp.bfloat16),
            pltpu.VMEM((jobs, SIDE, 48, WIDTH), jnp.bfloat16),
            pltpu.VMEM((jobs, SIDE, 48, WIDTH), jnp.bfloat16),
            pltpu.VMEM((jobs, 48, WIDTH), jnp.bfloat16),
            pltpu.VMEM((jobs, 48, WIDTH), jnp.bfloat16),
            pltpu.VMEM((jobs, 48, WIDTH), jnp.bfloat16),
            pltpu.VMEM((layers, 48, WIDTH), jnp.bfloat16),
            pltpu.VMEM((layers, 48, WIDTH), jnp.bfloat16),
            pltpu.SemaphoreType.DMA((slots,)),
            pltpu.SemaphoreType.DMA((slots,)),
        ],
        compiler_params=pltpu.CompilerParams(
            collective_id=1, has_side_effects=True, vmem_limit_bytes=60 * 2**20
        ),
        name="scatter_grads",
    )(grads)


def pack_rows(arrays):
    query, key, value, out, gate, up, down = arrays
    turned_out = jnp.swapaxes(out, 1, 2)
    turned_down = jnp.swapaxes(down, 1, 2)
    return jnp.concatenate([query, key, value, turned_out, gate, up, turned_down], axis=2)


norm_eps = 1e-05
rope_base = 100000.0


def rope_tables(seq_rows, head_width):
    half_width = head_width // 2
    position = jnp.arange(seq_rows, dtype=jnp.float32)[:, None]
    exponent = 2.0 * jnp.arange(half_width, dtype=jnp.float32) / head_width
    angles = position * (rope_base ** (-exponent))[None, :]
    return (jnp.cos(angles), jnp.sin(angles))


def rotate(values, cosine_table, sine_table):
    half_width = values.shape[-1] // 2
    first_half = values[..., :half_width]
    second_half = values[..., half_width:]
    cosine_wide = cosine_table[:, None, :]
    sine_wide = sine_table[:, None, :]
    return jnp.concatenate(
        [
            first_half * cosine_wide - second_half * sine_wide,
            second_half * cosine_wide + first_half * sine_wide,
        ],
        axis=-1,
    )


def unrotate(values, cosine_table, sine_table):
    half_width = values.shape[-1] // 2
    first_half = values[..., :half_width]
    second_half = values[..., half_width:]
    cosine_wide = cosine_table[:, None, :]
    sine_wide = sine_table[:, None, :]
    return jnp.concatenate(
        [
            first_half * cosine_wide + second_half * sine_wide,
            second_half * cosine_wide - first_half * sine_wide,
        ],
        axis=-1,
    )


def contract_rows(left_rows, right_rows):
    return lax.dot_general(
        left_rows, right_rows, (((0,), (0,)), ((), ())), preferred_element_type=jnp.float32
    )


def times_transpose(left_rows, weight):
    return lax.dot_general(
        left_rows, weight, (((1,), (1,)), ((), ())), preferred_element_type=jnp.float32
    )


def gather_rows(normed):
    return lax.all_gather(normed, "tensor", axis=0, tiled=True)


def gather_grads(gradient):
    return lax.all_gather(gradient, "tensor", axis=0, tiled=True)


def branch_sum(left_rows, weight):
    return lax.psum_scatter(
        jnp.dot(left_rows, weight, preferred_element_type=jnp.float32).astype(jnp.bfloat16),
        "tensor",
        scatter_dimension=0,
        tiled=True,
    ).astype(jnp.float32)


def input_sum(grad_pairs):
    summed = None
    for grad_part, weight in grad_pairs:
        product = times_transpose(grad_part, weight)
        summed = product if summed is None else summed + product
    return lax.psum_scatter(
        summed.astype(jnp.bfloat16), "tensor", scatter_dimension=0, tiled=True
    ).astype(jnp.float32)


def norm_forward(rows_in, gain):
    inverse = lax.rsqrt(jnp.mean(rows_in * rows_in, axis=-1, keepdims=True) + norm_eps)
    return (inverse, (rows_in * inverse * gain).astype(jnp.bfloat16))


def norm_backward(rows_in, inverse, gain, grad_normed):
    scaled = rows_in * inverse
    grad_gain = jnp.sum(grad_normed * scaled, axis=0)
    grad_scaled = grad_normed * gain
    grad_input = inverse * (
        grad_scaled - scaled * jnp.mean(grad_scaled * scaled, axis=-1, keepdims=True)
    )
    return (grad_input, grad_gain)


def masked_scores(query_part, key_rows, offset, block_rows, scaling):
    seq_rows = key_rows.shape[0]
    raw_scores = (
        jnp.einsum("qkgd,skd->kgqs", query_part, key_rows, preferred_element_type=jnp.float32)
        * scaling
    )
    row_places = offset + jnp.arange(block_rows, dtype=jnp.int32)
    key_places = jnp.arange(seq_rows, dtype=jnp.int32)
    allowed = row_places[:, None] >= key_places[None, :]
    return jnp.where(allowed, raw_scores, -1e30)


def attend(query_turned, key_turned, value_rows, scaling):
    seq_rows = query_turned.shape[0]
    block_rows = min(512, seq_rows)
    block_count = seq_rows // block_rows
    query_blocks = query_turned.reshape((block_count, block_rows) + query_turned.shape[1:])
    offsets = jnp.arange(block_count, dtype=jnp.int32) * block_rows

    def one_block(inputs):
        query_part, offset = inputs
        scores = masked_scores(query_part, key_turned, offset, block_rows, scaling)
        row_peak = jnp.max(scores, axis=-1, keepdims=True)
        exponent = jnp.exp(scores - row_peak)
        denominator = jnp.sum(exponent, axis=-1, keepdims=True)
        attn_weights = (exponent / denominator).astype(jnp.bfloat16)
        outputs = jnp.einsum(
            "kgqs,skd->qkgd", attn_weights, value_rows, preferred_element_type=jnp.float32
        )
        return (outputs, row_peak[..., 0] + jnp.log(denominator[..., 0]))

    outputs, logsums = lax.map(one_block, (query_blocks, offsets))
    return (outputs.reshape(seq_rows, -1), logsums)


def attend_back(query_turned, key_turned, value_rows, grad_attended, logsums, scaling):
    seq_rows = query_turned.shape[0]
    block_rows = min(512, seq_rows)
    block_count = seq_rows // block_rows
    query_blocks = query_turned.reshape((block_count, block_rows) + query_turned.shape[1:])
    grad_blocks = grad_attended.reshape((block_count, block_rows) + grad_attended.shape[1:])
    offsets = jnp.arange(block_count, dtype=jnp.int32) * block_rows

    def one_block(carried, inputs):
        grad_keys, grad_values = carried
        query_part, grad_part, logsum_part, offset = inputs
        scores = masked_scores(query_part, key_turned, offset, block_rows, scaling)
        attn_weights = jnp.exp(scores - logsum_part[..., None])
        grad_weights = jnp.einsum(
            "qkgd,skd->kgqs", grad_part, value_rows, preferred_element_type=jnp.float32
        )
        inner_sum = jnp.sum(grad_weights * attn_weights, axis=-1, keepdims=True)
        grad_scores = (attn_weights * (grad_weights - inner_sum)).astype(jnp.bfloat16)
        grad_query = (
            jnp.einsum(
                "kgqs,skd->qkgd", grad_scores, key_turned, preferred_element_type=jnp.float32
            )
            * scaling
        )
        grad_keys = (
            grad_keys
            + jnp.einsum(
                "kgqs,qkgd->skd", grad_scores, query_part, preferred_element_type=jnp.float32
            )
            * scaling
        )
        grad_values = grad_values + jnp.einsum(
            "kgqs,qkgd->skd",
            attn_weights.astype(jnp.bfloat16),
            grad_part,
            preferred_element_type=jnp.float32,
        )
        return ((grad_keys, grad_values), grad_query)

    zero_keys = jnp.zeros(key_turned.shape, jnp.float32)
    (grad_keys, grad_values), grad_query = lax.scan(
        one_block, (zero_keys, zero_keys), (query_blocks, grad_blocks, logsums, offsets)
    )
    return (grad_query.reshape(seq_rows, -1), grad_keys, grad_values)


def body(
    tokens,
    query_weight,
    key_weight,
    value_weight,
    out_weight,
    gate_weight,
    up_weight,
    down_weight,
    norm_gains,
    grad_out,
):
    layers = query_weight.shape[0]
    local_rows = tokens.shape[0]
    heads_local = query_weight.shape[2] // HD
    kv_local = key_weight.shape[2] // HD
    group_size = heads_local // kv_local
    scaling = 1.0 / math.sqrt(HD)
    seq_rows = local_rows * lax.axis_size("tensor")
    cosine_table, sine_table = rope_tables(seq_rows, HD)
    packed = pack_rows(
        (query_weight, key_weight, value_weight, out_weight, gate_weight, up_weight, down_weight)
    )
    gathered = gather_weights(packed).reshape(layers, -1, WIDTH)
    all_gains = lax.all_gather(norm_gains, "dp", axis=2, tiled=True)

    def unpack(layer_index):
        pieces, start = [], 0
        for width in COLS:
            pieces.append(gathered[layer_index, :, start : start + width])
            start += width
        query, key, value, out, gate, up, down = pieces
        return (query, key, value, out.T, gate, up, down.T, all_gains[layer_index])

    residual = tokens.astype(jnp.float32)
    saved = []
    kept_weights = []
    for layer_index in range(layers):
        weights = unpack(layer_index)
        query_full, key_full, value_full, out_full, gate_full, up_full, down_full, gain_full = (
            weights
        )
        gain_values = gain_full.astype(jnp.float32)
        inverse_first, normed_first = norm_forward(residual, gain_values[0])
        rows_first = gather_rows(normed_first)
        query_rows = jnp.dot(rows_first, query_full, preferred_element_type=jnp.float32).reshape(
            seq_rows, heads_local, HD
        )
        key_rows = jnp.dot(rows_first, key_full, preferred_element_type=jnp.float32).reshape(
            seq_rows, kv_local, HD
        )
        value_rows = (
            jnp.dot(rows_first, value_full, preferred_element_type=jnp.float32)
            .astype(jnp.bfloat16)
            .reshape(seq_rows, kv_local, HD)
        )
        query_turned = (
            rotate(query_rows, cosine_table, sine_table)
            .astype(jnp.bfloat16)
            .reshape(seq_rows, kv_local, group_size, HD)
        )
        key_turned = rotate(key_rows, cosine_table, sine_table).astype(jnp.bfloat16)
        attended, logsums = attend(query_turned, key_turned, value_rows, scaling)
        attended_low = attended.astype(jnp.bfloat16)
        middle = residual + branch_sum(attended_low, out_full)
        inverse_second, normed_second = norm_forward(middle, gain_values[1])
        rows_second = gather_rows(normed_second)
        gate_rows = jnp.dot(rows_second, gate_full, preferred_element_type=jnp.float32)
        upward = jnp.dot(rows_second, up_full, preferred_element_type=jnp.float32)
        hidden = (jax.nn.silu(gate_rows) * upward).astype(jnp.bfloat16)
        new_residual = middle + branch_sum(hidden, down_full)
        saved.append(
            (
                residual,
                inverse_first,
                rows_first,
                query_turned,
                key_turned,
                value_rows,
                attended_low,
                logsums,
                middle,
                inverse_second,
                rows_second,
                gate_rows,
                upward,
                hidden,
            )
        )
        kept_weights.append(None)
        residual = new_residual
    output = residual.astype(jnp.bfloat16)
    grad_residual = grad_out.astype(jnp.float32)
    layer_results = [None] * layers
    for layer_index in range(layers - 1, -1, -1):
        (
            residual,
            inverse_first,
            rows_first,
            query_turned,
            key_turned,
            value_rows,
            attended_low,
            logsums,
            middle,
            inverse_second,
            rows_second,
            gate_rows,
            upward,
            hidden,
        ) = saved[layer_index]
        weights = unpack(layer_index)
        query_full, key_full, value_full, out_full, gate_full, up_full, down_full, gain_full = (
            weights
        )
        gain_values = gain_full.astype(jnp.float32)
        grad_rows_mlp = gather_grads(grad_residual.astype(jnp.bfloat16))
        grad_hidden = times_transpose(grad_rows_mlp, down_full)
        grad_down = contract_rows(grad_rows_mlp, hidden)
        sigma = jax.nn.sigmoid(gate_rows)
        grad_gate_rows = (grad_hidden * upward * sigma * (1.0 + gate_rows * (1.0 - sigma))).astype(
            jnp.bfloat16
        )
        grad_upward = (grad_hidden * gate_rows * sigma).astype(jnp.bfloat16)
        grad_gate = contract_rows(rows_second, grad_gate_rows)
        grad_up = contract_rows(rows_second, grad_upward)
        grad_normed_second = input_sum(((grad_gate_rows, gate_full), (grad_upward, up_full)))
        grad_norm_second, gain_part_second = norm_backward(
            middle, inverse_second, gain_values[1], grad_normed_second
        )
        grad_middle = grad_residual + grad_norm_second
        grad_rows_attn = gather_grads(grad_middle.astype(jnp.bfloat16))
        grad_attended = times_transpose(grad_rows_attn, out_full).astype(jnp.bfloat16)
        grad_out_proj = contract_rows(grad_rows_attn, attended_low)
        grad_query_turned, grad_key_turned, grad_value_rows = attend_back(
            query_turned,
            key_turned,
            value_rows,
            grad_attended.reshape(seq_rows, kv_local, group_size, HD),
            logsums,
            scaling,
        )
        grad_query_rows = (
            unrotate(grad_query_turned.reshape(seq_rows, heads_local, HD), cosine_table, sine_table)
            .reshape(seq_rows, -1)
            .astype(jnp.bfloat16)
        )
        grad_key_rows = (
            unrotate(grad_key_turned, cosine_table, sine_table)
            .reshape(seq_rows, -1)
            .astype(jnp.bfloat16)
        )
        grad_value_low = grad_value_rows.reshape(seq_rows, -1).astype(jnp.bfloat16)
        grad_query = contract_rows(rows_first, grad_query_rows)
        grad_key = contract_rows(rows_first, grad_key_rows)
        grad_value = contract_rows(rows_first, grad_value_low)
        grad_normed_first = input_sum(
            ((grad_query_rows, query_full), (grad_key_rows, key_full), (grad_value_low, value_full))
        )
        grad_norm_first, gain_part_first = norm_backward(
            residual, inverse_first, gain_values[0], grad_normed_first
        )
        grad_residual = grad_middle + grad_norm_first
        gain_sums = lax.psum(jnp.stack([gain_part_first, gain_part_second]), "tensor")
        layer_grads = (
            grad_query,
            grad_key,
            grad_value,
            grad_out_proj,
            grad_gate,
            grad_up,
            grad_down,
            gain_sums,
        )
        layer_results[layer_index] = layer_grads
    grads = jnp.stack(
        [
            jnp.concatenate([part.astype(jnp.bfloat16) for part in layer_results[layer_index][:7]], axis=1)
            for layer_index in range(layers)
        ]
    ).reshape(layers, 2, SIDE, SIDE, 48, WIDTH)
    summed = scatter_grads(grads)
    gains_summed = lax.psum_scatter(
        jnp.stack([layer_results[layer_index][7] for layer_index in range(layers)]),
        "dp",
        scatter_dimension=2,
        tiled=True,
    )
    pieces, start = [], 0
    for width in COLS:
        pieces.append(summed[:, :, start : start + width])
        start += width
    query, key, value, out, gate, up, down = pieces
    return (
        output,
        grad_residual,
        query,
        key,
        value,
        jnp.swapaxes(out, 1, 2),
        gate,
        up,
        jnp.swapaxes(down, 1, 2),
        gains_summed,
    )


def solution(mesh):
    return jax.shard_map(
        body,
        mesh=mesh,
        in_specs=(
            P(("dp", "tensor"), None),
            P(None, "dp", "tensor"),
            P(None, "dp", "tensor"),
            P(None, "dp", "tensor"),
            P(None, "tensor", "dp"),
            P(None, "dp", "tensor"),
            P(None, "dp", "tensor"),
            P(None, "tensor", "dp"),
            P(None, None, "dp"),
            P(("dp", "tensor"), None),
        ),
        out_specs=(
            P(("dp", "tensor"), None),
            P(("dp", "tensor"), None),
            P(None, "dp", "tensor"),
            P(None, "dp", "tensor"),
            P(None, "dp", "tensor"),
            P(None, "tensor", "dp"),
            P(None, "dp", "tensor"),
            P(None, "dp", "tensor"),
            P(None, "tensor", "dp"),
            P(None, None, "dp"),
        ),
        check_vma=False,
    )
```

```python
import math

import jax
import jax.numpy as jnp
from jax import lax
from jax.experimental import pallas as pl
from jax.experimental.pallas import tpu as pltpu
from jax.sharding import PartitionSpec as P

HD = 96
MESH_IDS = pl.DeviceIdType.MESH
SIDE = 4
MODEL = 1536
SEQ_ROWS = 512
OWN = 128
QKV = (0, 768)
OUT = (768, 1152)
GATE = (1152, 2176)
UP = (2176, 3200)
DOWN = (3200, 4224)
COLS = (384, 192, 192, 384, 1024, 1024, 1024)
WIDTH = 4224
ATTN_PARTS = (((0, 256), (256, 512)), ((512, 768), (768, 1152)))
MLP_PARTS = (((1152, 1920), (1920, 2688)), ((2688, 3456), (3456, 4224)))

norm_eps = 1e-05
rope_base = 100000.0
SCALING = 1.0 / math.sqrt(HD)


def cut(cols):
    return pl.ds(cols[0], cols[1] - cols[0])


def shift(place, step):
    return lax.rem(place + step + 2 * SIDE, SIDE)


class Place:
    def __init__(self):
        dp = lax.axis_index("dp")
        tensor = lax.axis_index("tensor")
        self.z_hi, self.x, self.y = dp // 16, (dp // 4) % 4, dp % 4
        self.z_lo, self.core = tensor // 2, tensor % 2
        self.dp, self.tensor = dp, tensor

    def device(self, z_hi, x, y, tensor):
        return (z_hi * 16 + x * 4 + y, tensor)

    def beside(self, axis, step):
        if axis == "x":
            return self.device(self.z_hi, shift(self.x, step), self.y, self.tensor)
        return self.device(self.z_hi, self.x, shift(self.y, step), self.tensor)

    def across(self):
        return self.device(1 - self.z_hi, self.x, self.y, self.tensor)

    def twin(self):
        return (self.dp, self.z_lo * 2 + 1 - self.core)

    def above(self):
        return (self.dp, (1 - self.z_lo) * 2 + self.core)

    def greet(self):
        targets = [self.beside(axis, step) for axis in ("x", "y") for step in (1, 2, 3)]
        targets += [self.across(), self.twin(), self.above()]
        barrier = pltpu.get_barrier_semaphore()
        for target in targets:
            pl.semaphore_signal(barrier, inc=1, device_id=target, device_id_type=MESH_IDS)
        pl.semaphore_wait(barrier, len(targets))


class Wire:
    def __init__(self, send_sems, recv_sems):
        self.send_sems, self.recv_sems = send_sems, recv_sems
        self.count = 0
        self.sent = []

    def slot(self):
        self.count += 1
        return self.count - 1

    def send(self, slot, source, target_ref, target):
        copy = pltpu.make_async_remote_copy(
            src_ref=source,
            dst_ref=target_ref,
            send_sem=self.send_sems.at[slot],
            recv_sem=self.recv_sems.at[slot],
            device_id=target,
            device_id_type=MESH_IDS,
        )
        copy.start()
        self.sent.append(copy)
        return copy

    def arrive(self, slot, landed, target):
        pltpu.make_async_remote_copy(
            src_ref=landed,
            dst_ref=landed,
            send_sem=self.send_sems.at[slot],
            recv_sem=self.recv_sems.at[slot],
            device_id=target,
            device_id_type=MESH_IDS,
        ).wait_recv()

    def release(self, copy):
        copy.wait_send()
        self.sent = [other for other in self.sent if other is not copy]

    def drain(self):
        for copy in self.sent:
            copy.wait_send()
        self.sent = []


class Local:
    def __init__(self, sems):
        self.sems, self.count, self.open = sems, 0, []

    def start(self, source, target):
        copy = pltpu.make_async_copy(source, target, self.sems.at[self.count])
        self.count += 1
        copy.start()
        self.open.append(copy)
        return copy

    def wait(self, copy):
        copy.wait()
        self.open = [other for other in self.open if other is not copy]

    def drain(self):
        for copy in self.open:
            copy.wait()
        self.open = []


def sum_small(wire, at, value_ref, landing, whole_group):
    rounds = []
    if whole_group:
        rounds += [[at.twin()], [at.above()]]
    rounds += [[at.across()]]
    rounds += [[at.beside(axis, step) for step in (1, 2, 3)] for axis in ("y", "x")]
    place = 0
    for targets in rounds:
        slots = [wire.slot() for _ in targets]
        copies = []
        for index, target in enumerate(targets):
            copies.append(wire.send(slots[index], value_ref, landing.at[place + index], target))
        yield
        total = value_ref[...]
        for index, target in enumerate(targets):
            wire.arrive(slots[index], landing.at[place + index], target)
            total = total + landing[place + index]
        for copy in copies:
            wire.release(copy)
        value_ref[...] = total
        place += len(targets)
    yield


class Spread:
    pieces = 2

    def __init__(self, wire, at, rows_ref):
        self.wire, self.at, self.rows_ref = wire, at, rows_ref
        self.near = wire.slot()
        self.over = [wire.slot() for _ in range(self.pieces)]
        self.passed = [wire.slot() for _ in range(self.pieces)]
        self.size = OWN // self.pieces

    def rows(self, tensor, piece=None):
        start = pl.multiple_of(tensor * OWN, OWN)
        if piece is None:
            return self.rows_ref.at[pl.ds(start, OWN)]
        return self.rows_ref.at[
            pl.ds(pl.multiple_of(start + piece * self.size, self.size), self.size)
        ]

    def start(self):
        at, wire = self.at, self.wire
        own = at.tensor
        for piece in range(self.pieces):
            wire.send(self.over[piece], self.rows(own, piece), self.rows(own, piece), at.above())
        wire.send(self.near, self.rows(own), self.rows(own), at.twin())

    def near_done(self):
        at = self.at
        self.wire.arrive(self.near, self.rows(at.z_lo * 2 + 1 - at.core), at.twin())

    def pass_on(self):
        at, wire = self.at, self.wire
        there = (1 - at.z_lo) * 2 + at.core
        for piece in range(self.pieces):
            block = self.rows(there, piece)
            wire.arrive(self.over[piece], block, at.above())
            wire.send(self.passed[piece], block, block, at.twin())

    def far_done(self):
        at = self.at
        there = (1 - at.z_lo) * 2 + 1 - at.core
        for piece in range(self.pieces):
            self.wire.arrive(self.passed[piece], self.rows(there, piece), at.twin())


class Collect:
    pieces = 2

    def __init__(self, wire, at, part, help_ref, near_ref, over_ref):
        self.wire, self.at, self.part = wire, at, part
        self.help_ref, self.near_ref, self.over_ref = help_ref, near_ref, over_ref
        self.help = wire.slot()
        self.near = wire.slot()
        self.over = [wire.slot() for _ in range(self.pieces)]
        self.copies = []
        self.size = OWN // self.pieces

    def rows(self, z_lo, core):
        return pl.ds(pl.multiple_of((z_lo * 2 + core) * OWN, OWN), OWN)

    def other_ready(self):
        at = self.at
        block = self.part.at[self.rows(1 - at.z_lo, 1 - at.core)]
        self.copies.append(self.wire.send(self.help, block, self.help_ref, at.twin()))

    def own_ready(self):
        at = self.at
        block = self.part.at[self.rows(at.z_lo, 1 - at.core)]
        self.copies.append(self.wire.send(self.near, block, self.near_ref, at.twin()))

    def send_over(self):
        at = self.at
        self.wire.arrive(self.help, self.help_ref, at.twin())
        for piece in range(self.pieces):
            window = pl.ds(piece * self.size, self.size)
            start = ((1 - at.z_lo) * 2 + at.core) * OWN + piece * self.size
            rows = pl.ds(pl.multiple_of(start, self.size), self.size)
            total = self.part[rows, :].astype(jnp.float32) + self.help_ref[window, :].astype(
                jnp.float32
            )
            self.part[rows, :] = total.astype(jnp.bfloat16)
            self.copies.append(
                self.wire.send(
                    self.over[piece],
                    self.part.at[rows],
                    self.over_ref.at[window],
                    at.above(),
                )
            )

    def result(self):
        at = self.at
        self.wire.arrive(self.near, self.near_ref, at.twin())
        total = self.part[self.rows(at.z_lo, at.core), :].astype(jnp.float32) + self.near_ref[
            ...
        ].astype(jnp.float32)
        for piece in range(self.pieces):
            window = pl.ds(piece * self.size, self.size)
            self.wire.arrive(self.over[piece], self.over_ref.at[window], at.above())
        total = total + self.over_ref[...].astype(jnp.float32)
        for copy in self.copies:
            self.wire.release(copy)
        self.copies = []
        return total


def nn(left, right):
    return jnp.dot(left, right, preferred_element_type=jnp.float32)


def nt(left, right):
    return lax.dot_general(
        left, right, (((1,), (1,)), ((), ())), preferred_element_type=jnp.float32
    )


def tn(left, right):
    return lax.dot_general(
        left, right, (((0,), (0,)), ((), ())), preferred_element_type=jnp.float32
    )


def rope_tables(heads):
    half = HD // 2
    position = jnp.arange(SEQ_ROWS, dtype=jnp.float32)[:, None]
    exponent = 2.0 * jnp.arange(half, dtype=jnp.float32) / HD
    angles = position * (rope_base ** (-exponent))[None, :]
    cosine, sine = jnp.cos(angles), jnp.sin(angles)
    wide_cosine = jnp.concatenate([cosine, cosine], axis=1)
    wide_sine = jnp.concatenate([-sine, sine], axis=1)
    return jnp.tile(wide_cosine, (1, heads)), jnp.tile(wide_sine, (1, heads))


def swap_halves(values):
    width = values.shape[1]
    lane = lax.broadcasted_iota(jnp.int32, values.shape, 1)
    first = lax.rem(lane, HD) < HD // 2
    return jnp.where(
        first, pltpu.roll(values, width - HD // 2, 1), pltpu.roll(values, HD // 2, 1)
    )


def head_of(values, start):
    width = values.shape[1]
    moved = values if start == 0 else pltpu.roll(values, width - start, 1)
    moved = moved[:, :128]
    lane = lax.broadcasted_iota(jnp.int32, moved.shape, 1)
    return jnp.where(lane < HD, moved, 0.0)


def side_by_side(heads):
    tiles = []
    for tile in range(len(heads) * HD // 128):
        total = None
        lane = lax.broadcasted_iota(jnp.int32, heads[0].shape, 1)
        for index, head in enumerate(heads):
            start = index * HD - tile * 128
            if start <= -HD or start >= 128:
                continue
            moved = pltpu.roll(head, start % 128, 1) if start else head
            if start > 0 or start < 0:
                keep = (lane >= start) if start > 0 else (lane < start + HD)
                moved = jnp.where(keep, moved, 0.0)
            total = moved if total is None else total + moved
        tiles.append(total)
    return jnp.concatenate(tiles, axis=1)


def chip_rows(z_lo):
    return pl.ds(pl.multiple_of(z_lo * 256, 256), 256)


def weight(w_ref, layer, cols):
    value = w_ref[layer, :, :, cols]
    return value.reshape(MODEL, value.shape[-1])


def gather_job(wire, at, full, layer, group):
    parts = []
    for (first, second), (left, right) in zip((("y", "x"), ("x", "y")), group):

        def block(first_step, second_step, cols, first=first):
            x_step, y_step = (
                (first_step, second_step) if first == "x" else (second_step, first_step)
            )
            row = shift(at.x, x_step) * 192 + shift(at.y, y_step) * 48
            return full.at[layer, :, pl.ds(pl.multiple_of(row, 48), 48), cut(cols)]

        parts.append(
            dict(
                first=first,
                second=second,
                left=left,
                right=right,
                whole=(left[0], right[1]),
                block=block,
                one={s: wire.slot() for s in (1, -1)},
                two={s: wire.slot() for s in (1, -1)},
                side={(f, s): wire.slot() for f in (0, -1, 1, 2) for s in (1, -1)},
                far={(f, s): wire.slot() for f in (0, -1, 1, 2) for s in (1, -1)},
            )
        )

    def half(part, step):
        return part["left"] if step == 1 else part["right"]

    def one_start(part, step):
        piece = part["block"](0, 0, part["whole"])
        wire.send(part["one"][step], piece, piece, at.beside(part["first"], step))

    def side_start(part, first_step):
        for step in (1, -1):
            piece = part["block"](first_step, 0, part["whole"])
            wire.send(
                part["side"][first_step, step], piece, piece, at.beside(part["second"], step)
            )

    def one_done(part, step):
        target = at.beside(part["first"], step)
        wire.arrive(part["one"][step], part["block"](-step, 0, part["whole"]), target)
        piece = part["block"](-step, 0, half(part, step))
        wire.send(part["two"][step], piece, piece, target)

    def two_done(part):
        for step in (1, -1):
            piece = part["block"](2, 0, half(part, step))
            wire.arrive(part["two"][step], piece, at.beside(part["first"], step))

    def side_done(part, first_step):
        for step in (1, -1):
            target = at.beside(part["second"], step)
            landed = part["block"](first_step, -step, part["whole"])
            wire.arrive(part["side"][first_step, step], landed, target)
            piece = part["block"](first_step, -step, half(part, step))
            wire.send(part["far"][first_step, step], piece, piece, target)

    def far_done(part, first_step):
        for step in (1, -1):
            piece = part["block"](first_step, 2, half(part, step))
            wire.arrive(part["far"][first_step, step], piece, at.beside(part["second"], step))

    for part in parts:
        for step in (1, -1):
            one_start(part, step)
    for part in parts:
        side_start(part, 0)
    yield
    for step in (1, -1):
        for part in parts:
            one_done(part, step)
    for first_step in (-1, 1):
        for part in parts:
            side_start(part, first_step)
    yield
    for part in parts:
        two_done(part)
    for part in parts:
        side_start(part, 2)
    for part in parts:
        side_done(part, 0)
    yield
    for first_step in (-1, 1):
        for part in parts:
            side_done(part, first_step)
    yield
    for part in parts:
        side_done(part, 2)
    yield
    for first_step in (0, -1, 1, 2):
        for part in parts:
            far_done(part, first_step)
    yield


class Gather:
    def __init__(self, wire, local, at, shard, full, kept):
        self.wire, self.local, self.at, self.shard = wire, local, at, shard
        self.full, self.kept = full, kept
        self.groups = [
            (layer, group) for layer in range(2) for group in (ATTN_PARTS, MLP_PARTS)
        ]
        self.jobs = [gather_job(wire, at, full, *pair) for pair in self.groups]
        self.slots = [wire.slot() for _ in self.groups]
        self.own = []
        order = [(0, 0), (0, 1)]
        for index in range(len(self.jobs)):
            order += [(index, 2), (index + 1, 0), (index, 3), (index, 4), (index + 1, 1)]
            order += [(index, 5)]
        self.order = [pair for pair in order if pair[0] < len(self.jobs)]
        self.done = 0

    def columns(self, index):
        group = self.groups[index][1]
        return cut((group[0][0][0], group[1][1][1]))

    def mine(self, z_hi):
        row = self.at.x * 192 + self.at.y * 48
        return (z_hi, pl.ds(pl.multiple_of(row, 48), 48))

    def begin(self):
        at = self.at
        z_own, rows = self.mine(at.z_hi)
        for index, (layer, _) in enumerate(self.groups):
            cols = self.columns(index)
            source = self.shard.at[layer, :, cols]
            target = self.full.at[layer, z_own, rows, cols]
            self.wire.send(self.slots[index], source, target, at.across())
            self.own.append(self.local.start(source, target))

    def step(self, count=1):
        for _ in range(count):
            if self.done == len(self.order):
                return
            index, stage = self.order[self.done]
            self.done += 1
            layer = self.groups[index][0]
            cols = self.columns(index)
            if stage == 0:
                self.local.wait(self.own[index])
                z_other, rows = self.mine(1 - self.at.z_hi)
                landed = self.full.at[layer, z_other, rows, cols]
                self.wire.arrive(self.slots[index], landed, self.at.across())
            next(self.jobs[index])
            if stage == 5:
                self.local.start(
                    self.full.at[layer, :, :, cols], self.kept.at[layer, :, :, cols]
                )

    def until(self, index):
        while (index, 5) in self.order[self.done :]:
            self.step()


def normed(rows_in, gain):
    inverse = lax.rsqrt(jnp.mean(rows_in * rows_in, axis=-1, keepdims=True) + norm_eps)
    return (rows_in * inverse * gain).astype(jnp.bfloat16)


def project_heads(layer, rows, n1, w, cosine, sine, q_ref, k_ref, v_ref):
    left = n1[layer, rows, :]
    cosine_rows, sine_rows = cosine[rows, :], sine[rows, :]
    query = nn(left, weight(w, layer, pl.ds(0, 384)))
    turned = query * cosine_rows + swap_halves(query) * sine_rows
    for head in range(4):
        q_ref[layer, head, rows, :] = head_of(turned, head * HD).astype(jnp.bfloat16)
    both = nn(left, weight(w, layer, pl.ds(384, 384)))
    turned = both * cosine_rows + swap_halves(both) * sine_rows
    for head in range(2):
        k_ref[layer, head, rows, :] = head_of(turned, head * HD).astype(jnp.bfloat16)
        v_ref[layer, head, rows, :] = head_of(both, 192 + head * HD).astype(jnp.bfloat16)


def attend(layer, q_ref, k_ref, v_ref, p_ref, o_ref):
    for block in range(4):
        rows = pl.ds(block * 128, 128)
        keys = (block + 1) * 128
        outputs = []
        for head in range(2):
            pair = jnp.concatenate(
                [q_ref[layer, 2 * head, rows, :], q_ref[layer, 2 * head + 1, rows, :]], axis=0
            )
            scores = nt(pair, k_ref[layer, head, pl.ds(0, keys), :]) * SCALING
            row = lax.broadcasted_iota(jnp.int32, (256, keys), 0) % 128 + block * 128
            key = lax.broadcasted_iota(jnp.int32, (256, keys), 1)
            scores = jnp.where(row >= key, scores, -1e30)
            peak = jnp.max(scores, axis=-1, keepdims=True)
            exponent = jnp.exp(scores - peak)
            inverse = 1.0 / jnp.sum(exponent, axis=-1, keepdims=True)
            shares = (exponent * inverse).astype(jnp.bfloat16)
            p_ref[layer, 2 * head, rows, pl.ds(0, keys)] = shares[:128]
            p_ref[layer, 2 * head + 1, rows, pl.ds(0, keys)] = shares[128:]
            out = nn(shares, v_ref[layer, head, pl.ds(0, keys), :])
            outputs += [out[:128], out[128:]]
        o_ref[layer, rows, :] = side_by_side(outputs).astype(jnp.bfloat16)


def out_partial(layer, rows, o_ref, w, part):
    left = o_ref[layer, rows, :]
    for half in range(2):
        for tile in range(3):
            right = w[layer, half, pl.ds(tile * 256, 256), cut(OUT)]
            part[rows, pl.ds(half * 768 + tile * 256, 256)] = nt(left, right).astype(jnp.bfloat16)


def hidden_rows(layer, rows, n2, w, g_ref, u_ref, a_ref):
    left = n2[layer, rows, :]

    def tile(index, carry):
        start = pl.multiple_of(index * 256, 256)
        gate = nn(left, weight(w, layer, pl.ds(GATE[0] + start, 256)))
        up = nn(left, weight(w, layer, pl.ds(UP[0] + start, 256)))
        hidden = gate * up / (1.0 + jnp.exp(-gate))
        g_ref[layer, rows, pl.ds(start, 256)] = gate.astype(g_ref.dtype)
        u_ref[layer, rows, pl.ds(start, 256)] = up.astype(u_ref.dtype)
        a_ref[layer, rows, pl.ds(start, 256)] = hidden.astype(jnp.bfloat16)
        return carry

    lax.fori_loop(0, 4, tile, 0)


def down_partial(layer, rows, a_ref, w, part):
    left = a_ref[layer, rows, :]
    for half in range(2):

        def tile(index, carry, half=half):
            start = pl.multiple_of(index * 256, 256)
            right = w[layer, half, pl.ds(start, 256), cut(DOWN)]
            part[rows, pl.ds(pl.multiple_of(half * 768 + start, 256), 256)] = nt(
                left, right
            ).astype(jnp.bfloat16)
            return carry

        lax.fori_loop(0, 3, tile, 0)


def forward_kernel(
    shard,
    gains_placed,
    tokens,
    cosine,
    sine,
    w_kept,
    gains,
    output,
    n1_kept,
    n2_kept,
    q_kept,
    k_kept,
    v_kept,
    p_kept,
    o_kept,
    g_kept,
    u_kept,
    a_kept,
    x_kept,
    h_kept,
    w,
    n1,
    n2,
    q_ref,
    k_ref,
    v_ref,
    p_ref,
    o_ref,
    g_ref,
    u_ref,
    a_ref,
    x_ref,
    h_ref,
    part,
    help_ref,
    near_ref,
    over_ref,
    gains_landing,
    send_sems,
    recv_sems,
    local_sems,
):
    at = Place()
    at.greet()
    wire = Wire(send_sems, recv_sems)
    local = Local(local_sems)
    gather = Gather(wire, local, at, shard, w, w_kept)
    gather.begin()
    gather.step()
    gains[...] = gains_placed[...]
    rounds = sum_small(wire, at, gains, gains_landing, False)
    for _ in rounds:
        gather.step()
    x_ref[0] = tokens[...].astype(jnp.float32)
    own = pl.ds(pl.multiple_of(at.tensor * OWN, OWN), OWN)
    here, there = chip_rows(at.z_lo), chip_rows(1 - at.z_lo)
    turn = 0

    def collector():
        nonlocal turn
        turn += 1
        slot = turn % 2
        return Collect(
            wire, at, part, help_ref.at[slot], near_ref.at[slot], over_ref.at[slot]
        )

    for layer in range(2):
        n1[layer, own, :] = normed(x_ref[layer], gains[pl.ds(2 * layer, 1), :])
        spread = Spread(wire, at, n1.at[layer])
        spread.start()
        gather.until(2 * layer)
        heads = (n1, w, cosine, sine, q_ref, k_ref, v_ref)
        spread.near_done()
        project_heads(layer, here, *heads)
        gather.step()
        spread.pass_on()
        spread.far_done()
        project_heads(layer, there, *heads)
        for source, target in ((n1, n1_kept), (q_ref, q_kept), (k_ref, k_kept), (v_ref, v_kept)):
            local.start(source.at[layer], target.at[layer])
        gather.step()
        attend(layer, q_ref, k_ref, v_ref, p_ref, o_ref)
        for source, target in ((p_ref, p_kept), (o_ref, o_kept)):
            local.start(source.at[layer], target.at[layer])
        collect = collector()
        out_partial(layer, there, o_ref, w, part)
        collect.other_ready()
        out_partial(layer, here, o_ref, w, part)
        collect.own_ready()
        collect.send_over()
        gather.step()
        h_ref[layer] = x_ref[layer] + collect.result()
        n2[layer, own, :] = normed(h_ref[layer], gains[pl.ds(2 * layer + 1, 1), :])
        spread = Spread(wire, at, n2.at[layer])
        spread.start()
        gather.until(2 * layer + 1)
        spread.near_done()
        hidden_rows(layer, here, n2, w, g_ref, u_ref, a_ref)
        gather.step()
        spread.pass_on()
        spread.far_done()
        hidden_rows(layer, there, n2, w, g_ref, u_ref, a_ref)
        for source, target in (
            (n2, n2_kept),
            (h_ref, h_kept),
            (g_ref, g_kept),
            (u_ref, u_kept),
            (a_ref, a_kept),
        ):
            local.start(source.at[layer], target.at[layer])
        collect = collector()
        down_partial(layer, there, a_ref, w, part)
        collect.other_ready()
        down_partial(layer, here, a_ref, w, part)
        collect.own_ready()
        collect.send_over()
        gather.step()
        total = h_ref[layer] + collect.result()
        if layer == 0:
            x_ref[1] = total
            local.start(x_ref.at[1], x_kept)
        else:
            output[...] = total.astype(jnp.bfloat16)
    local.drain()
    wire.drain()


KEEP = jnp.bfloat16


def run_forward(shard, gains_placed, tokens, cosine, sine):
    def kept(*shape, kind=jnp.bfloat16):
        return jax.ShapeDtypeStruct(shape, kind)

    def held(*shape, kind=jnp.bfloat16):
        return pltpu.VMEM(shape, kind)

    vmem = pl.BlockSpec(memory_space=pltpu.VMEM)
    hbm = pl.BlockSpec(memory_space=pl.ANY)
    float32 = jnp.float32
    wires = 4 * 41 + 7 + 8 * 5 + 4
    return pl.pallas_call(
        forward_kernel,
        out_shape=(
            kept(2, 2, 768, WIDTH),
            kept(8, MODEL, kind=float32),
            kept(OWN, MODEL),
            kept(2, SEQ_ROWS, MODEL),
            kept(2, SEQ_ROWS, MODEL),
            kept(2, 4, SEQ_ROWS, 128),
            kept(2, 2, SEQ_ROWS, 128),
            kept(2, 2, SEQ_ROWS, 128),
            kept(2, 4, SEQ_ROWS, SEQ_ROWS),
            kept(2, SEQ_ROWS, 384),
            kept(2, SEQ_ROWS, 1024, kind=KEEP),
            kept(2, SEQ_ROWS, 1024, kind=KEEP),
            kept(2, SEQ_ROWS, 1024),
            kept(OWN, MODEL, kind=float32),
            kept(2, OWN, MODEL, kind=float32),
        ),
        in_specs=[vmem] * 5,
        out_specs=(hbm, vmem, vmem) + (hbm,) * 12,
        scratch_shapes=[
            held(2, 2, 768, WIDTH),
            held(2, SEQ_ROWS, MODEL),
            held(2, SEQ_ROWS, MODEL),
            held(2, 4, SEQ_ROWS, 128),
            held(2, 2, SEQ_ROWS, 128),
            held(2, 2, SEQ_ROWS, 128),
            held(2, 4, SEQ_ROWS, SEQ_ROWS),
            held(2, SEQ_ROWS, 384),
            held(2, SEQ_ROWS, 1024, kind=KEEP),
            held(2, SEQ_ROWS, 1024, kind=KEEP),
            held(2, SEQ_ROWS, 1024),
            held(2, OWN, MODEL, kind=float32),
            held(2, OWN, MODEL, kind=float32),
            held(SEQ_ROWS, MODEL),
            held(2, OWN, MODEL),
            held(2, OWN, MODEL),
            held(2, OWN, MODEL),
            held(7, 8, MODEL, kind=float32),
            pltpu.SemaphoreType.DMA((wires,)),
            pltpu.SemaphoreType.DMA((wires,)),
            pltpu.SemaphoreType.DMA((40,)),
        ],
        compiler_params=pltpu.CompilerParams(
            collective_id=0, has_side_effects=True, vmem_limit_bytes=62 * 2**20
        ),
        name="forward",
    )(shard, gains_placed, tokens, cosine, sine)


HALVES = (((0, 1024), (1024, 2048)), ((2048, 3072), (3072, 4224)))


def add_into(target, terms, rows_lead):
    def step(index, carry):
        lead, start = index // 3, pl.multiple_of((index % 3) * 16, 16)
        window = (lead, pl.ds(start, 16)) if rows_lead else (pl.ds(start, 16),)
        total = None
        for term in terms:
            value = term[window].astype(jnp.float32)
            total = value if total is None else total + value
        target[window] = total.astype(target.dtype)
        return carry

    lax.fori_loop(0, 3 * (SIDE if rows_lead else 1), step, 0)


def scatter_job(wire, at, grads, layer, z_data, job, bufs, finish):
    one, two_up, two_down, small_one, small_up, small_down = bufs

    def cut(cols):
        return pl.ds(cols[0], cols[1] - cols[0])

    parts = []
    for first, second, (left, right) in (("y", "x", HALVES[0]), ("x", "y", HALVES[1])):

        def region(step, cols, second=second):
            if second == "x":
                return grads.at[layer, z_data, shift(at.x, step), :, :, cut(cols)]
            return grads.at[layer, z_data, :, shift(at.y, step), :, cut(cols)]

        def mine(step, cols, first=first):
            place = at.y if first == "y" else at.x
            return two_up.at[job, shift(place, step), :, cut(cols)]

        parts.append(
            dict(
                first=first,
                second=second,
                left=left,
                right=right,
                whole=(left[0], right[1]),
                region=region,
                mine=mine,
                far={s: wire.slot() for s in (1, -1)},
                raw={s: wire.slot() for s in (1, -1)},
                sum={s: wire.slot() for s in (1, -1)},
                far2={s: wire.slot() for s in (1, -1)},
                raw2={s: wire.slot() for s in (1, -1)},
                sum2={s: wire.slot() for s in (1, -1)},
            )
        )

    def half(part, step):
        return part["left"] if step == 1 else part["right"]

    def other(part, step):
        return part["right"] if step == 1 else part["left"]

    def landing(step):
        return two_up if step == 1 else two_down

    def small_landing(step):
        return small_up if step == 1 else small_down

    for part in parts:
        for step in (1, -1):
            cols = half(part, step)
            wire.send(
                part["far"][step],
                part["region"](2, cols),
                one.at[job, :, :, cut(cols)],
                at.beside(part["second"], step),
            )
    for part in parts:
        for step in (1, -1):
            cols = other(part, step)
            wire.send(
                part["raw"][step],
                part["region"](step, cols),
                landing(step).at[job, :, :, cut(cols)],
                at.beside(part["second"], step),
            )
    yield
    for step in (1, -1):
        for part in parts:
            cols = half(part, step)
            target = at.beside(part["second"], step)
            piece = one.at[job, :, :, cut(cols)]
            wire.arrive(part["far"][step], piece, target)
            add_into(piece, (piece, part["region"](step, cols)), True)
            wire.send(part["sum"][step], piece, landing(step).at[job, :, :, cut(cols)], target)
    yield
    for part in parts:
        for step in (1, -1):
            target = at.beside(part["second"], step)
            cols = other(part, step)
            wire.arrive(part["raw"][step], landing(step).at[job, :, :, cut(cols)], target)
            cols = half(part, step)
            wire.arrive(part["sum"][step], landing(step).at[job, :, :, cut(cols)], target)
        cols = part["whole"]
        piece = two_up.at[job, :, :, cut(cols)]
        add_into(
            piece,
            (part["region"](0, cols), piece, two_down.at[job, :, :, cut(cols)]),
            True,
        )
        for step in (1, -1):
            cols = half(part, step)
            target = at.beside(part["first"], step)
            wire.send(
                part["far2"][step], part["mine"](2, cols), small_one.at[job, :, cut(cols)], target
            )
            cols = other(part, step)
            wire.send(
                part["raw2"][step],
                part["mine"](step, cols),
                small_landing(step).at[job, :, cut(cols)],
                target,
            )
    yield
    for step in (1, -1):
        for part in parts:
            cols = half(part, step)
            target = at.beside(part["first"], step)
            piece = small_one.at[job, :, cut(cols)]
            wire.arrive(part["far2"][step], piece, target)
            add_into(piece, (piece, part["mine"](step, cols)), False)
            wire.send(
                part["sum2"][step], piece, small_landing(step).at[job, :, cut(cols)], target
            )
    yield
    for part in parts:
        for step in (1, -1):
            target = at.beside(part["first"], step)
            cols = other(part, step)
            wire.arrive(part["raw2"][step], small_landing(step).at[job, :, cut(cols)], target)
            cols = half(part, step)
            wire.arrive(part["sum2"][step], small_landing(step).at[job, :, cut(cols)], target)
        cols = part["whole"]
        finish(
            cut(cols),
            (
                part["mine"](0, cols),
                small_up.at[job, :, cut(cols)],
                small_down.at[job, :, cut(cols)],
            ),
        )
    yield


def scatter_kernel(
    grads,
    out,
    one,
    two_up,
    two_down,
    small_one,
    small_up,
    small_down,
    leaving,
    landed,
    send_sems,
    recv_sems,
):
    at = Place()
    at.greet()
    wire = Wire(send_sems, recv_sems)
    layers = grads.shape[0]
    bufs = (one, two_up, two_down, small_one, small_up, small_down)
    jobs = []
    for layer in range(layers):
        across = [wire.slot() for _ in range(2)]
        places = (pl.ds(0, 2048), pl.ds(2048, WIDTH - 2048))
        turn = iter(range(2))

        def finish_other(cols, terms, layer=layer, across=across, turn=turn):
            piece = leaving.at[layer, :, cols]
            add_into(piece, terms, False)
            wire.send(
                across[next(turn)], piece, landed.at[layer, :, cols], at.across()
            )

        turn_own = iter(range(2))

        def finish_own(cols, terms, layer=layer, across=across, turn=turn_own):
            piece = landed.at[layer, :, cols]
            wire.arrive(across[next(turn)], piece, at.across())
            add_into(out.at[layer, :, cols], terms + (piece,), False)

        jobs.append(
            scatter_job(
                wire, at, grads, layer, 1 - at.z_hi, 2 * layer, bufs, finish_other
            )
        )
        jobs.append(
            scatter_job(wire, at, grads, layer, at.z_hi, 2 * layer + 1, bufs, finish_own)
        )

    def advance(index):
        if index < len(jobs):
            next(jobs[index])

    advance(0)
    advance(0)
    for index in range(len(jobs)):
        advance(index + 1)
        advance(index)
        advance(index)
        advance(index + 1)
        advance(index)
    wire.drain()


def scatter_grads(grads):
    layers = grads.shape[0]
    slots = layers * 50
    jobs = 2 * layers
    return pl.pallas_call(
        scatter_kernel,
        out_shape=jax.ShapeDtypeStruct((layers, 48, WIDTH), jnp.float32),
        in_specs=[pl.BlockSpec(memory_space=pltpu.VMEM)],
        out_specs=pl.BlockSpec(memory_space=pltpu.VMEM),
        scratch_shapes=[
            pltpu.VMEM((jobs, SIDE, 48, WIDTH), jnp.bfloat16),
            pltpu.VMEM((jobs, SIDE, 48, WIDTH), jnp.bfloat16),
            pltpu.VMEM((jobs, SIDE, 48, WIDTH), jnp.bfloat16),
            pltpu.VMEM((jobs, 48, WIDTH), jnp.bfloat16),
            pltpu.VMEM((jobs, 48, WIDTH), jnp.bfloat16),
            pltpu.VMEM((jobs, 48, WIDTH), jnp.bfloat16),
            pltpu.VMEM((layers, 48, WIDTH), jnp.bfloat16),
            pltpu.VMEM((layers, 48, WIDTH), jnp.bfloat16),
            pltpu.SemaphoreType.DMA((slots,)),
            pltpu.SemaphoreType.DMA((slots,)),
        ],
        compiler_params=pltpu.CompilerParams(
            collective_id=1, has_side_effects=True, vmem_limit_bytes=60 * 2**20
        ),
        name="scatter_grads",
    )(grads)


def pack_rows(arrays):
    query, key, value, out, gate, up, down = arrays
    turned_out = jnp.swapaxes(out, 1, 2)
    turned_down = jnp.swapaxes(down, 1, 2)
    return jnp.concatenate([query, key, value, turned_out, gate, up, turned_down], axis=2)


def norm_backward(rows_in, gain, grad_normed):
    inverse = lax.rsqrt(jnp.mean(rows_in * rows_in, axis=-1, keepdims=True) + norm_eps)
    scaled = rows_in * inverse
    grad_gain = jnp.sum(grad_normed * scaled, axis=0)
    grad_scaled = grad_normed * gain
    grad_input = inverse * (
        grad_scaled - scaled * jnp.mean(grad_scaled * scaled, axis=-1, keepdims=True)
    )
    return (grad_input, grad_gain)


def body(
    tokens,
    query_weight,
    key_weight,
    value_weight,
    out_weight,
    gate_weight,
    up_weight,
    down_weight,
    norm_gains,
    grad_out,
):
    layers = 2
    packed = pack_rows(
        (query_weight, key_weight, value_weight, out_weight, gate_weight, up_weight, down_weight)
    )
    dp = lax.axis_index("dp")
    gains_placed = lax.dynamic_update_slice(
        jnp.zeros((8, MODEL), jnp.float32),
        norm_gains.reshape(4, -1).astype(jnp.float32),
        (0, dp * 48),
    )
    cosine, sine = rope_tables(4)
    (
        w_kept, gains, output, n1, n2, q, k, v, p, o, g, u, a, x_second, h,
    ) = run_forward(packed, gains_placed, tokens, cosine, sine)
    w_kept = w_kept.reshape(2, MODEL, WIDTH)
    grad_residual = grad_out.astype(jnp.float32)
    layer_results = [None] * layers
    tri = jnp.tril(jnp.ones((512, 512), bool))
    def gat(r):
        return lax.all_gather(r.astype(jnp.bfloat16), "tensor", axis=0, tiled=True)
    def rs(r):
        return lax.psum_scatter(r.astype(jnp.bfloat16), "tensor", scatter_dimension=0, tiled=True).astype(jnp.float32)
    f32 = jnp.float32
    def unrot(vals):
        c, s = cosine[:, : vals.shape[1]], sine[:, : vals.shape[1]]
        v4 = vals.reshape(512, -1, 2, 48)
        sw = v4[:, :, ::-1].reshape(vals.shape)
        return vals * c - sw * s
    for l in (1, 0):
        W = w_kept[l]
        residual = tokens.astype(f32) if l == 0 else x_second
        dm = gat(grad_residual)
        da = nn(dm, W[:, 3200:4224])
        gd = tn(dm, a[l])
        G, U = g[l].astype(f32), u[l].astype(f32)
        sg = jax.nn.sigmoid(G)
        dg = (da * U * sg * (1 + G * (1 - sg))).astype(jnp.bfloat16)
        du = (da * G * sg).astype(jnp.bfloat16)
        gg, gu = tn(n2[l], dg), tn(n2[l], du)
        dn2 = rs(nt(dg, W[:, 1152:2176]) + nt(du, W[:, 2176:3200]))
        gn, gain2 = norm_backward(h[l], gains[2 * l + 1], dn2)
        gmid = grad_residual + gn
        dhb = gat(gmid)
        do = nn(dhb, W[:, 768:1152]).astype(jnp.bfloat16)
        go = tn(dhb, o[l])
        dqs, dks, dvs = [], [], []
        for kv in range(2):
            dk = dv = 0
            for hh in (2 * kv, 2 * kv + 1):
                P_ = jnp.where(tri, p[l, hh], 0).astype(f32)
                doh = do[:, hh * 96 : hh * 96 + 96]
                dP = nt(doh, v[l, kv, :, :96])
                dS = (P_ * (dP - jnp.sum(dP * P_, -1, keepdims=True))).astype(jnp.bfloat16)
                dqs.append(nn(dS, k[l, kv, :, :96]) * SCALING)
                dk = dk + tn(dS, q[l, hh, :, :96]) * SCALING
                dv = dv + tn(P_.astype(jnp.bfloat16), doh)
            dks.append(dk)
            dvs.append(dv)
        dq = unrot(jnp.concatenate(dqs, 1)).astype(jnp.bfloat16)
        dk = unrot(jnp.concatenate(dks, 1)).astype(jnp.bfloat16)
        dv = jnp.concatenate(dvs, 1).astype(jnp.bfloat16)
        dqkv = jnp.concatenate([dq, dk, dv], 1)
        gqkv = tn(n1[l], dqkv)
        dn1 = rs(nt(dqkv, W[:, :768]))
        gn, gain1 = norm_backward(residual, gains[2 * l], dn1)
        grad_residual = gmid + gn
        layer_results[l] = (gqkv, go, gg, gu, gd, jnp.stack([gain1, gain2]))
    grads = jnp.stack(
        [jnp.concatenate([t.astype(jnp.bfloat16) for t in r[:5]], axis=1) for r in layer_results]
    ).reshape(layers, 2, SIDE, SIDE, 48, WIDTH)
    summed = scatter_grads(grads)
    gains_summed = lax.psum_scatter(
        lax.psum(jnp.stack([r[5] for r in layer_results]), "tensor"), "dp", scatter_dimension=2, tiled=True
    )
    pieces, start = [], 0
    for width in COLS:
        pieces.append(summed[:, :, start : start + width])
        start += width
    query, key, value, out, gate, up, down = pieces
    return (
        output,
        grad_residual,
        query,
        key,
        value,
        jnp.swapaxes(out, 1, 2),
        gate,
        up,
        jnp.swapaxes(down, 1, 2),
        gains_summed,
    )


def solution(mesh):
    return jax.shard_map(
        body,
        mesh=mesh,
        in_specs=(
            P(("dp", "tensor"), None),
            P(None, "dp", "tensor"),
            P(None, "dp", "tensor"),
            P(None, "dp", "tensor"),
            P(None, "tensor", "dp"),
            P(None, "dp", "tensor"),
            P(None, "dp", "tensor"),
            P(None, "tensor", "dp"),
            P(None, None, "dp"),
            P(("dp", "tensor"), None),
        ),
        out_specs=(
            P(("dp", "tensor"), None),
            P(("dp", "tensor"), None),
            P(None, "dp", "tensor"),
            P(None, "dp", "tensor"),
            P(None, "dp", "tensor"),
            P(None, "tensor", "dp"),
            P(None, "dp", "tensor"),
            P(None, "dp", "tensor"),
            P(None, "tensor", "dp"),
            P(None, None, "dp"),
        ),
        check_vma=False,
    )
```

```python
import math

import jax
import jax.numpy as jnp
from jax import lax
from jax.experimental import pallas as pl
from jax.experimental.pallas import tpu as pltpu
from jax.sharding import PartitionSpec as P

HD = 96
MESH_IDS = pl.DeviceIdType.MESH
SIDE = 4
MODEL = 1536
SEQ_ROWS = 512
OWN = 128
QKV = (0, 768)
OUT = (768, 1152)
GATE = (1152, 2176)
UP = (2176, 3200)
DOWN = (3200, 4224)
COLS = (384, 192, 192, 384, 1024, 1024, 1024)
WIDTH = 4224
ATTN_PARTS = (((0, 256), (256, 512)), ((512, 768), (768, 1152)))
MLP_PARTS = (((1152, 1920), (1920, 2688)), ((2688, 3456), (3456, 4224)))

norm_eps = 1e-05
rope_base = 100000.0
SCALING = 1.0 / math.sqrt(HD)


def cut(cols):
    return pl.ds(cols[0], cols[1] - cols[0])


def shift(place, step):
    return lax.rem(place + step + 2 * SIDE, SIDE)


class Place:
    def __init__(self):
        dp = lax.axis_index("dp")
        tensor = lax.axis_index("tensor")
        self.z_hi, self.x, self.y = dp // 16, (dp // 4) % 4, dp % 4
        self.z_lo, self.core = tensor // 2, tensor % 2
        self.dp, self.tensor = dp, tensor

    def device(self, z_hi, x, y, tensor):
        return (z_hi * 16 + x * 4 + y, tensor)

    def beside(self, axis, step):
        if axis == "x":
            return self.device(self.z_hi, shift(self.x, step), self.y, self.tensor)
        return self.device(self.z_hi, self.x, shift(self.y, step), self.tensor)

    def across(self):
        return self.device(1 - self.z_hi, self.x, self.y, self.tensor)

    def twin(self):
        return (self.dp, self.z_lo * 2 + 1 - self.core)

    def above(self):
        return (self.dp, (1 - self.z_lo) * 2 + self.core)

    def greet(self):
        targets = [self.beside(axis, step) for axis in ("x", "y") for step in (1, 2, 3)]
        targets += [self.across(), self.twin(), self.above()]
        barrier = pltpu.get_barrier_semaphore()
        for target in targets:
            pl.semaphore_signal(barrier, inc=1, device_id=target, device_id_type=MESH_IDS)
        pl.semaphore_wait(barrier, len(targets))


class Wire:
    def __init__(self, send_sems, recv_sems):
        self.send_sems, self.recv_sems = send_sems, recv_sems
        self.count = 0
        self.sent = []

    def slot(self):
        self.count += 1
        return self.count - 1

    def send(self, slot, source, target_ref, target):
        copy = pltpu.make_async_remote_copy(
            src_ref=source,
            dst_ref=target_ref,
            send_sem=self.send_sems.at[slot],
            recv_sem=self.recv_sems.at[slot],
            device_id=target,
            device_id_type=MESH_IDS,
        )
        copy.start()
        self.sent.append(copy)
        return copy

    def arrive(self, slot, landed, target):
        pltpu.make_async_remote_copy(
            src_ref=landed,
            dst_ref=landed,
            send_sem=self.send_sems.at[slot],
            recv_sem=self.recv_sems.at[slot],
            device_id=target,
            device_id_type=MESH_IDS,
        ).wait_recv()

    def release(self, copy):
        copy.wait_send()
        self.sent = [other for other in self.sent if other is not copy]

    def drain(self):
        for copy in self.sent:
            copy.wait_send()
        self.sent = []


class Local:
    def __init__(self, sems):
        self.sems, self.count, self.open = sems, 0, []

    def start(self, source, target):
        copy = pltpu.make_async_copy(source, target, self.sems.at[self.count])
        self.count += 1
        copy.start()
        self.open.append(copy)
        return copy

    def wait(self, copy):
        copy.wait()
        self.open = [other for other in self.open if other is not copy]

    def drain(self):
        for copy in self.open:
            copy.wait()
        self.open = []


def sum_small(wire, at, value_ref, landing, whole_group):
    rounds = []
    if whole_group:
        rounds += [[at.twin()], [at.above()]]
    rounds += [[at.across()]]
    rounds += [[at.beside(axis, step) for step in (1, 2, 3)] for axis in ("y", "x")]
    place = 0
    for targets in rounds:
        slots = [wire.slot() for _ in targets]
        copies = []
        for index, target in enumerate(targets):
            copies.append(wire.send(slots[index], value_ref, landing.at[place + index], target))
        yield
        total = value_ref[...]
        for index, target in enumerate(targets):
            wire.arrive(slots[index], landing.at[place + index], target)
            total = total + landing[place + index]
        for copy in copies:
            wire.release(copy)
        value_ref[...] = total
        place += len(targets)
    yield


class Spread:
    pieces = 2

    def __init__(self, wire, at, rows_ref):
        self.wire, self.at, self.rows_ref = wire, at, rows_ref
        self.near = wire.slot()
        self.over = [wire.slot() for _ in range(self.pieces)]
        self.passed = [wire.slot() for _ in range(self.pieces)]
        self.size = OWN // self.pieces
        self.copies = []

    def rows(self, tensor, piece=None):
        start = pl.multiple_of(tensor * OWN, OWN)
        if piece is None:
            return self.rows_ref.at[pl.ds(start, OWN)]
        return self.rows_ref.at[
            pl.ds(pl.multiple_of(start + piece * self.size, self.size), self.size)
        ]

    def start(self):
        at, wire = self.at, self.wire
        own = at.tensor
        for piece in range(self.pieces):
            block = self.rows(own, piece)
            self.copies.append(wire.send(self.over[piece], block, block, at.above()))
        self.copies.append(wire.send(self.near, self.rows(own), self.rows(own), at.twin()))

    def near_done(self):
        at = self.at
        self.wire.arrive(self.near, self.rows(at.z_lo * 2 + 1 - at.core), at.twin())

    def pass_on(self):
        at, wire = self.at, self.wire
        there = (1 - at.z_lo) * 2 + at.core
        for piece in range(self.pieces):
            block = self.rows(there, piece)
            wire.arrive(self.over[piece], block, at.above())
            self.copies.append(wire.send(self.passed[piece], block, block, at.twin()))

    def far_done(self):
        at = self.at
        there = (1 - at.z_lo) * 2 + 1 - at.core
        for piece in range(self.pieces):
            self.wire.arrive(self.passed[piece], self.rows(there, piece), at.twin())
        for copy in self.copies:
            self.wire.release(copy)


class Collect:
    pieces = 2

    def __init__(self, wire, at, part, help_ref, near_ref, over_ref):
        self.wire, self.at, self.part = wire, at, part
        self.help_ref, self.near_ref, self.over_ref = help_ref, near_ref, over_ref
        self.help = wire.slot()
        self.near = wire.slot()
        self.over = [wire.slot() for _ in range(self.pieces)]
        self.copies = []
        self.size = OWN // self.pieces

    def rows(self, z_lo, core):
        return pl.ds(pl.multiple_of((z_lo * 2 + core) * OWN, OWN), OWN)

    def other_ready(self):
        at = self.at
        block = self.part.at[self.rows(1 - at.z_lo, 1 - at.core)]
        self.copies.append(self.wire.send(self.help, block, self.help_ref, at.twin()))

    def own_ready(self):
        at = self.at
        block = self.part.at[self.rows(at.z_lo, 1 - at.core)]
        self.copies.append(self.wire.send(self.near, block, self.near_ref, at.twin()))

    def send_over(self):
        at = self.at
        self.wire.arrive(self.help, self.help_ref, at.twin())
        for piece in range(self.pieces):
            window = pl.ds(piece * self.size, self.size)
            start = ((1 - at.z_lo) * 2 + at.core) * OWN + piece * self.size
            rows = pl.ds(pl.multiple_of(start, self.size), self.size)
            total = self.part[rows, :].astype(jnp.float32) + self.help_ref[window, :].astype(
                jnp.float32
            )
            self.part[rows, :] = total.astype(jnp.bfloat16)
            self.copies.append(
                self.wire.send(
                    self.over[piece],
                    self.part.at[rows],
                    self.over_ref.at[window],
                    at.above(),
                )
            )

    def result(self):
        at = self.at
        self.wire.arrive(self.near, self.near_ref, at.twin())
        total = self.part[self.rows(at.z_lo, at.core), :].astype(jnp.float32) + self.near_ref[
            ...
        ].astype(jnp.float32)
        for piece in range(self.pieces):
            window = pl.ds(piece * self.size, self.size)
            self.wire.arrive(self.over[piece], self.over_ref.at[window], at.above())
        total = total + self.over_ref[...].astype(jnp.float32)
        for copy in self.copies:
            self.wire.release(copy)
        self.copies = []
        return total


def nn(left, right):
    return jnp.dot(left, right, preferred_element_type=jnp.float32)


def nt(left, right):
    return lax.dot_general(
        left, right, (((1,), (1,)), ((), ())), preferred_element_type=jnp.float32
    )


def tn(left, right):
    return lax.dot_general(
        left, right, (((0,), (0,)), ((), ())), preferred_element_type=jnp.float32
    )


def rope_tables(heads):
    half = HD // 2
    position = jnp.arange(SEQ_ROWS, dtype=jnp.float32)[:, None]
    exponent = 2.0 * jnp.arange(half, dtype=jnp.float32) / HD
    angles = position * (rope_base ** (-exponent))[None, :]
    cosine, sine = jnp.cos(angles), jnp.sin(angles)
    wide_cosine = jnp.concatenate([cosine, cosine], axis=1)
    wide_sine = jnp.concatenate([-sine, sine], axis=1)
    return jnp.tile(wide_cosine, (1, heads)), jnp.tile(wide_sine, (1, heads))


def swap_halves(values):
    width = values.shape[1]
    lane = lax.broadcasted_iota(jnp.int32, values.shape, 1)
    first = lax.rem(lane, HD) < HD // 2
    return jnp.where(
        first, pltpu.roll(values, width - HD // 2, 1), pltpu.roll(values, HD // 2, 1)
    )


def head_of(values, start):
    width = values.shape[1]
    moved = values if start == 0 else pltpu.roll(values, width - start, 1)
    moved = moved[:, :128]
    lane = lax.broadcasted_iota(jnp.int32, moved.shape, 1)
    return jnp.where(lane < HD, moved, 0.0)


def side_by_side(heads):
    tiles = []
    for tile in range(len(heads) * HD // 128):
        total = None
        lane = lax.broadcasted_iota(jnp.int32, heads[0].shape, 1)
        for index, head in enumerate(heads):
            start = index * HD - tile * 128
            if start <= -HD or start >= 128:
                continue
            moved = pltpu.roll(head, start % 128, 1) if start else head
            if start > 0 or start < 0:
                keep = (lane >= start) if start > 0 else (lane < start + HD)
                moved = jnp.where(keep, moved, 0.0)
            total = moved if total is None else total + moved
        tiles.append(total)
    return jnp.concatenate(tiles, axis=1)


def chip_rows(z_lo):
    return pl.ds(pl.multiple_of(z_lo * 256, 256), 256)


def weight(w_ref, layer, cols):
    value = w_ref[layer, :, :, cols]
    return value.reshape(MODEL, value.shape[-1])


def turn_rows(source, target):
    def tile(index, carry):
        start = pl.multiple_of(index * 256, 256)
        target[pl.ds(start, 256), :] = source[:, pl.ds(start, 256)].T
        return carry

    lax.fori_loop(0, MODEL // 256, tile, 0)


def gather_job(wire, at, full, layer, group):
    parts = []
    for (first, second), (left, right) in zip((("y", "x"), ("x", "y")), group):

        def block(first_step, second_step, cols, first=first):
            x_step, y_step = (
                (first_step, second_step) if first == "x" else (second_step, first_step)
            )
            row = shift(at.x, x_step) * 192 + shift(at.y, y_step) * 48
            return full.at[layer, :, pl.ds(pl.multiple_of(row, 48), 48), cut(cols)]

        parts.append(
            dict(
                first=first,
                second=second,
                left=left,
                right=right,
                whole=(left[0], right[1]),
                block=block,
                one={s: wire.slot() for s in (1, -1)},
                two={s: wire.slot() for s in (1, -1)},
                side={(f, s): wire.slot() for f in (0, -1, 1, 2) for s in (1, -1)},
                far={(f, s): wire.slot() for f in (0, -1, 1, 2) for s in (1, -1)},
            )
        )

    def half(part, step):
        return part["left"] if step == 1 else part["right"]

    def one_start(part, step):
        piece = part["block"](0, 0, part["whole"])
        wire.send(part["one"][step], piece, piece, at.beside(part["first"], step))

    def side_start(part, first_step):
        for step in (1, -1):
            piece = part["block"](first_step, 0, part["whole"])
            wire.send(
                part["side"][first_step, step], piece, piece, at.beside(part["second"], step)
            )

    def one_done(part, step):
        target = at.beside(part["first"], step)
        wire.arrive(part["one"][step], part["block"](-step, 0, part["whole"]), target)
        piece = part["block"](-step, 0, half(part, step))
        wire.send(part["two"][step], piece, piece, target)

    def two_done(part):
        for step in (1, -1):
            piece = part["block"](2, 0, half(part, step))
            wire.arrive(part["two"][step], piece, at.beside(part["first"], step))

    def side_done(part, first_step):
        for step in (1, -1):
            target = at.beside(part["second"], step)
            landed = part["block"](first_step, -step, part["whole"])
            wire.arrive(part["side"][first_step, step], landed, target)
            piece = part["block"](first_step, -step, half(part, step))
            wire.send(part["far"][first_step, step], piece, piece, target)

    def far_done(part, first_step):
        for step in (1, -1):
            piece = part["block"](first_step, 2, half(part, step))
            wire.arrive(part["far"][first_step, step], piece, at.beside(part["second"], step))

    for part in parts:
        for step in (1, -1):
            one_start(part, step)
    for part in parts:
        side_start(part, 0)
    yield
    for step in (1, -1):
        for part in parts:
            one_done(part, step)
    for first_step in (-1, 1):
        for part in parts:
            side_start(part, first_step)
    yield
    for part in parts:
        two_done(part)
    for part in parts:
        side_start(part, 2)
    for part in parts:
        side_done(part, 0)
    yield
    for first_step in (-1, 1):
        for part in parts:
            side_done(part, first_step)
    yield
    for part in parts:
        side_done(part, 2)
    yield
    for first_step in (0, -1, 1, 2):
        for part in parts:
            far_done(part, first_step)
    yield


class Gather:
    def __init__(self, wire, local, at, shard, full, kept):
        self.wire, self.local, self.at, self.shard = wire, local, at, shard
        self.full, self.kept = full, kept
        self.groups = [
            (layer, group) for layer in range(2) for group in (ATTN_PARTS, MLP_PARTS)
        ]
        self.jobs = [gather_job(wire, at, full, *pair) for pair in self.groups]
        self.slots = [wire.slot() for _ in self.groups]
        self.own = []
        order = [(0, 0), (0, 1)]
        for index in range(len(self.jobs)):
            order += [(index, 2), (index + 1, 0), (index, 3), (index, 4), (index + 1, 1)]
            order += [(index, 5)]
        self.order = [pair for pair in order if pair[0] < len(self.jobs)]
        self.done = 0

    def columns(self, index):
        group = self.groups[index][1]
        return cut((group[0][0][0], group[1][1][1]))

    def mine(self, z_hi):
        row = self.at.x * 192 + self.at.y * 48
        return (z_hi, pl.ds(pl.multiple_of(row, 48), 48))

    def begin(self):
        at = self.at
        z_own, rows = self.mine(at.z_hi)
        for index, (layer, _) in enumerate(self.groups):
            cols = self.columns(index)
            source = self.shard.at[layer, :, cols]
            target = self.full.at[layer, z_own, rows, cols]
            self.wire.send(self.slots[index], source, target, at.across())
            self.own.append(self.local.start(source, target))

    def step(self, count=1):
        for _ in range(count):
            if self.done == len(self.order):
                return
            index, stage = self.order[self.done]
            self.done += 1
            layer = self.groups[index][0]
            cols = self.columns(index)
            if stage == 0:
                self.local.wait(self.own[index])
                z_other, rows = self.mine(1 - self.at.z_hi)
                landed = self.full.at[layer, z_other, rows, cols]
                self.wire.arrive(self.slots[index], landed, self.at.across())
            next(self.jobs[index])
            if stage == 5:
                self.local.start(
                    self.full.at[layer, :, :, cols], self.kept.at[layer, :, :, cols]
                )

    def until(self, index):
        while (index, 5) in self.order[self.done :]:
            self.step()


def normed(rows_in, gain):
    inverse = lax.rsqrt(jnp.mean(rows_in * rows_in, axis=-1, keepdims=True) + norm_eps)
    return (rows_in * inverse * gain).astype(jnp.bfloat16)


def project_heads(layer, rows, n1, w, cosine, sine, q_ref, k_ref, v_ref):
    left = n1[layer, rows, :]
    cosine_rows, sine_rows = cosine[rows, :], sine[rows, :]
    query = nn(left, weight(w, layer, pl.ds(0, 384)))
    turned = query * cosine_rows + swap_halves(query) * sine_rows
    for head in range(4):
        q_ref[layer, head, rows, :] = head_of(turned, head * HD).astype(jnp.bfloat16)
    both = nn(left, weight(w, layer, pl.ds(384, 384)))
    turned = both * cosine_rows + swap_halves(both) * sine_rows
    for head in range(2):
        k_ref[layer, head, rows, :] = head_of(turned, head * HD).astype(jnp.bfloat16)
        v_ref[layer, head, rows, :] = head_of(both, 192 + head * HD).astype(jnp.bfloat16)


def attend(layer, q_ref, k_ref, v_ref, p_ref, o_ref):
    for block in range(4):
        rows = pl.ds(block * 128, 128)
        keys = (block + 1) * 128
        outputs = []
        for head in range(2):
            pair = jnp.concatenate(
                [q_ref[layer, 2 * head, rows, :], q_ref[layer, 2 * head + 1, rows, :]], axis=0
            )
            scores = nt(pair, k_ref[layer, head, pl.ds(0, keys), :]) * SCALING
            row = lax.broadcasted_iota(jnp.int32, (256, keys), 0) % 128 + block * 128
            key = lax.broadcasted_iota(jnp.int32, (256, keys), 1)
            scores = jnp.where(row >= key, scores, -1e30)
            peak = jnp.max(scores, axis=-1, keepdims=True)
            exponent = jnp.exp(scores - peak)
            inverse = 1.0 / jnp.sum(exponent, axis=-1, keepdims=True)
            shares = (exponent * inverse).astype(jnp.bfloat16)
            p_ref[layer, 2 * head, rows, pl.ds(0, keys)] = shares[:128]
            p_ref[layer, 2 * head + 1, rows, pl.ds(0, keys)] = shares[128:]
            out = nn(shares, v_ref[layer, head, pl.ds(0, keys), :])
            outputs += [out[:128], out[128:]]
        o_ref[layer, rows, :] = side_by_side(outputs).astype(jnp.bfloat16)


def out_partial(layer, rows, o_ref, w, part):
    left = o_ref[layer, rows, :]
    for half in range(2):
        for tile in range(3):
            right = w[layer, half, pl.ds(tile * 256, 256), cut(OUT)]
            part[rows, pl.ds(half * 768 + tile * 256, 256)] = nt(left, right).astype(jnp.bfloat16)


def hidden_rows(layer, rows, n2, w, g_ref, u_ref, a_ref):
    left = n2[layer, rows, :]

    def tile(index, carry):
        start = pl.multiple_of(index * 256, 256)
        gate = nn(left, weight(w, layer, pl.ds(GATE[0] + start, 256)))
        up = nn(left, weight(w, layer, pl.ds(UP[0] + start, 256)))
        hidden = gate * up / (1.0 + jnp.exp(-gate))
        g_ref[layer, rows, pl.ds(start, 256)] = gate.astype(g_ref.dtype)
        u_ref[layer, rows, pl.ds(start, 256)] = up.astype(u_ref.dtype)
        a_ref[layer, rows, pl.ds(start, 256)] = hidden.astype(jnp.bfloat16)
        return carry

    lax.fori_loop(0, 4, tile, 0)


def down_partial(layer, rows, a_ref, w, part):
    left = a_ref[layer, rows, :]
    for half in range(2):

        def tile(index, carry, half=half):
            start = pl.multiple_of(index * 256, 256)
            right = w[layer, half, pl.ds(start, 256), cut(DOWN)]
            part[rows, pl.ds(pl.multiple_of(half * 768 + start, 256), 256)] = nt(
                left, right
            ).astype(jnp.bfloat16)
            return carry

        lax.fori_loop(0, 3, tile, 0)


def forward_kernel(
    shard,
    gains_placed,
    tokens,
    cosine,
    sine,
    w_kept,
    gains,
    output,
    n1_kept,
    n2_kept,
    q_kept,
    k_kept,
    v_kept,
    p_kept,
    o_kept,
    g_kept,
    u_kept,
    a_kept,
    x_kept,
    h_kept,
    w,
    n1,
    n2,
    q_ref,
    k_ref,
    v_ref,
    p_ref,
    o_ref,
    g_ref,
    u_ref,
    a_ref,
    x_ref,
    h_ref,
    n1_turned,
    n2_turned,
    part,
    help_ref,
    near_ref,
    over_ref,
    gains_landing,
    send_sems,
    recv_sems,
    local_sems,
):
    at = Place()
    at.greet()
    wire = Wire(send_sems, recv_sems)
    local = Local(local_sems)
    gather = Gather(wire, local, at, shard, w, w_kept)
    gather.begin()
    gather.step()
    gains[...] = gains_placed[...]
    rounds = sum_small(wire, at, gains, gains_landing, False)
    for _ in rounds:
        gather.step()
    x_ref[0] = tokens[...].astype(jnp.float32)
    own = pl.ds(pl.multiple_of(at.tensor * OWN, OWN), OWN)
    here, there = chip_rows(at.z_lo), chip_rows(1 - at.z_lo)
    turn = 0

    def collector():
        nonlocal turn
        turn += 1
        slot = turn % 2
        return Collect(
            wire, at, part, help_ref.at[slot], near_ref.at[slot], over_ref.at[slot]
        )

    turning = [None, None]
    for layer in range(2):
        n1[layer, own, :] = normed(x_ref[layer], gains[pl.ds(2 * layer, 1), :])
        spread = Spread(wire, at, n1.at[layer])
        spread.start()
        gather.until(2 * layer)
        heads = (n1, w, cosine, sine, q_ref, k_ref, v_ref)
        spread.near_done()
        project_heads(layer, here, *heads)
        gather.step()
        spread.pass_on()
        spread.far_done()
        project_heads(layer, there, *heads)
        for source, target in ((q_ref, q_kept), (k_ref, k_kept), (v_ref, v_kept)):
            local.start(source.at[layer], target.at[layer])
        gather.step()
        attend(layer, q_ref, k_ref, v_ref, p_ref, o_ref)
        for source, target in ((p_ref, p_kept), (o_ref, o_kept)):
            local.start(source.at[layer], target.at[layer])
        collect = collector()
        out_partial(layer, there, o_ref, w, part)
        collect.other_ready()
        out_partial(layer, here, o_ref, w, part)
        collect.own_ready()
        collect.send_over()
        if layer == 1:
            local.wait(turning[0])
        turn_rows(n1.at[layer], n1_turned)
        turning[0] = local.start(n1_turned, n1_kept.at[layer])
        gather.step()
        h_ref[layer] = x_ref[layer] + collect.result()
        n2[layer, own, :] = normed(h_ref[layer], gains[pl.ds(2 * layer + 1, 1), :])
        spread = Spread(wire, at, n2.at[layer])
        spread.start()
        gather.until(2 * layer + 1)
        spread.near_done()
        hidden_rows(layer, here, n2, w, g_ref, u_ref, a_ref)
        gather.step()
        spread.pass_on()
        spread.far_done()
        hidden_rows(layer, there, n2, w, g_ref, u_ref, a_ref)
        for source, target in (
            (h_ref, h_kept),
            (g_ref, g_kept),
            (u_ref, u_kept),
            (a_ref, a_kept),
        ):
            local.start(source.at[layer], target.at[layer])
        collect = collector()
        down_partial(layer, there, a_ref, w, part)
        collect.other_ready()
        down_partial(layer, here, a_ref, w, part)
        collect.own_ready()
        collect.send_over()
        if layer == 1:
            local.wait(turning[1])
        turn_rows(n2.at[layer], n2_turned)
        turning[1] = local.start(n2_turned, n2_kept.at[layer])
        gather.step()
        total = h_ref[layer] + collect.result()
        if layer == 0:
            x_ref[1] = total
            local.start(x_ref.at[1], x_kept)
        else:
            output[...] = total.astype(jnp.bfloat16)
    local.drain()
    wire.drain()


KEEP = jnp.bfloat16


def run_forward(shard, gains_placed, tokens, cosine, sine):
    def kept(*shape, kind=jnp.bfloat16):
        return jax.ShapeDtypeStruct(shape, kind)

    def held(*shape, kind=jnp.bfloat16):
        return pltpu.VMEM(shape, kind)

    vmem = pl.BlockSpec(memory_space=pltpu.VMEM)
    hbm = pl.BlockSpec(memory_space=pl.ANY)
    float32 = jnp.float32
    wires = 4 * 41 + 7 + 8 * 5 + 4
    return pl.pallas_call(
        forward_kernel,
        out_shape=(
            kept(2, 2, 768, WIDTH),
            kept(8, MODEL, kind=float32),
            kept(OWN, MODEL),
            kept(2, MODEL, SEQ_ROWS),
            kept(2, MODEL, SEQ_ROWS),
            kept(2, 4, SEQ_ROWS, 128),
            kept(2, 2, SEQ_ROWS, 128),
            kept(2, 2, SEQ_ROWS, 128),
            kept(2, 4, SEQ_ROWS, SEQ_ROWS),
            kept(2, SEQ_ROWS, 384),
            kept(2, SEQ_ROWS, 1024, kind=KEEP),
            kept(2, SEQ_ROWS, 1024, kind=KEEP),
            kept(2, SEQ_ROWS, 1024),
            kept(OWN, MODEL, kind=float32),
            kept(2, OWN, MODEL, kind=float32),
        ),
        in_specs=[vmem] * 5,
        out_specs=(hbm, vmem, vmem) + (hbm,) * 12,
        scratch_shapes=[
            held(2, 2, 768, WIDTH),
            held(2, SEQ_ROWS, MODEL),
            held(2, SEQ_ROWS, MODEL),
            held(2, 4, SEQ_ROWS, 128),
            held(2, 2, SEQ_ROWS, 128),
            held(2, 2, SEQ_ROWS, 128),
            held(2, 4, SEQ_ROWS, SEQ_ROWS),
            held(2, SEQ_ROWS, 384),
            held(2, SEQ_ROWS, 1024, kind=KEEP),
            held(2, SEQ_ROWS, 1024, kind=KEEP),
            held(2, SEQ_ROWS, 1024),
            held(2, OWN, MODEL, kind=float32),
            held(2, OWN, MODEL, kind=float32),
            held(MODEL, SEQ_ROWS),
            held(MODEL, SEQ_ROWS),
            held(SEQ_ROWS, MODEL),
            held(2, OWN, MODEL),
            held(2, OWN, MODEL),
            held(2, OWN, MODEL),
            held(7, 8, MODEL, kind=float32),
            pltpu.SemaphoreType.DMA((wires,)),
            pltpu.SemaphoreType.DMA((wires,)),
            pltpu.SemaphoreType.DMA((40,)),
        ],
        compiler_params=pltpu.CompilerParams(
            collective_id=0, has_side_effects=True, vmem_limit_bytes=62 * 2**20
        ),
        name="forward",
    )(shard, gains_placed, tokens, cosine, sine)


JOBS = (
    (((3200, 3456), (3456, 3712)), ((3712, 3968), (3968, 4224))),
    (((1152, 1408), (1408, 1664)), ((1664, 1920), (1920, 2176))),
    (((2176, 2432), (2432, 2688)), ((2688, 2944), (2944, 3200))),
    (((0, 256), (256, 512)), ((512, 768), (768, 1152))),
)
JOB_WIDTH = 1152
SETS = 2


def add_rows(target, terms):
    lead = target.shape[:-2]

    def step(index, carry):
        window = ()
        if lead:
            window = (index // lead[1], index % lead[1])
        total = None
        for term in terms:
            value = term[window + (slice(None), slice(None))].astype(jnp.float32)
            total = value if total is None else total + value
        target[window + (slice(None), slice(None))] = total.astype(target.dtype)
        return carry

    lax.fori_loop(0, math.prod(lead), step, 0)


def scatter_job(wire, local, at, grads, layer, group, bufs, finish):
    one, two_up, two_down, small_one, small_up, small_down, near_side, near_own = bufs
    base = group[0][0][0]
    parts = []
    for (first, second), (left, right) in zip((("y", "x"), ("x", "y")), group):

        def region(step, cols, second=second):
            if second == "x":
                return grads.at[layer, :, shift(at.x, step), :, :, cut(cols)]
            return grads.at[layer, :, :, shift(at.y, step), :, cut(cols)]

        def mine(step, cols, first=first):
            place = at.y if first == "y" else at.x
            return two_up.at[:, shift(place, step), :, inside(cols)]

        parts.append(
            dict(
                first=first,
                second=second,
                left=left,
                right=right,
                whole=(left[0], right[1]),
                region=region,
                mine=mine,
                **{
                    name: {s: wire.slot() for s in (1, -1)}
                    for name in ("far", "raw", "sum", "far2", "raw2", "sum2")
                },
            )
        )

    def inside(cols):
        return pl.ds(cols[0] - base, cols[1] - cols[0])

    def half(part, step):
        return part["left"] if step == 1 else part["right"]

    def other(part, step):
        return part["right"] if step == 1 else part["left"]

    def big(ref, cols):
        return ref.at[:, :, :, inside(cols)]

    def small(ref, cols):
        return ref.at[:, :, inside(cols)]

    copies = []
    near = {}
    for part in parts:
        for step in (1, -1):
            cols = half(part, step)
            target = at.beside(part["second"], step)
            copies.append(
                wire.send(part["far"][step], part["region"](2, cols), big(one, cols), target)
            )
    for number, part in enumerate(parts):
        for step in (1, -1):
            cols = other(part, step)
            landing = two_up if step == 1 else two_down
            target = at.beside(part["second"], step)
            copies.append(
                wire.send(part["raw"][step], part["region"](step, cols), big(landing, cols), target)
            )
            cols = half(part, step)
            near[number, step] = local.start(part["region"](step, cols), big(near_side, cols))
        cols = part["whole"]
        near[number, 0] = local.start(part["region"](0, cols), big(near_own, cols))
    yield
    for step in (1, -1):
        for number, part in enumerate(parts):
            cols = half(part, step)
            target = at.beside(part["second"], step)
            piece = big(one, cols)
            local.wait(near[number, step])
            wire.arrive(part["far"][step], piece, target)
            add_rows(piece, (piece, big(near_side, cols)))
            landing = two_up if step == 1 else two_down
            copies.append(wire.send(part["sum"][step], piece, big(landing, cols), target))
    yield
    for number, part in enumerate(parts):
        local.wait(near[number, 0])
        for step in (1, -1):
            target = at.beside(part["second"], step)
            landing = two_up if step == 1 else two_down
            for name, cols in (("raw", other(part, step)), ("sum", half(part, step))):
                wire.arrive(part[name][step], big(landing, cols), target)
        cols = part["whole"]
        add_rows(big(two_up, cols), (big(near_own, cols), big(two_up, cols), big(two_down, cols)))
        for step in (1, -1):
            target = at.beside(part["first"], step)
            cols = half(part, step)
            copies.append(
                wire.send(part["far2"][step], part["mine"](2, cols), small(small_one, cols), target)
            )
            cols = other(part, step)
            landing = small_up if step == 1 else small_down
            copies.append(
                wire.send(part["raw2"][step], part["mine"](step, cols), small(landing, cols), target)
            )
    yield
    for step in (1, -1):
        for part in parts:
            cols = half(part, step)
            target = at.beside(part["first"], step)
            piece = small(small_one, cols)
            wire.arrive(part["far2"][step], piece, target)
            own = part["mine"](step, cols)
            for z_hi in range(2):
                add_rows(piece.at[z_hi], (piece.at[z_hi], own.at[z_hi]))
            landing = small_up if step == 1 else small_down
            copies.append(wire.send(part["sum2"][step], piece, small(landing, cols), target))
    yield
    for part in parts:
        for step in (1, -1):
            target = at.beside(part["first"], step)
            landing = small_up if step == 1 else small_down
            for name, cols in (("raw2", other(part, step)), ("sum2", half(part, step))):
                wire.arrive(part[name][step], small(landing, cols), target)
        cols = part["whole"]
        finish(
            cols,
            [
                [
                    ref.at[z_hi]
                    for ref in (part["mine"](0, cols), small(small_up, cols), small(small_down, cols))
                ]
                for z_hi in (1 - at.z_hi, at.z_hi)
            ],
        )
    for copy in copies:
        wire.release(copy)
    yield


class Scatter:
    def __init__(self, wire, local, at, grads, summed, sets, leaving, landed, credits):
        self.wire, self.local, self.at, self.grads = wire, local, at, grads
        self.summed, self.leaving, self.landed, self.credits = summed, leaving, landed, credits
        self.groups = [(layer, group) for layer in (1, 0) for group in JOBS]
        self.last = []
        self.jobs = []
        for index, (layer, group) in enumerate(self.groups):
            bufs = tuple(ref.at[index % SETS] for ref in sets)
            self.jobs.append(
                scatter_job(
                    wire, local, at, grads, layer, group, bufs, self.finisher(index, layer, group)
                )
            )
        order = [(0, 0), (0, 1)]
        count = len(self.jobs)
        for index in range(count):
            order += [(index + 1, 0), (index, 2), (index, 3), (index + 1, 1), (index, 4)]
            order += [(index - 1, 5)]
        order += [(count - 1, 5)]
        self.order = [pair for pair in order if 0 <= pair[0] < count]
        self.done = 0
        self.ready = 0

    def finisher(self, index, layer, group):
        wire, at = self.wire, self.at
        base = group[0][0][0]

        def finish(cols, terms):
            theirs, own = terms
            window = pl.ds(cols[0] - base, cols[1] - cols[0])
            piece = self.leaving.at[index, :, window]
            add_rows(piece, theirs)
            slot = wire.slot()
            landing = self.landed.at[index, :, window]
            wire.send(slot, piece, landing, at.across())
            target = self.summed.at[layer, :, cut(cols)]
            add_rows(target, own)
            self.last.append((index, slot, landing, target))

        return finish

    def step(self, count=1):
        at = self.at
        for _ in range(count):
            if self.done == len(self.order):
                return
            index, stage = self.order[self.done]
            if index >= self.ready:
                return
            self.done += 1
            ways = [(axis, step) for axis in ("x", "y") for step in (1, -1)]
            if stage == 5:
                for job, slot, landing, target in self.last:
                    if job == index:
                        self.wire.arrive(slot, landing, at.across())
                        add_rows(target, (target, landing))
                continue
            if stage == 0 and index >= SETS:
                for number in range(4):
                    pl.semaphore_wait(self.credits.at[number], 1)
            next(self.jobs[index])
            if stage == 4 and index + SETS < len(self.jobs):
                for number, (axis, step) in enumerate(ways):
                    pl.semaphore_signal(
                        self.credits.at[number],
                        inc=1,
                        device_id=at.beside(axis, step),
                        device_id_type=MESH_IDS,
                    )


def norm_backward(rows_in, gain, grad_normed):
    inverse = lax.rsqrt(jnp.mean(rows_in * rows_in, axis=-1, keepdims=True) + norm_eps)
    scaled = rows_in * inverse
    grad_gain = jnp.sum(grad_normed * scaled, axis=0, keepdims=True)
    grad_scaled = grad_normed * gain
    grad_input = inverse * (
        grad_scaled - scaled * jnp.mean(grad_scaled * scaled, axis=-1, keepdims=True)
    )
    return grad_input, grad_gain


def hidden_back(rows, dm, w, g_ref, u_ref, dgu):
    left = dm[rows, :]

    def tile(index, carry):
        start = pl.multiple_of(index * 256, 256)
        grad = nn(left, weight(w, 0, pl.ds(DOWN[0] + start, 256)))
        gate = g_ref[rows, pl.ds(start, 256)].astype(jnp.float32)
        up = u_ref[rows, pl.ds(start, 256)].astype(jnp.float32)
        sigma = 1.0 / (1.0 + jnp.exp(-gate))
        dgu[rows, pl.ds(start, 256)] = (
            grad * up * sigma * (1.0 + gate * (1.0 - sigma))
        ).astype(jnp.bfloat16)
        dgu[rows, pl.ds(1024 + start, 256)] = (grad * gate * sigma).astype(jnp.bfloat16)
        return carry

    lax.fori_loop(0, 4, tile, 0)


def rows_partial(rows, left_ref, w, cols, part):
    left = left_ref[rows, :]
    for half in range(2):

        def tile(index, carry, half=half):
            start = pl.multiple_of(index * 256, 256)
            right = w[0, half, pl.ds(start, 256), cut(cols)]
            part[rows, pl.ds(pl.multiple_of(half * 768 + start, 256), 256)] = nt(
                left, right
            ).astype(jnp.bfloat16)
            return carry

        lax.fori_loop(0, 3, tile, 0)


def attend_back(q_ref, k_ref, v_ref, p_ref, do_ref, dk_ref, dv_ref, cosine, sine, dqkv):
    dk_ref[...] = jnp.zeros_like(dk_ref)
    dv_ref[...] = jnp.zeros_like(dv_ref)
    for block in range(4):
        rows = pl.ds(block * 128, 128)
        keys = pl.ds(0, (block + 1) * 128)
        queries = []
        for head in range(2):
            both = (2 * head, 2 * head + 1)
            shares = jnp.concatenate([p_ref[h, rows, keys] for h in both], axis=0)
            pair = jnp.concatenate([q_ref[h, rows, :] for h in both], axis=0)
            grad = jnp.concatenate([do_ref[h, rows, :] for h in both], axis=0)
            wide = shares.astype(jnp.float32)
            grad_shares = nt(grad, v_ref[head, keys, :])
            inner = jnp.sum(grad_shares * wide, axis=-1, keepdims=True)
            grad_scores = (wide * (grad_shares - inner)).astype(jnp.bfloat16)
            grad_pair = nn(grad_scores, k_ref[head, keys, :]) * SCALING
            queries += [grad_pair[:128], grad_pair[128:]]
            dk_ref[head, :, keys] += nn(pair.T, grad_scores)
            dv_ref[head, :, keys] += nn(grad.T, shares)
        grad_rows = side_by_side(queries)
        turned = grad_rows * cosine[rows, :] - swap_halves(grad_rows) * sine[rows, :]
        dqkv[rows, pl.ds(0, 384)] = turned.astype(jnp.bfloat16)
    both = side_by_side(
        [dk_ref[0].T * SCALING, dk_ref[1].T * SCALING, dv_ref[0].T, dv_ref[1].T]
    )
    turned = both * cosine[...] - swap_halves(both) * sine[...]
    lane = lax.broadcasted_iota(jnp.int32, both.shape, 1)
    dqkv[:, pl.ds(384, 384)] = jnp.where(lane < 192, turned, both).astype(jnp.bfloat16)


def backward_kernel(
    gains,
    grad_out,
    tokens,
    cosine,
    sine,
    x_second,
    h_ref,
    w_kept,
    n1_kept,
    n2_kept,
    q_kept,
    k_kept,
    v_kept,
    p_kept,
    o_kept,
    g_kept,
    u_kept,
    a_kept,
    input_grad,
    summed,
    gains_grad,
    grads,
    w,
    n1_turned,
    n2_turned,
    q_ref,
    k_ref,
    v_ref,
    p_ref,
    o_ref,
    g_ref,
    u_ref,
    a_ref,
    dm,
    turned,
    dgu,
    do_ref,
    dk_ref,
    dv_ref,
    dqkv,
    dx,
    part,
    help_ref,
    near_ref,
    over_ref,
    staged,
    one,
    two_up,
    two_down,
    small_one,
    small_up,
    small_down,
    near_side,
    near_own,
    leaving,
    landed,
    gains_landing,
    send_sems,
    recv_sems,
    local_sems,
    credits,
):
    at = Place()
    at.greet()
    wire = Wire(send_sems, recv_sems)
    local = Local(local_sems)
    sets = (one, two_up, two_down, small_one, small_up, small_down, near_side, near_own)
    scatter = Scatter(wire, local, at, grads, summed, sets, leaving, landed, credits)
    own = pl.ds(pl.multiple_of(at.tensor * OWN, OWN), OWN)
    here, there = chip_rows(at.z_lo), chip_rows(1 - at.z_lo)
    turn = 0

    def collector():
        nonlocal turn
        turn += 1
        slot = turn % 2
        return Collect(
            wire, at, part, help_ref.at[slot], near_ref.at[slot], over_ref.at[slot]
        )

    loads = {}

    def load(layer, names):
        pairs = dict(
            n1=(n1_kept, n1_turned),
            n2=(n2_kept, n2_turned),
            q=(q_kept, q_ref),
            k=(k_kept, k_ref),
            v=(v_kept, v_ref),
            p=(p_kept, p_ref),
            o=(o_kept, o_ref),
            g=(g_kept, g_ref),
            u=(u_kept, u_ref),
            a=(a_kept, a_ref),
        )
        columns = dict(down=DOWN, gu=(GATE[0], UP[1]), out=OUT, qkv=QKV)
        for name in names:
            if name in columns:
                cols = cut(columns[name])
                loads[name] = local.start(w_kept.at[layer, :, :, cols], w.at[0, :, :, cols])
            else:
                kept, held = pairs[name]
                loads[name] = local.start(kept.at[layer], held)

    def ready(*names):
        for name in names:
            local.wait(loads.pop(name))

    mlp_names = ("down", "g", "u", "gu", "a", "n2")
    attn_names = ("out", "v", "p", "k", "q", "qkv", "o", "n1")
    load(1, mlp_names)
    load(1, attn_names)
    staging = [None, None]
    tiles = 0

    def keep_grads(layer, left, right_ref, start, width, column):
        nonlocal tiles
        for tile in range(0, width, 256):
            size = min(256, width - tile)
            slot = tiles % 2
            tiles += 1
            if staging[slot] is not None:
                local.wait(staging[slot])
            product = nn(left[...], right_ref[:, pl.ds(start + tile, size)])
            staged[slot, :, :, :, :, pl.ds(0, size)] = product.astype(jnp.bfloat16).reshape(
                2, SIDE, SIDE, 48, size
            )
            staging[slot] = local.start(
                staged.at[slot, :, :, :, :, pl.ds(0, size)],
                grads.at[layer, :, :, :, :, pl.ds(column + tile, size)],
            )

    def grads_kept():
        for slot in range(2):
            if staging[slot] is not None:
                local.wait(staging[slot])
                staging[slot] = None
        scatter.ready += 1

    gains_grad[...] = jnp.zeros_like(gains_grad)
    dx[0] = grad_out[...].astype(jnp.float32)
    for layer in (1, 0):
        dm[0, own, :] = dx[0].astype(jnp.bfloat16)
        spread = Spread(wire, at, dm.at[0])
        spread.start()
        spread.near_done()
        ready("down", "g", "u")
        hidden_back(here, dm.at[0], w, g_ref, u_ref, dgu)
        if layer == 0:
            scatter.step()
        spread.pass_on()
        spread.far_done()
        hidden_back(there, dm.at[0], w, g_ref, u_ref, dgu)
        collect = collector()
        ready("gu")
        rows_partial(there, dgu, w, (GATE[0], UP[1]), part)
        collect.other_ready()
        rows_partial(here, dgu, w, (GATE[0], UP[1]), part)
        collect.own_ready()
        collect.send_over()
        if layer == 0:
            scatter.step(2)
        turn_rows(dm.at[0], turned)
        ready("a")
        keep_grads(layer, turned, a_ref, 0, 1024, DOWN[0])
        grads_kept()
        scatter.step()
        if layer == 1:
            total = collect.result()
        ready("n2")
        keep_grads(layer, n2_turned, dgu, 0, 1024, GATE[0])
        grads_kept()
        if layer == 0:
            total = collect.result()
        normed_grad, gain_row = norm_backward(
            h_ref[layer], gains[pl.ds(2 * layer + 1, 1), :], total
        )
        gains_grad[pl.ds(2 * layer + 1, 1), :] = gain_row
        dx[1] = dx[0] + normed_grad
        dm[1, own, :] = dx[1].astype(jnp.bfloat16)
        spread = Spread(wire, at, dm.at[1])
        spread.start()
        scatter.step(2)
        keep_grads(layer, n2_turned, dgu, 1024, 1024, UP[0])
        grads_kept()
        if layer == 1:
            load(0, mlp_names)
        ready("out")
        spread.near_done()

        def heads_back(rows):
            grad = nn(dm[1, rows, :], weight(w, 0, cut(OUT)))
            for head in range(4):
                do_ref[head, rows, :] = head_of(grad, head * HD).astype(jnp.bfloat16)

        heads_back(here)
        spread.pass_on()
        spread.far_done()
        heads_back(there)
        ready("v", "p", "k", "q")
        attend_back(
            q_ref, k_ref, v_ref, p_ref, do_ref, dk_ref, dv_ref, cosine, sine, dqkv
        )
        scatter.step()
        collect = collector()
        ready("qkv")
        rows_partial(there, dqkv, w, QKV, part)
        collect.other_ready()
        rows_partial(here, dqkv, w, QKV, part)
        collect.own_ready()
        collect.send_over()
        turn_rows(dm.at[1], turned)
        ready("o", "n1")
        keep_grads(layer, turned, o_ref, 0, 384, OUT[0])
        keep_grads(layer, n1_turned, dqkv, 0, 768, QKV[0])
        grads_kept()
        if layer == 1:
            load(0, attn_names)
        scatter.step(2)
        total = collect.result()
        rows_in = tokens[...].astype(jnp.float32) if layer == 0 else x_second[...]
        normed_grad, gain_row = norm_backward(rows_in, gains[pl.ds(2 * layer, 1), :], total)
        gains_grad[pl.ds(2 * layer, 1), :] = gain_row
        dx[0] = dx[1] + normed_grad
    input_grad[...] = dx[0]
    rounds = sum_small(wire, at, gains_grad, gains_landing, True)
    for _ in rounds:
        scatter.step()
    while scatter.done < len(scatter.order):
        scatter.step()
    local.drain()
    wire.drain()


def run_backward(gains, grad_out, tokens, cosine, sine, x_second, h, kept):
    def held(*shape, kind=jnp.bfloat16):
        return pltpu.VMEM(shape, kind)

    vmem = pl.BlockSpec(memory_space=pltpu.VMEM)
    hbm = pl.BlockSpec(memory_space=pl.ANY)
    float32 = jnp.float32
    wires = 8 * 26 + 9 + 8 * 5 + 4
    return pl.pallas_call(
        backward_kernel,
        out_shape=(
            jax.ShapeDtypeStruct((OWN, MODEL), float32),
            jax.ShapeDtypeStruct((2, 48, WIDTH), float32),
            jax.ShapeDtypeStruct((8, MODEL), float32),
            jax.ShapeDtypeStruct((2, 2, SIDE, SIDE, 48, WIDTH), jnp.bfloat16),
        ),
        in_specs=[vmem] * 7 + [hbm] * len(kept),
        out_specs=(vmem, vmem, vmem, hbm),
        scratch_shapes=[
            held(1, 2, 768, WIDTH),
            held(MODEL, SEQ_ROWS),
            held(MODEL, SEQ_ROWS),
            held(4, SEQ_ROWS, 128),
            held(2, SEQ_ROWS, 128),
            held(2, SEQ_ROWS, 128),
            held(4, SEQ_ROWS, SEQ_ROWS),
            held(SEQ_ROWS, 384),
            held(SEQ_ROWS, 1024, kind=KEEP),
            held(SEQ_ROWS, 1024, kind=KEEP),
            held(SEQ_ROWS, 1024),
            held(2, SEQ_ROWS, MODEL),
            held(MODEL, SEQ_ROWS),
            held(SEQ_ROWS, 2048),
            held(4, SEQ_ROWS, 128),
            held(2, 128, SEQ_ROWS, kind=float32),
            held(2, 128, SEQ_ROWS, kind=float32),
            held(SEQ_ROWS, 768),
            held(2, OWN, MODEL, kind=float32),
            held(SEQ_ROWS, MODEL),
            held(2, OWN, MODEL),
            held(2, OWN, MODEL),
            held(2, OWN, MODEL),
            held(2, 2, SIDE, SIDE, 48, 256),
            held(SETS, 2, SIDE, 48, JOB_WIDTH),
            held(SETS, 2, SIDE, 48, JOB_WIDTH),
            held(SETS, 2, SIDE, 48, JOB_WIDTH),
            held(SETS, 2, 48, JOB_WIDTH),
            held(SETS, 2, 48, JOB_WIDTH),
            held(SETS, 2, 48, JOB_WIDTH),
            held(SETS, 2, SIDE, 48, JOB_WIDTH),
            held(SETS, 2, SIDE, 48, JOB_WIDTH),
            held(8, 48, JOB_WIDTH),
            held(8, 48, JOB_WIDTH),
            held(9, 8, MODEL, kind=float32),
            pltpu.SemaphoreType.DMA((wires,)),
            pltpu.SemaphoreType.DMA((wires,)),
            pltpu.SemaphoreType.DMA((28 + 40 + 48,)),
            pltpu.SemaphoreType.REGULAR((4,)),
        ],
        compiler_params=pltpu.CompilerParams(
            collective_id=1, has_side_effects=True, vmem_limit_bytes=62 * 2**20
        ),
        name="backward",
    )(gains, grad_out, tokens, cosine, sine, x_second, h, *kept)


def pack_rows(arrays):
    query, key, value, out, gate, up, down = arrays
    turned_out = jnp.swapaxes(out, 1, 2)
    turned_down = jnp.swapaxes(down, 1, 2)
    return jnp.concatenate([query, key, value, turned_out, gate, up, turned_down], axis=2)


def body(
    tokens,
    query_weight,
    key_weight,
    value_weight,
    out_weight,
    gate_weight,
    up_weight,
    down_weight,
    norm_gains,
    grad_out,
):
    packed = pack_rows(
        (query_weight, key_weight, value_weight, out_weight, gate_weight, up_weight, down_weight)
    )
    dp = lax.axis_index("dp")
    gains_placed = lax.dynamic_update_slice(
        jnp.zeros((8, MODEL), jnp.float32),
        norm_gains.reshape(4, -1).astype(jnp.float32),
        (0, dp * 48),
    )
    cosine, sine = rope_tables(4)
    w_kept, gains, output, *kept, x_second, h = run_forward(
        packed, gains_placed, tokens, cosine, sine
    )
    input_grad, summed, gains_grad, _ = run_backward(
        gains, grad_out, tokens, cosine, sine, x_second, h, (w_kept, *kept)
    )
    gains_own = lax.dynamic_slice(gains_grad, (0, dp * 48), (4, 48)).reshape(2, 2, 48)
    pieces, start = [], 0
    for width in COLS:
        pieces.append(summed[:, :, start : start + width])
        start += width
    query, key, value, out, gate, up, down = pieces
    return (
        output,
        input_grad,
        query,
        key,
        value,
        jnp.swapaxes(out, 1, 2),
        gate,
        up,
        jnp.swapaxes(down, 1, 2),
        gains_own,
    )


def solution(mesh):
    return jax.shard_map(
        body,
        mesh=mesh,
        in_specs=(
            P(("dp", "tensor"), None),
            P(None, "dp", "tensor"),
            P(None, "dp", "tensor"),
            P(None, "dp", "tensor"),
            P(None, "tensor", "dp"),
            P(None, "dp", "tensor"),
            P(None, "dp", "tensor"),
            P(None, "tensor", "dp"),
            P(None, None, "dp"),
            P(("dp", "tensor"), None),
        ),
        out_specs=(
            P(("dp", "tensor"), None),
            P(("dp", "tensor"), None),
            P(None, "dp", "tensor"),
            P(None, "dp", "tensor"),
            P(None, "dp", "tensor"),
            P(None, "tensor", "dp"),
            P(None, "dp", "tensor"),
            P(None, "dp", "tensor"),
            P(None, "tensor", "dp"),
            P(None, None, "dp"),
        ),
        check_vma=False,
    )
```

```python
import math

import jax
import jax.numpy as jnp
from jax import lax
from jax.experimental import pallas as pl
from jax.experimental.pallas import tpu as pltpu
from jax.sharding import PartitionSpec as P

HD = 96
MESH_IDS = pl.DeviceIdType.MESH
SIDE = 4
MODEL = 1536
SEQ_ROWS = 512
OWN = 128
QKV = (0, 768)
OUT = (768, 1152)
GATE = (1152, 2176)
UP = (2176, 3200)
DOWN = (3200, 4224)
COLS = (384, 192, 192, 384, 1024, 1024, 1024)
WIDTH = 4224
ATTN_PARTS = (((0, 256), (256, 512)), ((512, 768), (768, 1152)))
GU_PARTS = (((1152, 1664), (1664, 2176)), ((2176, 2688), (2688, 3200)))
DOWN_PARTS = (((3200, 3456), (3456, 3712)), ((3712, 3968), (3968, 4224)))

norm_eps = 1e-05
rope_base = 100000.0
SCALING = 1.0 / math.sqrt(HD)


def cut(cols):
    return pl.ds(cols[0], cols[1] - cols[0])


def shift(place, step):
    return lax.rem(place + step + 2 * SIDE, SIDE)


class Place:
    def __init__(self):
        dp = lax.axis_index("dp")
        tensor = lax.axis_index("tensor")
        self.z_hi, self.x, self.y = dp // 16, (dp // 4) % 4, dp % 4
        self.z_lo, self.core = tensor // 2, tensor % 2
        self.dp, self.tensor = dp, tensor

    def device(self, z_hi, x, y, tensor):
        return (z_hi * 16 + x * 4 + y, tensor)

    def beside(self, axis, step):
        if axis == "x":
            return self.device(self.z_hi, shift(self.x, step), self.y, self.tensor)
        return self.device(self.z_hi, self.x, shift(self.y, step), self.tensor)

    def across(self):
        return self.device(1 - self.z_hi, self.x, self.y, self.tensor)

    def twin(self):
        return (self.dp, self.z_lo * 2 + 1 - self.core)

    def above(self):
        return (self.dp, (1 - self.z_lo) * 2 + self.core)

    def greet(self):
        targets = [self.beside(axis, step) for axis in ("x", "y") for step in (1, 2, 3)]
        targets += [self.across(), self.twin(), self.above()]
        barrier = pltpu.get_barrier_semaphore()
        for target in targets:
            pl.semaphore_signal(barrier, inc=1, device_id=target, device_id_type=MESH_IDS)
        pl.semaphore_wait(barrier, len(targets))


class Wire:
    def __init__(self, send_sems, recv_sems):
        self.send_sems, self.recv_sems = send_sems, recv_sems
        self.count = 0
        self.sent = []

    def slot(self):
        self.count += 1
        return self.count - 1

    def send(self, slot, source, target_ref, target):
        copy = pltpu.make_async_remote_copy(
            src_ref=source,
            dst_ref=target_ref,
            send_sem=self.send_sems.at[slot],
            recv_sem=self.recv_sems.at[slot],
            device_id=target,
            device_id_type=MESH_IDS,
        )
        copy.start()
        self.sent.append(copy)
        return copy

    def arrive(self, slot, landed, target):
        pltpu.make_async_remote_copy(
            src_ref=landed,
            dst_ref=landed,
            send_sem=self.send_sems.at[slot],
            recv_sem=self.recv_sems.at[slot],
            device_id=target,
            device_id_type=MESH_IDS,
        ).wait_recv()

    def release(self, copy):
        copy.wait_send()
        self.sent = [other for other in self.sent if other is not copy]

    def drain(self):
        for copy in self.sent:
            copy.wait_send()
        self.sent = []


class Local:
    def __init__(self, sems):
        self.sems, self.count, self.open = sems, 0, []

    def start(self, source, target):
        copy = pltpu.make_async_copy(source, target, self.sems.at[self.count])
        self.count += 1
        copy.start()
        self.open.append(copy)
        return copy

    def wait(self, copy):
        copy.wait()
        self.open = [other for other in self.open if other is not copy]

    def drain(self):
        for copy in self.open:
            copy.wait()
        self.open = []


def sum_small(wire, at, value_ref, landing, whole_group):
    rounds = []
    if whole_group:
        rounds += [[at.twin()], [at.above()]]
    rounds += [[at.across()]]
    rounds += [[at.beside(axis, step) for step in (1, 2, 3)] for axis in ("y", "x")]
    place = 0
    for targets in rounds:
        slots = [wire.slot() for _ in targets]
        copies = []
        for index, target in enumerate(targets):
            copies.append(wire.send(slots[index], value_ref, landing.at[place + index], target))
        yield
        total = value_ref[...]
        for index, target in enumerate(targets):
            wire.arrive(slots[index], landing.at[place + index], target)
            total = total + landing[place + index]
        for copy in copies:
            wire.release(copy)
        value_ref[...] = total
        place += len(targets)
    yield


PIECES = 2
PIECE = OWN // PIECES


class Spread:
    def __init__(self, wire, at, rows_ref):
        self.wire, self.at, self.rows_ref = wire, at, rows_ref
        self.near = [wire.slot() for _ in range(PIECES)]
        self.over = [wire.slot() for _ in range(PIECES)]
        self.passed = [wire.slot() for _ in range(PIECES)]
        self.copies = []

    def rows(self, tensor, piece):
        start = pl.multiple_of(tensor * OWN + piece * PIECE, PIECE)
        return self.rows_ref.at[pl.ds(start, PIECE)]

    def send(self, piece):
        at, wire = self.at, self.wire
        block = self.rows(at.tensor, piece)
        self.copies.append(wire.send(self.over[piece], block, block, at.above()))
        self.copies.append(wire.send(self.near[piece], block, block, at.twin()))

    def near_done(self):
        at = self.at
        for piece in range(PIECES):
            block = self.rows(at.z_lo * 2 + 1 - at.core, piece)
            self.wire.arrive(self.near[piece], block, at.twin())

    def pass_on(self, piece):
        at, wire = self.at, self.wire
        block = self.rows((1 - at.z_lo) * 2 + at.core, piece)
        wire.arrive(self.over[piece], block, at.above())
        self.copies.append(wire.send(self.passed[piece], block, block, at.twin()))

    def far_done(self, piece):
        at = self.at
        block = self.rows((1 - at.z_lo) * 2 + 1 - at.core, piece)
        self.wire.arrive(self.passed[piece], block, at.twin())
        if piece == PIECES - 1:
            for copy in self.copies:
                self.wire.release(copy)


class Collect:
    def __init__(self, wire, at, part, help_ref, near_ref, over_ref):
        self.wire, self.at, self.part = wire, at, part
        self.help_ref, self.near_ref, self.over_ref = help_ref, near_ref, over_ref
        self.help = [wire.slot() for _ in range(PIECES)]
        self.near = wire.slot()
        self.over = [wire.slot() for _ in range(PIECES)]
        self.copies = []

    def rows(self, z_lo, core, piece):
        start = (z_lo * 2 + core) * OWN + piece * PIECE
        return pl.ds(pl.multiple_of(start, PIECE), PIECE)

    def other_ready(self, piece):
        at = self.at
        block = self.part.at[self.rows(1 - at.z_lo, 1 - at.core, piece)]
        landing = self.help_ref.at[pl.ds(piece * PIECE, PIECE)]
        self.copies.append(self.wire.send(self.help[piece], block, landing, at.twin()))

    def own_ready(self):
        at = self.at
        start = pl.multiple_of((at.z_lo * 2 + 1 - at.core) * OWN, OWN)
        block = self.part.at[pl.ds(start, OWN)]
        self.copies.append(self.wire.send(self.near, block, self.near_ref, at.twin()))

    def send_over(self, piece):
        at = self.at
        window = pl.ds(piece * PIECE, PIECE)
        self.wire.arrive(self.help[piece], self.help_ref.at[window], at.twin())
        rows = self.rows(1 - at.z_lo, at.core, piece)
        total = self.part[rows, :].astype(jnp.float32) + self.help_ref[window, :].astype(
            jnp.float32
        )
        self.part[rows, :] = total.astype(jnp.bfloat16)
        self.copies.append(
            self.wire.send(
                self.over[piece], self.part.at[rows], self.over_ref.at[window], at.above()
            )
        )

    def result(self, piece):
        at = self.at
        window = pl.ds(piece * PIECE, PIECE)
        if piece == 0:
            self.wire.arrive(self.near, self.near_ref, at.twin())
        total = self.part[self.rows(at.z_lo, at.core, piece), :].astype(
            jnp.float32
        ) + self.near_ref[window, :].astype(jnp.float32)
        self.wire.arrive(self.over[piece], self.over_ref.at[window], at.above())
        total = total + self.over_ref[window, :].astype(jnp.float32)
        if piece == PIECES - 1:
            for copy in self.copies:
                self.wire.release(copy)
        return total


def here_rows(at):
    return ((at.z_lo * 2 * OWN, 2 * OWN),)


def there_rows(at, piece):
    start = (1 - at.z_lo) * 2 * OWN + piece * PIECE
    return ((start, PIECE), (start + OWN, PIECE))


def windows(rows):
    return [pl.ds(pl.multiple_of(start, size), size) for start, size in rows]


def take(ref, rows, cols=slice(None)):
    pieces = [ref[window, cols] for window in windows(rows)]
    return pieces[0] if len(pieces) == 1 else jnp.concatenate(pieces, axis=0)


def put(ref, rows, cols, value):
    place = 0
    for window, (_, size) in zip(windows(rows), rows):
        ref[window, cols] = value[place : place + size]
        place += size


def nn(left, right):
    return jnp.dot(left, right, preferred_element_type=jnp.float32)


def nt(left, right):
    return lax.dot_general(
        left, right, (((1,), (1,)), ((), ())), preferred_element_type=jnp.float32
    )


def tn(left, right):
    return lax.dot_general(
        left, right, (((0,), (0,)), ((), ())), preferred_element_type=jnp.float32
    )


def rope_tables(heads):
    half = HD // 2
    position = jnp.arange(SEQ_ROWS, dtype=jnp.float32)[:, None]
    exponent = 2.0 * jnp.arange(half, dtype=jnp.float32) / HD
    angles = position * (rope_base ** (-exponent))[None, :]
    cosine, sine = jnp.cos(angles), jnp.sin(angles)
    wide_cosine = jnp.concatenate([cosine, cosine], axis=1)
    wide_sine = jnp.concatenate([-sine, sine], axis=1)
    return jnp.tile(wide_cosine, (1, heads)), jnp.tile(wide_sine, (1, heads))


def swap_halves(values):
    width = values.shape[1]
    lane = lax.broadcasted_iota(jnp.int32, values.shape, 1)
    first = lax.rem(lane, HD) < HD // 2
    return jnp.where(
        first, pltpu.roll(values, width - HD // 2, 1), pltpu.roll(values, HD // 2, 1)
    )


def head_of(values, start):
    width = values.shape[1]
    moved = values if start == 0 else pltpu.roll(values, width - start, 1)
    moved = moved[:, :128]
    lane = lax.broadcasted_iota(jnp.int32, moved.shape, 1)
    return jnp.where(lane < HD, moved, 0.0)


def side_by_side(heads):
    tiles = []
    for tile in range(len(heads) * HD // 128):
        total = None
        lane = lax.broadcasted_iota(jnp.int32, heads[0].shape, 1)
        for index, head in enumerate(heads):
            start = index * HD - tile * 128
            if start <= -HD or start >= 128:
                continue
            moved = pltpu.roll(head, start % 128, 1) if start else head
            if start > 0 or start < 0:
                keep = (lane >= start) if start > 0 else (lane < start + HD)
                moved = jnp.where(keep, moved, 0.0)
            total = moved if total is None else total + moved
        tiles.append(total)
    return jnp.concatenate(tiles, axis=1)


def weight(w_ref, layer, cols):
    value = w_ref[layer, :, :, cols]
    return value.reshape(MODEL, value.shape[-1])


def turn_rows(source, target):
    def tile(index, carry):
        start = pl.multiple_of(index * 256, 256)
        target[pl.ds(start, 256), :] = source[:, pl.ds(start, 256)].T
        return carry

    lax.fori_loop(0, MODEL // 256, tile, 0)


def gather_job(wire, at, full, layer, group):
    parts = []
    for (first, second), (left, right) in zip((("y", "x"), ("x", "y")), group):

        def block(first_step, second_step, cols, first=first):
            x_step, y_step = (
                (first_step, second_step) if first == "x" else (second_step, first_step)
            )
            row = shift(at.x, x_step) * 192 + shift(at.y, y_step) * 48
            return full.at[layer, :, pl.ds(pl.multiple_of(row, 48), 48), cut(cols)]

        parts.append(
            dict(
                first=first,
                second=second,
                left=left,
                right=right,
                whole=(left[0], right[1]),
                block=block,
                one={s: wire.slot() for s in (1, -1)},
                two={s: wire.slot() for s in (1, -1)},
                side={(f, s): wire.slot() for f in (0, -1, 1, 2) for s in (1, -1)},
                far={(f, s): wire.slot() for f in (0, -1, 1, 2) for s in (1, -1)},
            )
        )

    def half(part, step):
        return part["left"] if step == 1 else part["right"]

    def one_start(part, step):
        piece = part["block"](0, 0, part["whole"])
        wire.send(part["one"][step], piece, piece, at.beside(part["first"], step))

    def side_start(part, first_step):
        for step in (1, -1):
            piece = part["block"](first_step, 0, part["whole"])
            wire.send(
                part["side"][first_step, step], piece, piece, at.beside(part["second"], step)
            )

    def one_done(part, step):
        target = at.beside(part["first"], step)
        wire.arrive(part["one"][step], part["block"](-step, 0, part["whole"]), target)
        piece = part["block"](-step, 0, half(part, step))
        wire.send(part["two"][step], piece, piece, target)

    def two_done(part):
        for step in (1, -1):
            piece = part["block"](2, 0, half(part, step))
            wire.arrive(part["two"][step], piece, at.beside(part["first"], step))

    def side_done(part, first_step):
        for step in (1, -1):
            target = at.beside(part["second"], step)
            landed = part["block"](first_step, -step, part["whole"])
            wire.arrive(part["side"][first_step, step], landed, target)
            piece = part["block"](first_step, -step, half(part, step))
            wire.send(part["far"][first_step, step], piece, piece, target)

    def far_done(part, first_step):
        for step in (1, -1):
            piece = part["block"](first_step, 2, half(part, step))
            wire.arrive(part["far"][first_step, step], piece, at.beside(part["second"], step))

    for part in parts:
        for step in (1, -1):
            one_start(part, step)
    for part in parts:
        side_start(part, 0)
    yield
    for step in (1, -1):
        for part in parts:
            one_done(part, step)
    for first_step in (-1, 1):
        for part in parts:
            side_start(part, first_step)
    yield
    for part in parts:
        two_done(part)
    for part in parts:
        side_start(part, 2)
    for part in parts:
        side_done(part, 0)
    yield
    for first_step in (-1, 1):
        for part in parts:
            side_done(part, first_step)
    yield
    for part in parts:
        side_done(part, 2)
    yield
    for first_step in (0, -1, 1, 2):
        for part in parts:
            far_done(part, first_step)
    yield


LAG = 2


class Gather:
    def __init__(self, wire, local, at, shard, full, kept):
        self.wire, self.local, self.at, self.shard = wire, local, at, shard
        self.full, self.kept = full, kept
        self.groups = [
            (layer, group)
            for layer in range(2)
            for group in (ATTN_PARTS, GU_PARTS, DOWN_PARTS)
        ]
        self.jobs = [gather_job(wire, at, full, *pair) for pair in self.groups]
        self.slots = [wire.slot() for _ in self.groups]
        self.own = []
        count = len(self.jobs)
        self.order = [
            (index, turn - LAG * index)
            for turn in range(LAG * count + 6)
            for index in range(count)
            if 0 <= turn - LAG * index < 6
        ]
        self.done = 0

    def columns(self, index):
        group = self.groups[index][1]
        return cut((group[0][0][0], group[1][1][1]))

    def mine(self, z_hi):
        row = self.at.x * 192 + self.at.y * 48
        return (z_hi, pl.ds(pl.multiple_of(row, 48), 48))

    def begin(self):
        at = self.at
        z_own, rows = self.mine(at.z_hi)
        for index, (layer, _) in enumerate(self.groups):
            cols = self.columns(index)
            source = self.shard.at[layer, :, cols]
            target = self.full.at[layer, z_own, rows, cols]
            self.wire.send(self.slots[index], source, target, at.across())
            self.own.append(self.local.start(source, target))

    def step(self, count=1):
        for _ in range(count):
            if self.done == len(self.order):
                return
            index, stage = self.order[self.done]
            self.done += 1
            layer = self.groups[index][0]
            cols = self.columns(index)
            if stage == 0:
                self.local.wait(self.own[index])
                z_other, rows = self.mine(1 - self.at.z_hi)
                landed = self.full.at[layer, z_other, rows, cols]
                self.wire.arrive(self.slots[index], landed, self.at.across())
            next(self.jobs[index])
            if stage == 5:
                self.local.start(
                    self.full.at[layer, :, :, cols], self.kept.at[layer, :, :, cols]
                )

    def until(self, index):
        while (index, 5) in self.order[self.done :]:
            self.step()


def normed(rows_in, gain):
    inverse = lax.rsqrt(jnp.mean(rows_in * rows_in, axis=-1, keepdims=True) + norm_eps)
    return (rows_in * inverse * gain).astype(jnp.bfloat16)


def project_heads(layer, rows, n1, w, cosine, sine, q_ref, k_ref, v_ref):
    left = take(n1.at[layer], rows)
    cosine_rows, sine_rows = take(cosine, rows), take(sine, rows)
    every = slice(None)
    query = nn(left, weight(w, layer, pl.ds(0, 384)))
    turned = query * cosine_rows + swap_halves(query) * sine_rows
    for head in range(4):
        put(q_ref.at[layer, head], rows, every, head_of(turned, head * HD).astype(jnp.bfloat16))
    both = nn(left, weight(w, layer, pl.ds(384, 384)))
    turned = both * cosine_rows + swap_halves(both) * sine_rows
    for head in range(2):
        put(k_ref.at[layer, head], rows, every, head_of(turned, head * HD).astype(jnp.bfloat16))
        value = head_of(both, 192 + head * HD).astype(jnp.bfloat16)
        put(v_ref.at[layer, head], rows, every, value)


def attend(layer, blocks, q_ref, k_ref, v_ref, p_ref, o_ref):
    for block in blocks:
        rows = pl.ds(block * 128, 128)
        keys = (block + 1) * 128
        outputs = []
        for head in range(2):
            pair = jnp.concatenate(
                [q_ref[layer, 2 * head, rows, :], q_ref[layer, 2 * head + 1, rows, :]], axis=0
            )
            scores = nt(pair, k_ref[layer, head, pl.ds(0, keys), :]) * SCALING
            row = lax.broadcasted_iota(jnp.int32, (256, keys), 0) % 128 + block * 128
            key = lax.broadcasted_iota(jnp.int32, (256, keys), 1)
            scores = jnp.where(row >= key, scores, -1e30)
            peak = jnp.max(scores, axis=-1, keepdims=True)
            exponent = jnp.exp(scores - peak)
            inverse = 1.0 / jnp.sum(exponent, axis=-1, keepdims=True)
            shares = (exponent * inverse).astype(jnp.bfloat16)
            p_ref[layer, 2 * head, rows, pl.ds(0, keys)] = shares[:128]
            p_ref[layer, 2 * head + 1, rows, pl.ds(0, keys)] = shares[128:]
            out = nn(shares, v_ref[layer, head, pl.ds(0, keys), :])
            outputs += [out[:128], out[128:]]
        o_ref[layer, rows, :] = side_by_side(outputs).astype(jnp.bfloat16)


def rows_partial(layer, rows, left_ref, w, cols, part):
    left = take(left_ref, rows)
    for half in range(2):

        def tile(index, carry, half=half):
            start = pl.multiple_of(index * 256, 256)
            right = w[layer, half, pl.ds(start, 256), cut(cols)]
            column = pl.ds(pl.multiple_of(half * 768 + start, 256), 256)
            put(part, rows, column, nt(left, right).astype(jnp.bfloat16))
            return carry

        lax.fori_loop(0, 3, tile, 0)


def hidden_rows(layer, rows, n2, w, g_ref, u_ref, a_ref):
    left = take(n2.at[layer], rows)

    def tile(index, carry):
        start = pl.multiple_of(index * 256, 256)
        column = pl.ds(start, 256)
        gate = nn(left, weight(w, layer, pl.ds(GATE[0] + start, 256)))
        up = nn(left, weight(w, layer, pl.ds(UP[0] + start, 256)))
        hidden = gate * up / (1.0 + jnp.exp(-gate))
        put(g_ref.at[layer], rows, column, gate.astype(g_ref.dtype))
        put(u_ref.at[layer], rows, column, up.astype(u_ref.dtype))
        put(a_ref.at[layer], rows, column, hidden.astype(jnp.bfloat16))
        return carry

    lax.fori_loop(0, 4, tile, 0)


def forward_kernel(
    shard,
    gains_placed,
    tokens,
    grad_out,
    cosine,
    sine,
    w_kept,
    gains,
    dm_kept,
    dm_turned_kept,
    n1_kept,
    n2_kept,
    q_kept,
    k_kept,
    v_kept,
    p_kept,
    o_kept,
    g_kept,
    u_kept,
    a_kept,
    x_kept,
    h_kept,
    w,
    n1,
    n2,
    q_ref,
    k_ref,
    v_ref,
    p_ref,
    o_ref,
    g_ref,
    u_ref,
    a_ref,
    x_ref,
    h_ref,
    dm,
    n1_turned,
    n2_turned,
    part,
    help_ref,
    near_ref,
    over_ref,
    gains_landing,
    send_sems,
    recv_sems,
    local_sems,
):
    at = Place()
    at.greet()
    wire = Wire(send_sems, recv_sems)
    local = Local(local_sems)
    gather = Gather(wire, local, at, shard, w, w_kept)
    gather.begin()
    gather.step()
    gains[...] = gains_placed[...]
    rounds = sum_small(wire, at, gains, gains_landing, False)
    for _ in rounds:
        gather.step()
    turn = 0

    def collector():
        nonlocal turn
        turn += 1
        slot = turn % 2
        return Collect(
            wire, at, part, help_ref.at[slot], near_ref.at[slot], over_ref.at[slot]
        )

    def own(piece):
        return pl.ds(pl.multiple_of(at.tensor * OWN + piece * PIECE, PIECE), PIECE)

    def window(piece):
        return pl.ds(piece * PIECE, PIECE)

    here = here_rows(at)
    turning = [None, None]
    spread = Spread(wire, at, n1.at[0])
    for piece in range(PIECES):
        x_rows = tokens[window(piece), :].astype(jnp.float32)
        x_ref[0, window(piece), :] = x_rows
        n1[0, own(piece), :] = normed(x_rows, gains[pl.ds(0, 1), :])
        spread.send(piece)
    for layer in range(2):
        heads = (n1, w, cosine, sine, q_ref, k_ref, v_ref)
        spread.near_done()
        gather.until(3 * layer)
        project_heads(layer, here, *heads)
        spread.pass_on(0)
        gather.step()
        spread.far_done(0)
        project_heads(layer, there_rows(at, 0), *heads)
        spread.pass_on(1)
        spread.far_done(1)
        project_heads(layer, there_rows(at, 1), *heads)
        for source, target in ((q_ref, q_kept), (k_ref, k_kept), (v_ref, v_kept)):
            local.start(source.at[layer], target.at[layer])
        collect = collector()
        around = (q_ref, k_ref, v_ref, p_ref, o_ref)

        def blocks(first, second, layer=layer, around=around):
            @pl.when(at.z_lo == 0)
            def _():
                attend(layer, first, *around)

            @pl.when(at.z_lo == 1)
            def _():
                attend(layer, second, *around)

        blocks((2, 3), (0, 1))
        for piece in range(PIECES):
            rows_partial(layer, there_rows(at, piece), o_ref.at[layer], w, OUT, part)
            collect.other_ready(piece)
        gather.step()
        collect.send_over(0)
        collect.send_over(1)
        blocks((0, 1), (2, 3))
        rows_partial(layer, here, o_ref.at[layer], w, OUT, part)
        collect.own_ready()
        for source, target in ((p_ref, p_kept), (o_ref, o_kept)):
            local.start(source.at[layer], target.at[layer])
        gather.step()
        spread = Spread(wire, at, n2.at[layer])
        for piece in range(PIECES):
            h_rows = x_ref[layer, window(piece), :] + collect.result(piece)
            h_ref[layer, window(piece), :] = h_rows
            n2[layer, own(piece), :] = normed(h_rows, gains[pl.ds(2 * layer + 1, 1), :])
            spread.send(piece)
        if layer == 1:
            spread_back = Spread(wire, at, dm)
            for piece in range(PIECES):
                dm[own(piece), :] = grad_out[window(piece), :]
                spread_back.send(piece)
        if layer == 1:
            local.wait(turning[0])
        turn_rows(n1.at[layer], n1_turned)
        turning[0] = local.start(n1_turned, n1_kept.at[layer])
        spread.near_done()
        gather.until(3 * layer + 1)
        mlp = (n2, w, g_ref, u_ref, a_ref)
        hidden_rows(layer, here, *mlp)
        if layer == 1:
            spread.pass_on(0)
            spread_back.pass_on(0)
            spread.far_done(0)
            hidden_rows(layer, there_rows(at, 0), *mlp)
            spread.pass_on(1)
            spread_back.pass_on(1)
            spread.far_done(1)
            hidden_rows(layer, there_rows(at, 1), *mlp)
            spread_back.near_done()
            spread_back.far_done(0)
            spread_back.far_done(1)
        else:
            collect = collector()
            spread.pass_on(0)
            gather.until(2)
            rows_partial(layer, here, a_ref.at[layer], w, DOWN, part)
            collect.own_ready()
            gather.step()
            for piece in range(PIECES):
                spread.far_done(piece)
                hidden_rows(layer, there_rows(at, piece), *mlp)
                rows_partial(layer, there_rows(at, piece), a_ref.at[layer], w, DOWN, part)
                collect.other_ready(piece)
                if piece + 1 < PIECES:
                    spread.pass_on(piece + 1)
                collect.send_over(piece)
        for source, target in (
            (h_ref, h_kept),
            (g_ref, g_kept),
            (u_ref, u_kept),
            (a_ref, a_kept),
        ):
            local.start(source.at[layer], target.at[layer])
        if layer == 1:
            local.wait(turning[1])
        turn_rows(n2.at[layer], n2_turned)
        turning[1] = local.start(n2_turned, n2_kept.at[layer])
        gather.step()
        if layer == 1:
            local.start(dm, dm_kept)
            local.wait(turning[0])
            turn_rows(dm, n1_turned)
            local.start(n1_turned, dm_turned_kept)
            break
        spread = Spread(wire, at, n1.at[1])
        for piece in range(PIECES):
            total = h_ref[layer, window(piece), :] + collect.result(piece)
            x_ref[1, window(piece), :] = total
            n1[1, own(piece), :] = normed(total, gains[pl.ds(2, 1), :])
            spread.send(piece)
        local.start(x_ref.at[1], x_kept)
    gather.until(5)
    local.drain()
    wire.drain()


KEEP = jnp.bfloat16


def run_forward(shard, gains_placed, tokens, grad_out, cosine, sine):
    def kept(*shape, kind=jnp.bfloat16):
        return jax.ShapeDtypeStruct(shape, kind)

    def held(*shape, kind=jnp.bfloat16):
        return pltpu.VMEM(shape, kind)

    vmem = pl.BlockSpec(memory_space=pltpu.VMEM)
    hbm = pl.BlockSpec(memory_space=pl.ANY)
    float32 = jnp.float32
    wires = 6 * 41 + 7 + 5 * 6 + 3 * 5
    return pl.pallas_call(
        forward_kernel,
        out_shape=(
            kept(2, 2, 768, WIDTH),
            kept(8, MODEL, kind=float32),
            kept(SEQ_ROWS, MODEL),
            kept(MODEL, SEQ_ROWS),
            kept(2, MODEL, SEQ_ROWS),
            kept(2, MODEL, SEQ_ROWS),
            kept(2, 4, SEQ_ROWS, 128),
            kept(2, 2, SEQ_ROWS, 128),
            kept(2, 2, SEQ_ROWS, 128),
            kept(2, 4, SEQ_ROWS, SEQ_ROWS),
            kept(2, SEQ_ROWS, 384),
            kept(2, SEQ_ROWS, 1024, kind=KEEP),
            kept(2, SEQ_ROWS, 1024, kind=KEEP),
            kept(2, SEQ_ROWS, 1024),
            kept(OWN, MODEL, kind=float32),
            kept(2, OWN, MODEL, kind=float32),
        ),
        in_specs=[vmem] * 6,
        out_specs=(hbm, vmem) + (hbm,) * 14,
        scratch_shapes=[
            held(2, 2, 768, WIDTH),
            held(2, SEQ_ROWS, MODEL),
            held(2, SEQ_ROWS, MODEL),
            held(2, 4, SEQ_ROWS, 128),
            held(2, 2, SEQ_ROWS, 128),
            held(2, 2, SEQ_ROWS, 128),
            held(2, 4, SEQ_ROWS, SEQ_ROWS),
            held(2, SEQ_ROWS, 384),
            held(2, SEQ_ROWS, 1024, kind=KEEP),
            held(2, SEQ_ROWS, 1024, kind=KEEP),
            held(2, SEQ_ROWS, 1024),
            held(2, OWN, MODEL, kind=float32),
            held(2, OWN, MODEL, kind=float32),
            held(SEQ_ROWS, MODEL),
            held(MODEL, SEQ_ROWS),
            held(MODEL, SEQ_ROWS),
            held(SEQ_ROWS, MODEL),
            held(2, OWN, MODEL),
            held(2, OWN, MODEL),
            held(2, OWN, MODEL),
            held(7, 8, MODEL, kind=float32),
            pltpu.SemaphoreType.DMA((wires,)),
            pltpu.SemaphoreType.DMA((wires,)),
            pltpu.SemaphoreType.DMA((48,)),
        ],
        compiler_params=pltpu.CompilerParams(
            collective_id=0, has_side_effects=True, vmem_limit_bytes=62 * 2**20
        ),
        name="forward",
    )(shard, gains_placed, tokens, grad_out, cosine, sine)


JOBS = (
    (((3200, 3456), (3456, 3712)), ((3712, 3968), (3968, 4224))),
    (((1152, 1408), (1408, 1664)), ((1664, 1920), (1920, 2176))),
    (((2176, 2432), (2432, 2688)), ((2688, 2944), (2944, 3200))),
    (((0, 256), (256, 512)), ((512, 768), (768, 1152))),
)
JOB_WIDTH = 1152
SETS = 3
LAG_BACK = 2


def add_rows(target, terms):
    lead = target.shape[:-2]

    def step(index, carry):
        window = ()
        if lead:
            window = (index // lead[1], index % lead[1])
        total = None
        for term in terms:
            value = term[window + (slice(None), slice(None))].astype(jnp.float32)
            total = value if total is None else total + value
        target[window + (slice(None), slice(None))] = total.astype(target.dtype)
        return carry

    lax.fori_loop(0, math.prod(lead), step, 0)


def scatter_job(wire, local, at, grads, layer, group, bufs, finish):
    one, two_up, two_down, small_one, small_up, small_down, near_side, near_own = bufs
    base = group[0][0][0]
    parts = []
    for (first, second), (left, right) in zip((("y", "x"), ("x", "y")), group):

        def region(step, cols, second=second):
            if second == "x":
                return grads.at[layer, :, shift(at.x, step), :, :, cut(cols)]
            return grads.at[layer, :, :, shift(at.y, step), :, cut(cols)]

        def mine(step, cols, first=first):
            place = at.y if first == "y" else at.x
            return two_up.at[:, shift(place, step), :, inside(cols)]

        parts.append(
            dict(
                first=first,
                second=second,
                left=left,
                right=right,
                whole=(left[0], right[1]),
                region=region,
                mine=mine,
                **{
                    name: {s: wire.slot() for s in (1, -1)}
                    for name in ("far", "raw", "sum", "far2", "raw2", "sum2")
                },
            )
        )

    def inside(cols):
        return pl.ds(cols[0] - base, cols[1] - cols[0])

    def half(part, step):
        return part["left"] if step == 1 else part["right"]

    def other(part, step):
        return part["right"] if step == 1 else part["left"]

    def big(ref, cols):
        return ref.at[:, :, :, inside(cols)]

    def small(ref, cols):
        return ref.at[:, :, inside(cols)]

    copies = []
    near = {}
    for part in parts:
        for step in (1, -1):
            cols = half(part, step)
            target = at.beside(part["second"], step)
            copies.append(
                wire.send(part["far"][step], part["region"](2, cols), big(one, cols), target)
            )
    for number, part in enumerate(parts):
        for step in (1, -1):
            cols = other(part, step)
            landing = two_up if step == 1 else two_down
            target = at.beside(part["second"], step)
            copies.append(
                wire.send(part["raw"][step], part["region"](step, cols), big(landing, cols), target)
            )
            cols = half(part, step)
            near[number, step] = local.start(part["region"](step, cols), big(near_side, cols))
    yield
    for number, part in enumerate(parts):
        cols = part["whole"]
        near[number, 0] = local.start(part["region"](0, cols), big(near_own, cols))
    for step in (1, -1):
        for number, part in enumerate(parts):
            cols = half(part, step)
            target = at.beside(part["second"], step)
            piece = big(one, cols)
            local.wait(near[number, step])
            wire.arrive(part["far"][step], piece, target)
            add_rows(piece, (piece, big(near_side, cols)))
            landing = two_up if step == 1 else two_down
            copies.append(wire.send(part["sum"][step], piece, big(landing, cols), target))
    yield
    for number, part in enumerate(parts):
        local.wait(near[number, 0])
        for step in (1, -1):
            target = at.beside(part["second"], step)
            landing = two_up if step == 1 else two_down
            for name, cols in (("raw", other(part, step)), ("sum", half(part, step))):
                wire.arrive(part[name][step], big(landing, cols), target)
        cols = part["whole"]
        add_rows(big(two_up, cols), (big(near_own, cols), big(two_up, cols), big(two_down, cols)))
        for step in (1, -1):
            target = at.beside(part["first"], step)
            cols = half(part, step)
            copies.append(
                wire.send(part["far2"][step], part["mine"](2, cols), small(small_one, cols), target)
            )
            cols = other(part, step)
            landing = small_up if step == 1 else small_down
            copies.append(
                wire.send(part["raw2"][step], part["mine"](step, cols), small(landing, cols), target)
            )
    yield
    for step in (1, -1):
        for part in parts:
            cols = half(part, step)
            target = at.beside(part["first"], step)
            piece = small(small_one, cols)
            wire.arrive(part["far2"][step], piece, target)
            own = part["mine"](step, cols)
            for z_hi in range(2):
                add_rows(piece.at[z_hi], (piece.at[z_hi], own.at[z_hi]))
            landing = small_up if step == 1 else small_down
            copies.append(wire.send(part["sum2"][step], piece, small(landing, cols), target))
    yield
    for part in parts:
        for step in (1, -1):
            target = at.beside(part["first"], step)
            landing = small_up if step == 1 else small_down
            for name, cols in (("raw2", other(part, step)), ("sum2", half(part, step))):
                wire.arrive(part[name][step], small(landing, cols), target)
        cols = part["whole"]
        finish(
            cols,
            [
                [
                    ref.at[z_hi]
                    for ref in (part["mine"](0, cols), small(small_up, cols), small(small_down, cols))
                ]
                for z_hi in (1 - at.z_hi, at.z_hi)
            ],
        )
    for copy in copies:
        wire.release(copy)
    yield


class Scatter:
    def __init__(self, wire, local, at, grads, summed, sets, leaving, landed, credits):
        self.wire, self.local, self.at, self.grads = wire, local, at, grads
        self.summed, self.leaving, self.landed, self.credits = summed, leaving, landed, credits
        self.groups = [(layer, group) for layer in (1, 0) for group in JOBS]
        self.last = []
        self.jobs = []
        for index, (layer, group) in enumerate(self.groups):
            bufs = tuple(ref.at[index % ref.shape[0]] for ref in sets)
            self.jobs.append(
                scatter_job(
                    wire, local, at, grads, layer, group, bufs, self.finisher(index, layer, group)
                )
            )
        count = len(self.jobs)
        self.order = [
            (index, turn - LAG_BACK * index)
            for turn in range(LAG_BACK * count + 6)
            for index in range(count)
            if 0 <= turn - LAG_BACK * index < 6
        ]
        self.done = 0
        self.ready = 0

    def finisher(self, index, layer, group):
        wire, at = self.wire, self.at
        base = group[0][0][0]

        def finish(cols, terms):
            theirs, own = terms
            window = pl.ds(cols[0] - base, cols[1] - cols[0])
            piece = self.leaving.at[index, :, window]
            add_rows(piece, theirs)
            slot = wire.slot()
            landing = self.landed.at[index, :, window]
            wire.send(slot, piece, landing, at.across())
            target = self.summed.at[layer, :, cut(cols)]
            add_rows(target, own)
            self.last.append((index, slot, landing, target))

        return finish

    def turn(self):
        if self.done < len(self.order):
            index, stage = self.order[self.done]
            now = LAG_BACK * index + stage
            while self.done < len(self.order):
                index, stage = self.order[self.done]
                if LAG_BACK * index + stage != now or index >= self.ready:
                    return
                self.step()

    def step(self, count=1):
        at = self.at
        for _ in range(count):
            if self.done == len(self.order):
                return
            index, stage = self.order[self.done]
            if index >= self.ready:
                return
            self.done += 1
            ways = [(axis, step) for axis in ("x", "y") for step in (1, -1)]
            if stage == 5:
                for job, slot, landing, target in self.last:
                    if job == index:
                        self.wire.arrive(slot, landing, at.across())
                        add_rows(target, (target, landing))
                continue
            if stage == 0 and index >= SETS:
                for number in range(4):
                    pl.semaphore_wait(self.credits.at[number], 1)
            next(self.jobs[index])
            if stage == 4 and index + SETS < len(self.jobs):
                for number, (axis, step) in enumerate(ways):
                    pl.semaphore_signal(
                        self.credits.at[number],
                        inc=1,
                        device_id=at.beside(axis, step),
                        device_id_type=MESH_IDS,
                    )


def norm_backward(rows_in, gain, grad_normed):
    inverse = lax.rsqrt(jnp.mean(rows_in * rows_in, axis=-1, keepdims=True) + norm_eps)
    scaled = rows_in * inverse
    grad_gain = jnp.sum(grad_normed * scaled, axis=0, keepdims=True)
    grad_scaled = grad_normed * gain
    grad_input = inverse * (
        grad_scaled - scaled * jnp.mean(grad_scaled * scaled, axis=-1, keepdims=True)
    )
    return grad_input, grad_gain


def hidden_back(rows, dm, w, g_ref, u_ref, dgu):
    left = take(dm, rows)

    def tile(index, carry):
        start = pl.multiple_of(index * 256, 256)
        column = pl.ds(start, 256)
        grad = nn(left, weight(w, 0, pl.ds(DOWN[0] + start, 256)))
        gate = take(g_ref, rows, column).astype(jnp.float32)
        up = take(u_ref, rows, column).astype(jnp.float32)
        sigma = 1.0 / (1.0 + jnp.exp(-gate))
        grad_gate = grad * up * sigma * (1.0 + gate * (1.0 - sigma))
        put(dgu, rows, column, grad_gate.astype(jnp.bfloat16))
        column = pl.ds(pl.multiple_of(1024 + start, 256), 256)
        put(dgu, rows, column, (grad * gate * sigma).astype(jnp.bfloat16))
        return carry

    lax.fori_loop(0, 4, tile, 0)


def attend_back(q_ref, k_ref, v_ref, p_ref, do_ref, dk_ref, dv_ref, cosine, sine, dqkv):
    dk_ref[...] = jnp.zeros_like(dk_ref)
    dv_ref[...] = jnp.zeros_like(dv_ref)
    for block in range(4):
        rows = pl.ds(block * 128, 128)
        keys = pl.ds(0, (block + 1) * 128)
        queries = []
        for head in range(2):
            both = (2 * head, 2 * head + 1)
            shares = jnp.concatenate([p_ref[h, rows, keys] for h in both], axis=0)
            pair = jnp.concatenate([q_ref[h, rows, :] for h in both], axis=0)
            grad = jnp.concatenate([do_ref[h, rows, :] for h in both], axis=0)
            wide = shares.astype(jnp.float32)
            grad_shares = nt(grad, v_ref[head, keys, :])
            inner = jnp.sum(grad_shares * wide, axis=-1, keepdims=True)
            grad_scores = (wide * (grad_shares - inner)).astype(jnp.bfloat16)
            grad_pair = nn(grad_scores, k_ref[head, keys, :]) * SCALING
            queries += [grad_pair[:128], grad_pair[128:]]
            dk_ref[head, :, keys] += nn(pair.T, grad_scores)
            dv_ref[head, :, keys] += nn(grad.T, shares)
        grad_rows = side_by_side(queries)
        turned = grad_rows * cosine[rows, :] - swap_halves(grad_rows) * sine[rows, :]
        dqkv[rows, pl.ds(0, 384)] = turned.astype(jnp.bfloat16)
    both = side_by_side(
        [dk_ref[0].T * SCALING, dk_ref[1].T * SCALING, dv_ref[0].T, dv_ref[1].T]
    )
    turned = both * cosine[...] - swap_halves(both) * sine[...]
    lane = lax.broadcasted_iota(jnp.int32, both.shape, 1)
    dqkv[:, pl.ds(384, 384)] = jnp.where(lane < 192, turned, both).astype(jnp.bfloat16)


def backward_kernel(
    gains,
    grad_out,
    tokens,
    cosine,
    sine,
    x_second,
    h_ref,
    w_kept,
    dm_kept,
    dm_turned_kept,
    n1_kept,
    n2_kept,
    q_kept,
    k_kept,
    v_kept,
    p_kept,
    o_kept,
    g_kept,
    u_kept,
    a_kept,
    output,
    input_grad,
    summed,
    gains_grad,
    grads,
    w,
    n1_turned,
    n2_turned,
    q_ref,
    k_ref,
    v_ref,
    p_ref,
    o_ref,
    g_ref,
    u_ref,
    a_ref,
    dm,
    turned,
    dgu,
    do_ref,
    dk_ref,
    dv_ref,
    dqkv,
    dx,
    part,
    help_ref,
    near_ref,
    over_ref,
    staged,
    one,
    two_up,
    two_down,
    small_one,
    small_up,
    small_down,
    near_side,
    near_own,
    leaving,
    landed,
    gains_landing,
    send_sems,
    recv_sems,
    local_sems,
    credits,
):
    at = Place()
    at.greet()
    wire = Wire(send_sems, recv_sems)
    local = Local(local_sems)
    sets = (one, two_up, two_down, small_one, small_up, small_down, near_side, near_own)
    scatter = Scatter(wire, local, at, grads, summed, sets, leaving, landed, credits)
    turn = 0

    def collector():
        nonlocal turn
        turn += 1
        slot = turn % 2
        return Collect(
            wire, at, part, help_ref.at[slot], near_ref.at[slot], over_ref.at[slot]
        )

    loads = {}

    def load(layer, names):
        pairs = dict(
            n1=(n1_kept, n1_turned),
            n2=(n2_kept, n2_turned),
            q=(q_kept, q_ref),
            k=(k_kept, k_ref),
            v=(v_kept, v_ref),
            p=(p_kept, p_ref),
            o=(o_kept, o_ref),
            g=(g_kept, g_ref),
            u=(u_kept, u_ref),
            a=(a_kept, a_ref),
            dm=(dm_kept, dm.at[0]),
            turned=(dm_turned_kept, turned),
        )
        columns = dict(down=DOWN, gu=(GATE[0], UP[1]), out=OUT, qkv=QKV)
        for name in names:
            if name in columns:
                cols = cut(columns[name])
                loads[name] = local.start(w_kept.at[layer, :, :, cols], w.at[0, :, :, cols])
            else:
                kept, held = pairs[name]
                source = kept if name in ("dm", "turned") else kept.at[layer]
                loads[name] = local.start(source, held)

    def ready(*names):
        for name in names:
            local.wait(loads.pop(name))

    mlp_names = ("down", "g", "u", "gu", "a", "n2")
    attn_names = ("out", "v", "p", "k", "q", "qkv", "o", "n1")
    load(1, ("a", "down", "turned", "dm", "g", "u", "gu", "n2"))
    load(1, attn_names)
    staging = [None, None]
    tiles = 0
    behind = []

    def keep_tile(layer, left, right_ref, start, size, column):
        nonlocal tiles
        slot = tiles % 2
        tiles += 1
        if staging[slot] is not None:
            local.wait(staging[slot])
        product = nn(left[...], right_ref[:, pl.ds(start, size)])
        staged[slot, :, :, :, :, pl.ds(0, size)] = product.astype(jnp.bfloat16).reshape(
            2, SIDE, SIDE, 48, size
        )
        staging[slot] = local.start(
            staged.at[slot, :, :, :, :, pl.ds(0, size)],
            grads.at[layer, :, :, :, :, pl.ds(column, size)],
        )

    def keep_grads(layer, left, right_ref, start, width, column):
        for tile in range(0, width, 256):
            size = min(256, width - tile)
            behind.append(
                lambda tile=tile, size=size: keep_tile(
                    layer, left, right_ref, start + tile, size, column + tile
                )
            )

    def grads_kept():
        for slot in range(2):
            if staging[slot] is not None:
                local.wait(staging[slot])
                staging[slot] = None
        scatter.ready += 1

    def fill(count):
        for _ in range(min(count, len(behind))):
            behind.pop(0)()

    def own(piece):
        return pl.ds(pl.multiple_of(at.tensor * OWN + piece * PIECE, PIECE), PIECE)

    def window(piece):
        return pl.ds(piece * PIECE, PIECE)

    here = here_rows(at)
    gains_grad[...] = jnp.zeros_like(gains_grad)
    every = ((0, SEQ_ROWS),)
    dx[0] = grad_out[...].astype(jnp.float32)
    mlp = (dm.at[0], w, g_ref, u_ref, dgu)
    gu_columns = (GATE[0], UP[1])
    spread = None
    for layer in (1, 0):
        if layer == 1:
            collect_out = collector()
            ready("a", "down")
            for piece in range(PIECES):
                rows_partial(0, there_rows(at, piece), a_ref, w, DOWN, part)
                collect_out.other_ready(piece)
            ready("turned")
            keep_grads(layer, turned, a_ref, 0, 1024, DOWN[0])
            behind.append(grads_kept)
            fill(3)
            collect_out.send_over(0)
            collect_out.send_over(1)
            rows_partial(0, here, a_ref, w, DOWN, part)
            collect_out.own_ready()
            fill(len(behind))
            scatter.turn()
            ready("dm", "g", "u")
            hidden_back(every, *mlp)
            ready("n2")
            keep_grads(layer, n2_turned, dgu, 0, 1024, GATE[0])
            behind.append(grads_kept)
            keep_grads(layer, n2_turned, dgu, 1024, 1024, UP[0])
            behind.append(grads_kept)
            fill(2)
            for piece in range(PIECES):
                total = h_ref[1, window(piece), :] + collect_out.result(piece)
                output[window(piece), :] = total.astype(jnp.bfloat16)
            scatter.turn()
            ready("gu")
            collect = collector()
            for piece in range(PIECES):
                rows_partial(0, there_rows(at, piece), dgu, w, gu_columns, part)
                collect.other_ready(piece)
            fill(1)
            collect.send_over(0)
            collect.send_over(1)
            rows_partial(0, here, dgu, w, gu_columns, part)
            collect.own_ready()
            scatter.turn()
        else:
            spread.near_done()
            ready("down", "g", "u")
            hidden_back(here, *mlp)
            scatter.turn()
            fill(2)
            spread.pass_on(0)
            fill(1)
            collect = collector()
            for piece in range(PIECES):
                spread.far_done(piece)
                hidden_back(there_rows(at, piece), *mlp)
                if piece == 0:
                    ready("gu")
                rows_partial(0, there_rows(at, piece), dgu, w, gu_columns, part)
                collect.other_ready(piece)
                if piece + 1 < PIECES:
                    spread.pass_on(piece + 1)
                    fill(2)
                    scatter.turn()
                collect.send_over(piece)
            rows_partial(0, here, dgu, w, gu_columns, part)
            collect.own_ready()
            fill(len(behind))
            load(0, attn_names)
            ready("a", "n2")
            turn_rows(dm.at[0], turned)
            scatter.turn()
            keep_grads(layer, turned, a_ref, 0, 1024, DOWN[0])
            behind.append(grads_kept)
            keep_grads(layer, n2_turned, dgu, 0, 1024, GATE[0])
            behind.append(grads_kept)
            keep_grads(layer, n2_turned, dgu, 1024, 1024, UP[0])
            behind.append(grads_kept)
        fill(3)
        spread = Spread(wire, at, dm.at[1])
        gain_rows = None
        for piece in range(PIECES):
            normed_grad, gain_row = norm_backward(
                h_ref[layer, window(piece), :],
                gains[pl.ds(2 * layer + 1, 1), :],
                collect.result(piece),
            )
            gain_rows = gain_row if gain_rows is None else gain_rows + gain_row
            dh = dx[0, window(piece), :] + normed_grad
            dx[1, window(piece), :] = dh
            dm[1, own(piece), :] = dh.astype(jnp.bfloat16)
            spread.send(piece)
            if piece + 1 < PIECES:
                fill(2)
        gains_grad[pl.ds(2 * layer + 1, 1), :] = gain_rows
        scatter.turn()
        ready("out")

        def heads_back(rows):
            grad = nn(take(dm.at[1], rows), weight(w, 0, cut(OUT)))
            for head in range(4):
                put(do_ref.at[head], rows, slice(None), head_of(grad, head * HD).astype(jnp.bfloat16))

        spread.near_done()
        heads_back(here)
        fill(4)
        spread.pass_on(0)
        fill(3)
        spread.far_done(0)
        heads_back(there_rows(at, 0))
        scatter.turn()
        spread.pass_on(1)
        fill(len(behind))
        if layer == 1:
            load(0, mlp_names)
        spread.far_done(1)
        heads_back(there_rows(at, 1))
        ready("v", "p", "k", "q")
        attend_back(
            q_ref, k_ref, v_ref, p_ref, do_ref, dk_ref, dv_ref, cosine, sine, dqkv
        )
        collect = collector()
        ready("qkv")
        for piece in range(PIECES):
            rows_partial(0, there_rows(at, piece), dqkv, w, QKV, part)
            collect.other_ready(piece)
        scatter.turn()
        collect.send_over(0)
        collect.send_over(1)
        rows_partial(0, here, dqkv, w, QKV, part)
        collect.own_ready()
        turn_rows(dm.at[1], turned)
        ready("o", "n1")
        keep_grads(layer, turned, o_ref, 0, 384, OUT[0])
        keep_grads(layer, n1_turned, dqkv, 0, 768, QKV[0])
        behind.append(grads_kept)
        fill(2)
        if layer == 0:
            scatter.turn()
        rows_in = tokens if layer == 0 else x_second
        spread = Spread(wire, at, dm.at[0]) if layer == 1 else None
        gain_rows = None
        for piece in range(PIECES):
            normed_grad, gain_row = norm_backward(
                rows_in[window(piece), :].astype(jnp.float32),
                gains[pl.ds(2 * layer, 1), :],
                collect.result(piece),
            )
            gain_rows = gain_row if gain_rows is None else gain_rows + gain_row
            dx_rows = dx[1, window(piece), :] + normed_grad
            if layer == 1:
                dx[0, window(piece), :] = dx_rows
                dm[0, own(piece), :] = dx_rows.astype(jnp.bfloat16)
                spread.send(piece)
                if piece == 0:
                    fill(1)
                    scatter.turn()
            else:
                input_grad[window(piece), :] = dx_rows
        gains_grad[pl.ds(2 * layer, 1), :] = gain_rows
    fill(len(behind))
    rounds = sum_small(wire, at, gains_grad, gains_landing, True)
    for _ in rounds:
        scatter.turn()
    while scatter.done < len(scatter.order):
        scatter.step()
    local.drain()
    wire.drain()


def run_backward(gains, grad_out, tokens, cosine, sine, x_second, h, kept):
    def held(*shape, kind=jnp.bfloat16):
        return pltpu.VMEM(shape, kind)

    vmem = pl.BlockSpec(memory_space=pltpu.VMEM)
    hbm = pl.BlockSpec(memory_space=pl.ANY)
    float32 = jnp.float32
    wires = 8 * 26 + 9 + 3 * 6 + 5 * 5
    return pl.pallas_call(
        backward_kernel,
        out_shape=(
            jax.ShapeDtypeStruct((OWN, MODEL), jnp.bfloat16),
            jax.ShapeDtypeStruct((OWN, MODEL), float32),
            jax.ShapeDtypeStruct((2, 48, WIDTH), float32),
            jax.ShapeDtypeStruct((8, MODEL), float32),
            jax.ShapeDtypeStruct((2, 2, SIDE, SIDE, 48, WIDTH), jnp.bfloat16),
        ),
        in_specs=[vmem] * 7 + [hbm] * len(kept),
        out_specs=(vmem, vmem, vmem, vmem, hbm),
        scratch_shapes=[
            held(1, 2, 768, WIDTH),
            held(MODEL, SEQ_ROWS),
            held(MODEL, SEQ_ROWS),
            held(4, SEQ_ROWS, 128),
            held(2, SEQ_ROWS, 128),
            held(2, SEQ_ROWS, 128),
            held(4, SEQ_ROWS, SEQ_ROWS),
            held(SEQ_ROWS, 384),
            held(SEQ_ROWS, 1024, kind=KEEP),
            held(SEQ_ROWS, 1024, kind=KEEP),
            held(SEQ_ROWS, 1024),
            held(2, SEQ_ROWS, MODEL),
            held(MODEL, SEQ_ROWS),
            held(SEQ_ROWS, 2048),
            held(4, SEQ_ROWS, 128),
            held(2, 128, SEQ_ROWS, kind=float32),
            held(2, 128, SEQ_ROWS, kind=float32),
            held(SEQ_ROWS, 768),
            held(2, OWN, MODEL, kind=float32),
            held(SEQ_ROWS, MODEL),
            held(2, OWN, MODEL),
            held(2, OWN, MODEL),
            held(2, OWN, MODEL),
            held(2, 2, SIDE, SIDE, 48, 256),
            held(SETS, 2, SIDE, 48, JOB_WIDTH),
            held(SETS, 2, SIDE, 48, JOB_WIDTH),
            held(SETS, 2, SIDE, 48, JOB_WIDTH),
            held(SETS, 2, 48, JOB_WIDTH),
            held(SETS, 2, 48, JOB_WIDTH),
            held(SETS, 2, 48, JOB_WIDTH),
            held(1, 2, SIDE, 48, JOB_WIDTH),
            held(1, 2, SIDE, 48, JOB_WIDTH),
            held(8, 48, JOB_WIDTH),
            held(8, 48, JOB_WIDTH),
            held(9, 8, MODEL, kind=float32),
            pltpu.SemaphoreType.DMA((wires,)),
            pltpu.SemaphoreType.DMA((wires,)),
            pltpu.SemaphoreType.DMA((30 + 40 + 48,)),
            pltpu.SemaphoreType.REGULAR((4,)),
        ],
        compiler_params=pltpu.CompilerParams(
            collective_id=1, has_side_effects=True, vmem_limit_bytes=63 * 2**20
        ),
        name="backward",
    )(gains, grad_out, tokens, cosine, sine, x_second, h, *kept)


def pack_rows(arrays):
    query, key, value, out, gate, up, down = arrays
    turned_out = jnp.swapaxes(out, 1, 2)
    turned_down = jnp.swapaxes(down, 1, 2)
    return jnp.concatenate([query, key, value, turned_out, gate, up, turned_down], axis=2)


def body(
    tokens,
    query_weight,
    key_weight,
    value_weight,
    out_weight,
    gate_weight,
    up_weight,
    down_weight,
    norm_gains,
    grad_out,
):
    packed = pack_rows(
        (query_weight, key_weight, value_weight, out_weight, gate_weight, up_weight, down_weight)
    )
    dp = lax.axis_index("dp")
    gains_placed = lax.dynamic_update_slice(
        jnp.zeros((8, MODEL), jnp.float32),
        norm_gains.reshape(4, -1).astype(jnp.float32),
        (0, dp * 48),
    )
    cosine, sine = rope_tables(4)
    w_kept, gains, *kept, x_second, h = run_forward(
        packed, gains_placed, tokens, grad_out, cosine, sine
    )
    output, input_grad, summed, gains_grad, _ = run_backward(
        gains, grad_out, tokens, cosine, sine, x_second, h, (w_kept, *kept)
    )
    gains_own = lax.dynamic_slice(gains_grad, (0, dp * 48), (4, 48)).reshape(2, 2, 48)
    pieces, start = [], 0
    for width in COLS:
        pieces.append(summed[:, :, start : start + width])
        start += width
    query, key, value, out, gate, up, down = pieces
    return (
        output,
        input_grad,
        query,
        key,
        value,
        jnp.swapaxes(out, 1, 2),
        gate,
        up,
        jnp.swapaxes(down, 1, 2),
        gains_own,
    )


def solution(mesh):
    return jax.shard_map(
        body,
        mesh=mesh,
        in_specs=(
            P(("dp", "tensor"), None),
            P(None, "dp", "tensor"),
            P(None, "dp", "tensor"),
            P(None, "dp", "tensor"),
            P(None, "tensor", "dp"),
            P(None, "dp", "tensor"),
            P(None, "dp", "tensor"),
            P(None, "tensor", "dp"),
            P(None, None, "dp"),
            P(("dp", "tensor"), None),
        ),
        out_specs=(
            P(("dp", "tensor"), None),
            P(("dp", "tensor"), None),
            P(None, "dp", "tensor"),
            P(None, "dp", "tensor"),
            P(None, "dp", "tensor"),
            P(None, "tensor", "dp"),
            P(None, "dp", "tensor"),
            P(None, "dp", "tensor"),
            P(None, "tensor", "dp"),
            P(None, None, "dp"),
        ),
        check_vma=False,
    )
```

```python
import math

import jax
import jax.numpy as jnp
from jax import lax
from jax.experimental import pallas as pl
from jax.experimental.pallas import tpu as pltpu
from jax.sharding import PartitionSpec as P

HD = 96
MESH_IDS = pl.DeviceIdType.MESH
SIDE = 4
MODEL = 1536
SEQ_ROWS = 512
OWN = 128
QKV = (0, 768)
OUT = (768, 1152)
GATE = (1152, 2176)
UP = (2176, 3200)
DOWN = (3200, 4224)
COLS = (384, 192, 192, 384, 1024, 1024, 1024)
WIDTH = 4224
ATTN_PARTS = (((0, 256), (256, 512)), ((512, 768), (768, 1152)))
GU_PARTS = (((1152, 1664), (1664, 2176)), ((2176, 2688), (2688, 3200)))
DOWN_PARTS = (((3200, 3456), (3456, 3712)), ((3712, 3968), (3968, 4224)))

norm_eps = 1e-05
rope_base = 100000.0
SCALING = 1.0 / math.sqrt(HD)


def cut(cols):
    return pl.ds(cols[0], cols[1] - cols[0])


def shift(place, step):
    return lax.rem(place + step + 2 * SIDE, SIDE)


class Place:
    def __init__(self):
        dp = lax.axis_index("dp")
        tensor = lax.axis_index("tensor")
        self.z_hi, self.x, self.y = dp // 16, (dp // 4) % 4, dp % 4
        self.z_lo, self.core = tensor // 2, tensor % 2
        self.dp, self.tensor = dp, tensor

    def device(self, z_hi, x, y, tensor):
        return (z_hi * 16 + x * 4 + y, tensor)

    def beside(self, axis, step):
        if axis == "x":
            return self.device(self.z_hi, shift(self.x, step), self.y, self.tensor)
        return self.device(self.z_hi, self.x, shift(self.y, step), self.tensor)

    def across(self):
        return self.device(1 - self.z_hi, self.x, self.y, self.tensor)

    def twin(self):
        return (self.dp, self.z_lo * 2 + 1 - self.core)

    def above(self):
        return (self.dp, (1 - self.z_lo) * 2 + self.core)

    def greet(self):
        targets = [self.beside(axis, step) for axis in ("x", "y") for step in (1, 2, 3)]
        targets += [self.across(), self.twin(), self.above()]
        barrier = pltpu.get_barrier_semaphore()
        for target in targets:
            pl.semaphore_signal(barrier, inc=1, device_id=target, device_id_type=MESH_IDS)
        pl.semaphore_wait(barrier, len(targets))


class Wire:
    def __init__(self, send_sems, recv_sems):
        self.send_sems, self.recv_sems = send_sems, recv_sems
        self.count = 0
        self.sent = []

    def slot(self):
        self.count += 1
        return self.count - 1

    def send(self, slot, source, target_ref, target):
        copy = pltpu.make_async_remote_copy(
            src_ref=source,
            dst_ref=target_ref,
            send_sem=self.send_sems.at[slot],
            recv_sem=self.recv_sems.at[slot],
            device_id=target,
            device_id_type=MESH_IDS,
        )
        copy.start()
        self.sent.append(copy)
        return copy

    def arrive(self, slot, landed, target):
        pltpu.make_async_remote_copy(
            src_ref=landed,
            dst_ref=landed,
            send_sem=self.send_sems.at[slot],
            recv_sem=self.recv_sems.at[slot],
            device_id=target,
            device_id_type=MESH_IDS,
        ).wait_recv()

    def release(self, copy):
        copy.wait_send()
        self.sent = [other for other in self.sent if other is not copy]

    def drain(self):
        for copy in self.sent:
            copy.wait_send()
        self.sent = []


class Local:
    def __init__(self, sems):
        self.sems, self.count, self.open = sems, 0, []

    def start(self, source, target):
        copy = pltpu.make_async_copy(source, target, self.sems.at[self.count])
        self.count += 1
        copy.start()
        self.open.append(copy)
        return copy

    def wait(self, copy):
        copy.wait()
        self.open = [other for other in self.open if other is not copy]

    def drain(self):
        for copy in self.open:
            copy.wait()
        self.open = []


def sum_small(wire, at, value_ref, landing, whole_group):
    rounds = []
    if whole_group:
        rounds += [[at.twin()], [at.above()]]
    rounds += [[at.across()]]
    rounds += [[at.beside(axis, step) for step in (1, 2, 3)] for axis in ("y", "x")]
    place = 0
    for targets in rounds:
        slots = [wire.slot() for _ in targets]
        copies = []
        for index, target in enumerate(targets):
            copies.append(wire.send(slots[index], value_ref, landing.at[place + index], target))
        yield
        total = value_ref[...]
        for index, target in enumerate(targets):
            wire.arrive(slots[index], landing.at[place + index], target)
            total = total + landing[place + index]
        for copy in copies:
            wire.release(copy)
        value_ref[...] = total
        place += len(targets)
    yield


PIECES = 2
PIECE = OWN // PIECES


class Spread:
    def __init__(self, wire, at, rows_ref):
        self.wire, self.at, self.rows_ref = wire, at, rows_ref
        self.near = [wire.slot() for _ in range(PIECES)]
        self.over = [wire.slot() for _ in range(PIECES)]
        self.passed = [wire.slot() for _ in range(PIECES)]
        self.copies = []

    def rows(self, tensor, piece):
        start = pl.multiple_of(tensor * OWN + piece * PIECE, PIECE)
        return self.rows_ref.at[pl.ds(start, PIECE)]

    def send(self, piece):
        at, wire = self.at, self.wire
        block = self.rows(at.tensor, piece)
        self.copies.append(wire.send(self.over[piece], block, block, at.above()))
        self.copies.append(wire.send(self.near[piece], block, block, at.twin()))

    def near_done(self):
        at = self.at
        for piece in range(PIECES):
            block = self.rows(at.z_lo * 2 + 1 - at.core, piece)
            self.wire.arrive(self.near[piece], block, at.twin())

    def pass_on(self, piece):
        at, wire = self.at, self.wire
        block = self.rows((1 - at.z_lo) * 2 + at.core, piece)
        wire.arrive(self.over[piece], block, at.above())
        self.copies.append(wire.send(self.passed[piece], block, block, at.twin()))

    def far_done(self, piece):
        at = self.at
        block = self.rows((1 - at.z_lo) * 2 + 1 - at.core, piece)
        self.wire.arrive(self.passed[piece], block, at.twin())
        if piece == PIECES - 1:
            for copy in self.copies:
                self.wire.release(copy)


class Collect:
    def __init__(self, wire, at, part, help_ref, near_ref, over_ref):
        self.wire, self.at, self.part = wire, at, part
        self.help_ref, self.near_ref, self.over_ref = help_ref, near_ref, over_ref
        self.help = [wire.slot() for _ in range(PIECES)]
        self.near = wire.slot()
        self.over = [wire.slot() for _ in range(PIECES)]
        self.copies = []

    def rows(self, z_lo, core, piece):
        start = (z_lo * 2 + core) * OWN + piece * PIECE
        return pl.ds(pl.multiple_of(start, PIECE), PIECE)

    def other_ready(self, piece):
        at = self.at
        block = self.part.at[self.rows(1 - at.z_lo, 1 - at.core, piece)]
        landing = self.help_ref.at[pl.ds(piece * PIECE, PIECE)]
        self.copies.append(self.wire.send(self.help[piece], block, landing, at.twin()))

    def own_ready(self):
        at = self.at
        start = pl.multiple_of((at.z_lo * 2 + 1 - at.core) * OWN, OWN)
        block = self.part.at[pl.ds(start, OWN)]
        self.copies.append(self.wire.send(self.near, block, self.near_ref, at.twin()))

    def send_over(self, piece):
        at = self.at
        window = pl.ds(piece * PIECE, PIECE)
        self.wire.arrive(self.help[piece], self.help_ref.at[window], at.twin())
        rows = self.rows(1 - at.z_lo, at.core, piece)
        total = self.part[rows, :].astype(jnp.float32) + self.help_ref[window, :].astype(
            jnp.float32
        )
        self.part[rows, :] = total.astype(jnp.bfloat16)
        self.copies.append(
            self.wire.send(
                self.over[piece], self.part.at[rows], self.over_ref.at[window], at.above()
            )
        )

    def result(self, piece):
        at = self.at
        window = pl.ds(piece * PIECE, PIECE)
        if piece == 0:
            self.wire.arrive(self.near, self.near_ref, at.twin())
        total = self.part[self.rows(at.z_lo, at.core, piece), :].astype(
            jnp.float32
        ) + self.near_ref[window, :].astype(jnp.float32)
        self.wire.arrive(self.over[piece], self.over_ref.at[window], at.above())
        total = total + self.over_ref[window, :].astype(jnp.float32)
        if piece == PIECES - 1:
            for copy in self.copies:
                self.wire.release(copy)
        return total


def here_rows(at):
    return ((at.z_lo * 2 * OWN, 2 * OWN),)


def there_rows(at, piece):
    start = (1 - at.z_lo) * 2 * OWN + piece * PIECE
    return ((start, PIECE), (start + OWN, PIECE))


def windows(rows):
    return [pl.ds(pl.multiple_of(start, size), size) for start, size in rows]


def take(ref, rows, cols=slice(None)):
    pieces = [ref[window, cols] for window in windows(rows)]
    return pieces[0] if len(pieces) == 1 else jnp.concatenate(pieces, axis=0)


def put(ref, rows, cols, value):
    place = 0
    for window, (_, size) in zip(windows(rows), rows):
        ref[window, cols] = value[place : place + size]
        place += size


def nn(left, right):
    return jnp.dot(left, right, preferred_element_type=jnp.float32)


def nt(left, right):
    return lax.dot_general(
        left, right, (((1,), (1,)), ((), ())), preferred_element_type=jnp.float32
    )


def tn(left, right):
    return lax.dot_general(
        left, right, (((0,), (0,)), ((), ())), preferred_element_type=jnp.float32
    )


def rope_tables(heads):
    half = HD // 2
    position = jnp.arange(SEQ_ROWS, dtype=jnp.float32)[:, None]
    exponent = 2.0 * jnp.arange(half, dtype=jnp.float32) / HD
    angles = position * (rope_base ** (-exponent))[None, :]
    cosine, sine = jnp.cos(angles), jnp.sin(angles)
    wide_cosine = jnp.concatenate([cosine, cosine], axis=1)
    wide_sine = jnp.concatenate([-sine, sine], axis=1)
    return jnp.tile(wide_cosine, (1, heads)), jnp.tile(wide_sine, (1, heads))


def swap_halves(values):
    width = values.shape[1]
    lane = lax.broadcasted_iota(jnp.int32, values.shape, 1)
    first = lax.rem(lane, HD) < HD // 2
    return jnp.where(
        first, pltpu.roll(values, width - HD // 2, 1), pltpu.roll(values, HD // 2, 1)
    )


def head_of(values, start):
    width = values.shape[1]
    moved = values if start == 0 else pltpu.roll(values, width - start, 1)
    moved = moved[:, :128]
    lane = lax.broadcasted_iota(jnp.int32, moved.shape, 1)
    return jnp.where(lane < HD, moved, 0.0)


def side_by_side(heads):
    tiles = []
    for tile in range(len(heads) * HD // 128):
        total = None
        lane = lax.broadcasted_iota(jnp.int32, heads[0].shape, 1)
        for index, head in enumerate(heads):
            start = index * HD - tile * 128
            if start <= -HD or start >= 128:
                continue
            moved = pltpu.roll(head, start % 128, 1) if start else head
            if start > 0 or start < 0:
                keep = (lane >= start) if start > 0 else (lane < start + HD)
                moved = jnp.where(keep, moved, 0.0)
            total = moved if total is None else total + moved
        tiles.append(total)
    return jnp.concatenate(tiles, axis=1)


def weight(w_ref, layer, cols):
    value = w_ref[layer, :, :, cols]
    return value.reshape(MODEL, value.shape[-1])


def turn_rows(source, target):
    def tile(index, carry):
        start = pl.multiple_of(index * 256, 256)
        target[pl.ds(start, 256), :] = source[:, pl.ds(start, 256)].T
        return carry

    lax.fori_loop(0, MODEL // 256, tile, 0)


def gather_job(wire, at, full, layer, group):
    parts = []
    for (first, second), (left, right) in zip((("y", "x"), ("x", "y")), group):

        def block(first_step, second_step, cols, first=first):
            x_step, y_step = (
                (first_step, second_step) if first == "x" else (second_step, first_step)
            )
            row = shift(at.x, x_step) * 192 + shift(at.y, y_step) * 48
            return full.at[layer, :, pl.ds(pl.multiple_of(row, 48), 48), cut(cols)]

        parts.append(
            dict(
                first=first,
                second=second,
                left=left,
                right=right,
                whole=(left[0], right[1]),
                block=block,
                one={s: wire.slot() for s in (1, -1)},
                two={s: wire.slot() for s in (1, -1)},
                side={(f, s): wire.slot() for f in (0, -1, 1, 2) for s in (1, -1)},
                far={(f, s): wire.slot() for f in (0, -1, 1, 2) for s in (1, -1)},
            )
        )

    def half(part, step):
        return part["left"] if step == 1 else part["right"]

    def one_start(part, step):
        piece = part["block"](0, 0, part["whole"])
        wire.send(part["one"][step], piece, piece, at.beside(part["first"], step))

    def side_start(part, first_step):
        for step in (1, -1):
            piece = part["block"](first_step, 0, part["whole"])
            wire.send(
                part["side"][first_step, step], piece, piece, at.beside(part["second"], step)
            )

    def one_done(part, step):
        target = at.beside(part["first"], step)
        wire.arrive(part["one"][step], part["block"](-step, 0, part["whole"]), target)
        piece = part["block"](-step, 0, half(part, step))
        wire.send(part["two"][step], piece, piece, target)

    def two_done(part):
        for step in (1, -1):
            piece = part["block"](2, 0, half(part, step))
            wire.arrive(part["two"][step], piece, at.beside(part["first"], step))

    def side_done(part, first_step):
        for step in (1, -1):
            target = at.beside(part["second"], step)
            landed = part["block"](first_step, -step, part["whole"])
            wire.arrive(part["side"][first_step, step], landed, target)
            piece = part["block"](first_step, -step, half(part, step))
            wire.send(part["far"][first_step, step], piece, piece, target)

    def far_done(part, first_step):
        for step in (1, -1):
            piece = part["block"](first_step, 2, half(part, step))
            wire.arrive(part["far"][first_step, step], piece, at.beside(part["second"], step))

    for part in parts:
        for step in (1, -1):
            one_start(part, step)
    for part in parts:
        side_start(part, 0)
    yield
    for step in (1, -1):
        for part in parts:
            one_done(part, step)
    for first_step in (-1, 1):
        for part in parts:
            side_start(part, first_step)
    yield
    for part in parts:
        two_done(part)
    for part in parts:
        side_start(part, 2)
    for part in parts:
        side_done(part, 0)
    yield
    for first_step in (-1, 1):
        for part in parts:
            side_done(part, first_step)
    yield
    for part in parts:
        side_done(part, 2)
    yield
    for first_step in (0, -1, 1, 2):
        for part in parts:
            far_done(part, first_step)
    yield


STEPS = (1, 2, 1, 2)
LAG = 2


class Gather:
    def __init__(self, wire, local, at, shard, full, kept):
        self.wire, self.local, self.at, self.shard = wire, local, at, shard
        self.full, self.kept = full, kept
        self.groups = [
            (layer, group)
            for layer in range(2)
            for group in (ATTN_PARTS, GU_PARTS, DOWN_PARTS)
        ]
        self.jobs = [gather_job(wire, at, full, *pair) for pair in self.groups]
        self.slots = [wire.slot() for _ in self.groups]
        self.own = []
        count = len(self.jobs)
        self.order = [
            (index, turn - LAG * index)
            for turn in range(LAG * count + 6)
            for index in range(count)
            if 0 <= turn - LAG * index < 6
        ]
        self.done = 0

    def columns(self, index):
        group = self.groups[index][1]
        return cut((group[0][0][0], group[1][1][1]))

    def mine(self, z_hi):
        row = self.at.x * 192 + self.at.y * 48
        return (z_hi, pl.ds(pl.multiple_of(row, 48), 48))

    def begin(self):
        at = self.at
        z_own, rows = self.mine(at.z_hi)
        for index, (layer, _) in enumerate(self.groups):
            cols = self.columns(index)
            source = self.shard.at[layer, :, cols]
            target = self.full.at[layer, z_own, rows, cols]
            self.wire.send(self.slots[index], source, target, at.across())
            self.own.append(self.local.start(source, target))

    def step(self, count=1):
        for _ in range(count):
            if self.done == len(self.order):
                return
            index, stage = self.order[self.done]
            self.done += 1
            layer = self.groups[index][0]
            cols = self.columns(index)
            if stage == 0:
                self.local.wait(self.own[index])
                z_other, rows = self.mine(1 - self.at.z_hi)
                landed = self.full.at[layer, z_other, rows, cols]
                self.wire.arrive(self.slots[index], landed, self.at.across())
            next(self.jobs[index])
            if stage == 5:
                self.local.start(
                    self.full.at[layer, :, :, cols], self.kept.at[layer, :, :, cols]
                )

    def until(self, index):
        while (index, 5) in self.order[self.done :]:
            self.step()


def normed(rows_in, gain):
    inverse = lax.rsqrt(jnp.mean(rows_in * rows_in, axis=-1, keepdims=True) + norm_eps)
    return (rows_in * inverse * gain).astype(jnp.bfloat16)


def project_heads(layer, rows, n1, w, cosine, sine, q_ref, k_ref, v_ref):
    left = take(n1.at[layer], rows)
    cosine_rows, sine_rows = take(cosine, rows), take(sine, rows)
    every = slice(None)
    query = nn(left, weight(w, layer, pl.ds(0, 384)))
    turned = query * cosine_rows + swap_halves(query) * sine_rows
    for head in range(4):
        put(q_ref.at[layer, head], rows, every, head_of(turned, head * HD).astype(jnp.bfloat16))
    both = nn(left, weight(w, layer, pl.ds(384, 384)))
    turned = both * cosine_rows + swap_halves(both) * sine_rows
    for head in range(2):
        put(k_ref.at[layer, head], rows, every, head_of(turned, head * HD).astype(jnp.bfloat16))
        value = head_of(both, 192 + head * HD).astype(jnp.bfloat16)
        put(v_ref.at[layer, head], rows, every, value)


def attend(layer, blocks, q_ref, k_ref, v_ref, p_ref, o_ref):
    for block in blocks:
        rows = pl.ds(block * 128, 128)
        keys = (block + 1) * 128
        outputs = []
        for head in range(2):
            pair = jnp.concatenate(
                [q_ref[layer, 2 * head, rows, :], q_ref[layer, 2 * head + 1, rows, :]], axis=0
            )
            scores = nt(pair, k_ref[layer, head, pl.ds(0, keys), :]) * SCALING
            row = lax.broadcasted_iota(jnp.int32, (256, keys), 0) % 128 + block * 128
            key = lax.broadcasted_iota(jnp.int32, (256, keys), 1)
            scores = jnp.where(row >= key, scores, -1e30)
            peak = jnp.max(scores, axis=-1, keepdims=True)
            exponent = jnp.exp(scores - peak)
            inverse = 1.0 / jnp.sum(exponent, axis=-1, keepdims=True)
            shares = (exponent * inverse).astype(jnp.bfloat16)
            p_ref[layer, 2 * head, rows, pl.ds(0, keys)] = shares[:128]
            p_ref[layer, 2 * head + 1, rows, pl.ds(0, keys)] = shares[128:]
            out = nn(shares, v_ref[layer, head, pl.ds(0, keys), :])
            outputs += [out[:128], out[128:]]
        o_ref[layer, rows, :] = side_by_side(outputs).astype(jnp.bfloat16)


def rows_partial(layer, rows, left_ref, w, cols, part):
    left = take(left_ref, rows)
    for half in range(2):

        def tile(index, carry, half=half):
            start = pl.multiple_of(index * 256, 256)
            right = w[layer, half, pl.ds(start, 256), cut(cols)]
            column = pl.ds(pl.multiple_of(half * 768 + start, 256), 256)
            put(part, rows, column, nt(left, right).astype(jnp.bfloat16))
            return carry

        lax.fori_loop(0, 3, tile, 0)


def hidden_rows(layer, rows, n2, w, g_ref, u_ref, a_ref):
    left = take(n2.at[layer], rows)

    def tile(index, carry):
        start = pl.multiple_of(index * 256, 256)
        column = pl.ds(start, 256)
        gate = nn(left, weight(w, layer, pl.ds(GATE[0] + start, 256)))
        up = nn(left, weight(w, layer, pl.ds(UP[0] + start, 256)))
        hidden = gate * up / (1.0 + jnp.exp(-gate))
        put(g_ref.at[layer], rows, column, gate.astype(g_ref.dtype))
        put(u_ref.at[layer], rows, column, up.astype(u_ref.dtype))
        put(a_ref.at[layer], rows, column, hidden.astype(jnp.bfloat16))
        return carry

    lax.fori_loop(0, 4, tile, 0)


def forward_kernel(
    shard,
    gains_placed,
    tokens,
    grad_out,
    cosine_kept,
    sine_kept,
    w_kept,
    gains,
    dm_kept,
    dm_turned_kept,
    n1_kept,
    n2_kept,
    q_kept,
    k_kept,
    v_kept,
    p_kept,
    o_kept,
    g_kept,
    u_kept,
    a_kept,
    x_kept,
    h_kept,
    cosine,
    sine,
    w,
    n1,
    n2,
    q_ref,
    k_ref,
    v_ref,
    p_ref,
    o_ref,
    g_ref,
    u_ref,
    a_ref,
    x_ref,
    h_ref,
    dm,
    n1_turned,
    n2_turned,
    part,
    help_ref,
    near_ref,
    over_ref,
    gains_landing,
    send_sems,
    recv_sems,
    local_sems,
):
    at = Place()
    at.greet()
    wire = Wire(send_sems, recv_sems)
    local = Local(local_sems)
    gather = Gather(wire, local, at, shard, w, w_kept)
    gather.begin()
    tables = [local.start(cosine_kept, cosine), local.start(sine_kept, sine)]
    gather.step()
    gains[...] = gains_placed[...]
    rounds = sum_small(wire, at, gains, gains_landing, False)
    for _ in rounds:
        gather.step()
    turn = 0

    def collector():
        nonlocal turn
        turn += 1
        slot = turn % 2
        return Collect(
            wire, at, part, help_ref.at[slot], near_ref.at[slot], over_ref.at[slot]
        )

    def own(piece):
        return pl.ds(pl.multiple_of(at.tensor * OWN + piece * PIECE, PIECE), PIECE)

    def window(piece):
        return pl.ds(piece * PIECE, PIECE)

    here = here_rows(at)
    turning = [None, None]
    spread = Spread(wire, at, n1.at[0])
    for piece in range(PIECES):
        x_rows = tokens[window(piece), :].astype(jnp.float32)
        x_ref[0, window(piece), :] = x_rows
        n1[0, own(piece), :] = normed(x_rows, gains[pl.ds(0, 1), :])
        spread.send(piece)
    for layer in range(2):
        heads = (n1, w, cosine, sine, q_ref, k_ref, v_ref)
        spread.near_done()
        gather.until(3 * layer)
        while tables:
            local.wait(tables.pop())
        project_heads(layer, here, *heads)
        gather.step(STEPS[0])
        spread.pass_on(0)
        spread.far_done(0)
        project_heads(layer, there_rows(at, 0), *heads)
        spread.pass_on(1)
        spread.far_done(1)
        project_heads(layer, there_rows(at, 1), *heads)
        for source, target in ((q_ref, q_kept), (k_ref, k_kept), (v_ref, v_kept)):
            local.start(source.at[layer], target.at[layer])
        collect = collector()
        around = (q_ref, k_ref, v_ref, p_ref, o_ref)

        def blocks(first, second, layer=layer, around=around):
            @pl.when(at.z_lo == 0)
            def _():
                attend(layer, first, *around)

            @pl.when(at.z_lo == 1)
            def _():
                attend(layer, second, *around)

        blocks((2, 3), (0, 1))
        for piece in range(PIECES):
            rows_partial(layer, there_rows(at, piece), o_ref.at[layer], w, OUT, part)
            collect.other_ready(piece)
        collect.send_over(0)
        collect.send_over(1)
        blocks((0, 1), (2, 3))
        rows_partial(layer, here, o_ref.at[layer], w, OUT, part)
        collect.own_ready()
        for source, target in ((p_ref, p_kept), (o_ref, o_kept)):
            local.start(source.at[layer], target.at[layer])
        gather.step(STEPS[1])
        spread = Spread(wire, at, n2.at[layer])
        for piece in range(PIECES):
            h_rows = x_ref[layer, window(piece), :] + collect.result(piece)
            h_ref[layer, window(piece), :] = h_rows
            n2[layer, own(piece), :] = normed(h_rows, gains[pl.ds(2 * layer + 1, 1), :])
            spread.send(piece)
        if layer == 1:
            spread_back = Spread(wire, at, dm)
            for piece in range(PIECES):
                dm[own(piece), :] = grad_out[window(piece), :]
                spread_back.send(piece)
        if layer == 1:
            local.wait(turning[0])
        turn_rows(n1.at[layer], n1_turned)
        turning[0] = local.start(n1_turned, n1_kept.at[layer])
        spread.near_done()
        gather.until(3 * layer + 1)
        mlp = (n2, w, g_ref, u_ref, a_ref)
        hidden_rows(layer, here, *mlp)
        gather.step(STEPS[2])
        if layer == 1:
            spread.pass_on(0)
            spread_back.pass_on(0)
            spread.far_done(0)
            hidden_rows(layer, there_rows(at, 0), *mlp)
            gather.step()
            spread.pass_on(1)
            spread_back.pass_on(1)
            spread.far_done(1)
            hidden_rows(layer, there_rows(at, 1), *mlp)
            gather.step()
            spread_back.near_done()
            spread_back.far_done(0)
            spread_back.far_done(1)
        else:
            spread.pass_on(0)
            spread.far_done(0)
            hidden_rows(layer, there_rows(at, 0), *mlp)
            spread.pass_on(1)
            spread.far_done(1)
            hidden_rows(layer, there_rows(at, 1), *mlp)
            gather.until(2)
            collect = collector()
            for piece in range(PIECES):
                rows_partial(layer, there_rows(at, piece), a_ref.at[layer], w, DOWN, part)
                collect.other_ready(piece)
            collect.send_over(0)
            rows_partial(layer, here, a_ref.at[layer], w, DOWN, part)
            collect.own_ready()
            collect.send_over(1)
        for source, target in (
            (h_ref, h_kept),
            (g_ref, g_kept),
            (u_ref, u_kept),
            (a_ref, a_kept),
        ):
            local.start(source.at[layer], target.at[layer])
        if layer == 1:
            local.wait(turning[1])
        turn_rows(n2.at[layer], n2_turned)
        turning[1] = local.start(n2_turned, n2_kept.at[layer])
        gather.step(STEPS[3])
        if layer == 1:
            local.start(dm, dm_kept)
            local.wait(turning[0])
            turn_rows(dm, n1_turned)
            local.start(n1_turned, dm_turned_kept)
            break
        spread = Spread(wire, at, n1.at[1])
        for piece in range(PIECES):
            total = h_ref[layer, window(piece), :] + collect.result(piece)
            x_ref[1, window(piece), :] = total
            n1[1, own(piece), :] = normed(total, gains[pl.ds(2, 1), :])
            spread.send(piece)
        local.start(x_ref.at[1], x_kept)
    gather.until(5)
    local.drain()
    wire.drain()


KEEP = jnp.bfloat16


def run_forward(shard, gains_placed, tokens, grad_out, cosine, sine):
    def kept(*shape, kind=jnp.bfloat16):
        return jax.ShapeDtypeStruct(shape, kind)

    def held(*shape, kind=jnp.bfloat16):
        return pltpu.VMEM(shape, kind)

    vmem = pl.BlockSpec(memory_space=pltpu.VMEM)
    hbm = pl.BlockSpec(memory_space=pl.ANY)
    float32 = jnp.float32
    wires = 6 * 41 + 7 + 5 * 6 + 3 * 5
    return pl.pallas_call(
        forward_kernel,
        out_shape=(
            kept(2, 2, 768, WIDTH),
            kept(8, MODEL, kind=float32),
            kept(SEQ_ROWS, MODEL),
            kept(MODEL, SEQ_ROWS),
            kept(2, MODEL, SEQ_ROWS),
            kept(2, MODEL, SEQ_ROWS),
            kept(2, 4, SEQ_ROWS, 128),
            kept(2, 2, SEQ_ROWS, 128),
            kept(2, 2, SEQ_ROWS, 128),
            kept(2, 4, SEQ_ROWS, SEQ_ROWS),
            kept(2, SEQ_ROWS, 384),
            kept(2, SEQ_ROWS, 1024, kind=KEEP),
            kept(2, SEQ_ROWS, 1024, kind=KEEP),
            kept(2, SEQ_ROWS, 1024),
            kept(OWN, MODEL, kind=float32),
            kept(2, OWN, MODEL, kind=float32),
        ),
        in_specs=[hbm] + [vmem] * 3 + [hbm] * 2,
        out_specs=(hbm, vmem) + (hbm,) * 14,
        scratch_shapes=[
            held(SEQ_ROWS, 384, kind=float32),
            held(SEQ_ROWS, 384, kind=float32),
            held(2, 2, 768, WIDTH),
            held(2, SEQ_ROWS, MODEL),
            held(2, SEQ_ROWS, MODEL),
            held(2, 4, SEQ_ROWS, 128),
            held(2, 2, SEQ_ROWS, 128),
            held(2, 2, SEQ_ROWS, 128),
            held(2, 4, SEQ_ROWS, SEQ_ROWS),
            held(2, SEQ_ROWS, 384),
            held(2, SEQ_ROWS, 1024, kind=KEEP),
            held(2, SEQ_ROWS, 1024, kind=KEEP),
            held(2, SEQ_ROWS, 1024),
            held(2, OWN, MODEL, kind=float32),
            held(2, OWN, MODEL, kind=float32),
            held(SEQ_ROWS, MODEL),
            held(MODEL, SEQ_ROWS),
            held(MODEL, SEQ_ROWS),
            held(SEQ_ROWS, MODEL),
            held(2, OWN, MODEL),
            held(2, OWN, MODEL),
            held(2, OWN, MODEL),
            held(7, 8, MODEL, kind=float32),
            pltpu.SemaphoreType.DMA((wires,)),
            pltpu.SemaphoreType.DMA((wires,)),
            pltpu.SemaphoreType.DMA((48,)),
        ],
        compiler_params=pltpu.CompilerParams(
            collective_id=0, has_side_effects=True, vmem_limit_bytes=62 * 2**20
        ),
        name="forward",
    )(shard, gains_placed, tokens, grad_out, cosine, sine)


JOBS = (
    (((3200, 3456), (3456, 3712)), ((3712, 3968), (3968, 4224))),
    (((1152, 1408), (1408, 1664)), ((1664, 1920), (1920, 2176))),
    (((2176, 2432), (2432, 2688)), ((2688, 2944), (2944, 3200))),
    (((0, 256), (256, 512)), ((512, 768), (768, 1152))),
)
JOB_WIDTH = 1152
SETS = 3
LAG_BACK = 2


def add_rows(target, terms):
    lead = target.shape[:-2]

    def step(index, carry):
        window = ()
        if lead:
            window = (index // lead[1], index % lead[1])
        total = None
        for term in terms:
            value = term[window + (slice(None), slice(None))].astype(jnp.float32)
            total = value if total is None else total + value
        target[window + (slice(None), slice(None))] = total.astype(target.dtype)
        return carry

    lax.fori_loop(0, math.prod(lead), step, 0)


def scatter_job(wire, local, at, grads, layer, group, bufs, finish):
    one, two_up, two_down, small_one, small_up, small_down, near_side, near_own = bufs
    base = group[0][0][0]
    parts = []
    for (first, second), (left, right) in zip((("y", "x"), ("x", "y")), group):

        def region(step, cols, second=second):
            if second == "x":
                return grads.at[layer, :, shift(at.x, step), :, :, cut(cols)]
            return grads.at[layer, :, :, shift(at.y, step), :, cut(cols)]

        def mine(step, cols, first=first):
            place = at.y if first == "y" else at.x
            return two_up.at[:, shift(place, step), :, inside(cols)]

        parts.append(
            dict(
                first=first,
                second=second,
                left=left,
                right=right,
                whole=(left[0], right[1]),
                region=region,
                mine=mine,
                **{
                    name: {s: wire.slot() for s in (1, -1)}
                    for name in ("far", "raw", "sum", "far2", "raw2", "sum2")
                },
            )
        )

    def inside(cols):
        return pl.ds(cols[0] - base, cols[1] - cols[0])

    def half(part, step):
        return part["left"] if step == 1 else part["right"]

    def other(part, step):
        return part["right"] if step == 1 else part["left"]

    def big(ref, cols):
        return ref.at[:, :, :, inside(cols)]

    def small(ref, cols):
        return ref.at[:, :, inside(cols)]

    copies = []
    near = {}
    for part in parts:
        for step in (1, -1):
            cols = half(part, step)
            target = at.beside(part["second"], step)
            copies.append(
                wire.send(part["far"][step], part["region"](2, cols), big(one, cols), target)
            )
    for number, part in enumerate(parts):
        for step in (1, -1):
            cols = other(part, step)
            landing = two_up if step == 1 else two_down
            target = at.beside(part["second"], step)
            copies.append(
                wire.send(part["raw"][step], part["region"](step, cols), big(landing, cols), target)
            )
            cols = half(part, step)
            near[number, step] = local.start(part["region"](step, cols), big(near_side, cols))
    yield
    for number, part in enumerate(parts):
        cols = part["whole"]
        near[number, 0] = local.start(part["region"](0, cols), big(near_own, cols))
    for step in (1, -1):
        for number, part in enumerate(parts):
            cols = half(part, step)
            target = at.beside(part["second"], step)
            piece = big(one, cols)
            local.wait(near[number, step])
            wire.arrive(part["far"][step], piece, target)
            add_rows(piece, (piece, big(near_side, cols)))
            landing = two_up if step == 1 else two_down
            copies.append(wire.send(part["sum"][step], piece, big(landing, cols), target))
    yield
    for number, part in enumerate(parts):
        local.wait(near[number, 0])
        for step in (1, -1):
            target = at.beside(part["second"], step)
            landing = two_up if step == 1 else two_down
            for name, cols in (("raw", other(part, step)), ("sum", half(part, step))):
                wire.arrive(part[name][step], big(landing, cols), target)
        cols = part["whole"]
        add_rows(big(two_up, cols), (big(near_own, cols), big(two_up, cols), big(two_down, cols)))
        for step in (1, -1):
            target = at.beside(part["first"], step)
            cols = half(part, step)
            copies.append(
                wire.send(part["far2"][step], part["mine"](2, cols), small(small_one, cols), target)
            )
            cols = other(part, step)
            landing = small_up if step == 1 else small_down
            copies.append(
                wire.send(part["raw2"][step], part["mine"](step, cols), small(landing, cols), target)
            )
    yield
    for step in (1, -1):
        for part in parts:
            cols = half(part, step)
            target = at.beside(part["first"], step)
            piece = small(small_one, cols)
            wire.arrive(part["far2"][step], piece, target)
            own = part["mine"](step, cols)
            for z_hi in range(2):
                add_rows(piece.at[z_hi], (piece.at[z_hi], own.at[z_hi]))
            landing = small_up if step == 1 else small_down
            copies.append(wire.send(part["sum2"][step], piece, small(landing, cols), target))
    yield
    for part in parts:
        for step in (1, -1):
            target = at.beside(part["first"], step)
            landing = small_up if step == 1 else small_down
            for name, cols in (("raw2", other(part, step)), ("sum2", half(part, step))):
                wire.arrive(part[name][step], small(landing, cols), target)
        cols = part["whole"]
        finish(
            cols,
            [
                [
                    ref.at[z_hi]
                    for ref in (part["mine"](0, cols), small(small_up, cols), small(small_down, cols))
                ]
                for z_hi in (1 - at.z_hi, at.z_hi)
            ],
        )
    for copy in copies:
        wire.release(copy)
    yield


class Scatter:
    def __init__(self, wire, local, at, grads, summed, sets, leaving, landed, credits):
        self.wire, self.local, self.at, self.grads = wire, local, at, grads
        self.summed, self.leaving, self.landed, self.credits = summed, leaving, landed, credits
        self.groups = [(layer, group) for layer in (1, 0) for group in JOBS]
        self.last = []
        self.jobs = []
        for index, (layer, group) in enumerate(self.groups):
            bufs = tuple(ref.at[index % ref.shape[0]] for ref in sets)
            self.jobs.append(
                scatter_job(
                    wire, local, at, grads, layer, group, bufs, self.finisher(index, layer, group)
                )
            )
        count = len(self.jobs)
        self.order = [
            (index, turn - LAG_BACK * index)
            for turn in range(LAG_BACK * count + 6)
            for index in range(count)
            if 0 <= turn - LAG_BACK * index < 6
        ]
        self.done = 0
        self.ready = 0

    def finisher(self, index, layer, group):
        wire, at = self.wire, self.at
        base = group[0][0][0]

        def finish(cols, terms):
            theirs, own = terms
            window = pl.ds(cols[0] - base, cols[1] - cols[0])
            piece = self.leaving.at[index, :, window]
            add_rows(piece, theirs)
            slot = wire.slot()
            landing = self.landed.at[index, :, window]
            wire.send(slot, piece, landing, at.across())
            target = self.summed.at[layer, :, cut(cols)]
            add_rows(target, own)
            self.last.append((index, slot, landing, target))

        return finish

    def turn(self):
        if self.done < len(self.order):
            index, stage = self.order[self.done]
            now = LAG_BACK * index + stage
            while self.done < len(self.order):
                index, stage = self.order[self.done]
                if LAG_BACK * index + stage != now or index >= self.ready:
                    return
                self.step()

    def step(self, count=1):
        at = self.at
        for _ in range(count):
            if self.done == len(self.order):
                return
            index, stage = self.order[self.done]
            if index >= self.ready:
                return
            self.done += 1
            ways = [(axis, step) for axis in ("x", "y") for step in (1, -1)]
            if stage == 5:
                for job, slot, landing, target in self.last:
                    if job == index:
                        self.wire.arrive(slot, landing, at.across())
                        add_rows(target, (target, landing))
                continue
            if stage == 0 and index >= SETS:
                for number in range(4):
                    pl.semaphore_wait(self.credits.at[number], 1)
            next(self.jobs[index])
            if stage == 4 and index + SETS < len(self.jobs):
                for number, (axis, step) in enumerate(ways):
                    pl.semaphore_signal(
                        self.credits.at[number],
                        inc=1,
                        device_id=at.beside(axis, step),
                        device_id_type=MESH_IDS,
                    )


def norm_backward(rows_in, gain, grad_normed):
    inverse = lax.rsqrt(jnp.mean(rows_in * rows_in, axis=-1, keepdims=True) + norm_eps)
    scaled = rows_in * inverse
    grad_gain = jnp.sum(grad_normed * scaled, axis=0, keepdims=True)
    grad_scaled = grad_normed * gain
    grad_input = inverse * (
        grad_scaled - scaled * jnp.mean(grad_scaled * scaled, axis=-1, keepdims=True)
    )
    return grad_input, grad_gain


def hidden_back(rows, dm, w, g_ref, u_ref, dgu):
    left = take(dm, rows)

    def tile(index, carry):
        start = pl.multiple_of(index * 256, 256)
        column = pl.ds(start, 256)
        grad = nn(left, weight(w, 0, pl.ds(DOWN[0] + start, 256)))
        gate = take(g_ref, rows, column).astype(jnp.float32)
        up = take(u_ref, rows, column).astype(jnp.float32)
        sigma = 1.0 / (1.0 + jnp.exp(-gate))
        grad_gate = grad * up * sigma * (1.0 + gate * (1.0 - sigma))
        put(dgu, rows, column, grad_gate.astype(jnp.bfloat16))
        column = pl.ds(pl.multiple_of(1024 + start, 256), 256)
        put(dgu, rows, column, (grad * gate * sigma).astype(jnp.bfloat16))
        return carry

    lax.fori_loop(0, 4, tile, 0)


def attend_back(q_ref, k_ref, v_ref, p_ref, do_ref, dk_ref, dv_ref, cosine, sine, dqkv):
    dk_ref[...] = jnp.zeros_like(dk_ref)
    dv_ref[...] = jnp.zeros_like(dv_ref)
    for block in range(4):
        rows = pl.ds(block * 128, 128)
        keys = pl.ds(0, (block + 1) * 128)
        queries = []
        for head in range(2):
            both = (2 * head, 2 * head + 1)
            shares = jnp.concatenate([p_ref[h, rows, keys] for h in both], axis=0)
            pair = jnp.concatenate([q_ref[h, rows, :] for h in both], axis=0)
            grad = jnp.concatenate([do_ref[h, rows, :] for h in both], axis=0)
            wide = shares.astype(jnp.float32)
            grad_shares = nt(grad, v_ref[head, keys, :])
            inner = jnp.sum(grad_shares * wide, axis=-1, keepdims=True)
            grad_scores = (wide * (grad_shares - inner)).astype(jnp.bfloat16)
            grad_pair = nn(grad_scores, k_ref[head, keys, :]) * SCALING
            queries += [grad_pair[:128], grad_pair[128:]]
            dk_ref[head, :, keys] += nn(pair.T, grad_scores)
            dv_ref[head, :, keys] += nn(grad.T, shares)
        grad_rows = side_by_side(queries)
        turned = grad_rows * cosine[rows, :] - swap_halves(grad_rows) * sine[rows, :]
        dqkv[rows, pl.ds(0, 384)] = turned.astype(jnp.bfloat16)
    both = side_by_side(
        [dk_ref[0].T * SCALING, dk_ref[1].T * SCALING, dv_ref[0].T, dv_ref[1].T]
    )
    turned = both * cosine[...] - swap_halves(both) * sine[...]
    lane = lax.broadcasted_iota(jnp.int32, both.shape, 1)
    dqkv[:, pl.ds(384, 384)] = jnp.where(lane < 192, turned, both).astype(jnp.bfloat16)


def backward_kernel(
    gains,
    grad_out,
    tokens,
    cosine_kept,
    sine_kept,
    x_kept,
    h_kept,
    w_kept,
    dm_kept,
    dm_turned_kept,
    n1_kept,
    n2_kept,
    q_kept,
    k_kept,
    v_kept,
    p_kept,
    o_kept,
    g_kept,
    u_kept,
    a_kept,
    output,
    input_grad,
    summed,
    gains_grad,
    grads,
    cosine,
    sine,
    x_second,
    h_ref,
    w,
    n1_turned,
    n2_turned,
    q_ref,
    k_ref,
    v_ref,
    p_ref,
    o_ref,
    g_ref,
    u_ref,
    a_ref,
    dm,
    turned,
    dgu,
    do_ref,
    dk_ref,
    dv_ref,
    dqkv,
    dx,
    part,
    help_ref,
    near_ref,
    over_ref,
    staged,
    one,
    two_up,
    two_down,
    small_one,
    small_up,
    small_down,
    near_side,
    near_own,
    leaving,
    landed,
    gains_landing,
    send_sems,
    recv_sems,
    local_sems,
    credits,
):
    at = Place()
    at.greet()
    wire = Wire(send_sems, recv_sems)
    local = Local(local_sems)
    sets = (one, two_up, two_down, small_one, small_up, small_down, near_side, near_own)
    scatter = Scatter(wire, local, at, grads, summed, sets, leaving, landed, credits)
    turn = 0

    def collector():
        nonlocal turn
        turn += 1
        slot = turn % 2
        return Collect(
            wire, at, part, help_ref.at[slot], near_ref.at[slot], over_ref.at[slot]
        )

    loads = {}

    def load(layer, names):
        pairs = dict(
            n1=(n1_kept, n1_turned),
            n2=(n2_kept, n2_turned),
            q=(q_kept, q_ref),
            k=(k_kept, k_ref),
            v=(v_kept, v_ref),
            p=(p_kept, p_ref),
            o=(o_kept, o_ref),
            g=(g_kept, g_ref),
            u=(u_kept, u_ref),
            a=(a_kept, a_ref),
            dm=(dm_kept, dm.at[0]),
            turned=(dm_turned_kept, turned),
        )
        columns = dict(down=DOWN, gu=(GATE[0], UP[1]), out=OUT, qkv=QKV)
        for name in names:
            if name in columns:
                cols = cut(columns[name])
                loads[name] = local.start(w_kept.at[layer, :, :, cols], w.at[0, :, :, cols])
            else:
                kept, held = pairs[name]
                source = kept if name in ("dm", "turned") else kept.at[layer]
                loads[name] = local.start(source, held)

    def ready(*names):
        for name in names:
            local.wait(loads.pop(name))

    mlp_names = ("down", "g", "u", "gu", "a", "n2")
    attn_names = ("out", "v", "p", "k", "q", "qkv", "o", "n1")
    load(1, ("a", "down", "turned", "dm", "g", "u", "gu", "n2"))
    load(1, attn_names)
    tables = [
        local.start(*pair)
        for pair in (
            (h_kept, h_ref),
            (x_kept, x_second),
            (cosine_kept, cosine),
            (sine_kept, sine),
        )
    ]
    staging = [None, None]
    tiles = 0
    behind = []

    def keep_tile(layer, left, right_ref, start, size, column):
        nonlocal tiles
        slot = tiles % 2
        tiles += 1
        if staging[slot] is not None:
            local.wait(staging[slot])
        product = nn(left[...], right_ref[:, pl.ds(start, size)])
        staged[slot, :, :, :, :, pl.ds(0, size)] = product.astype(jnp.bfloat16).reshape(
            2, SIDE, SIDE, 48, size
        )
        staging[slot] = local.start(
            staged.at[slot, :, :, :, :, pl.ds(0, size)],
            grads.at[layer, :, :, :, :, pl.ds(column, size)],
        )

    def keep_grads(layer, left, right_ref, start, width, column):
        for tile in range(0, width, 256):
            size = min(256, width - tile)
            behind.append(
                lambda tile=tile, size=size: keep_tile(
                    layer, left, right_ref, start + tile, size, column + tile
                )
            )

    def grads_kept():
        for slot in range(2):
            if staging[slot] is not None:
                local.wait(staging[slot])
                staging[slot] = None
        scatter.ready += 1

    def fill(count):
        for _ in range(min(count, len(behind))):
            behind.pop(0)()

    def own(piece):
        return pl.ds(pl.multiple_of(at.tensor * OWN + piece * PIECE, PIECE), PIECE)

    def window(piece):
        return pl.ds(piece * PIECE, PIECE)

    here = here_rows(at)
    gains_grad[...] = jnp.zeros_like(gains_grad)
    every = ((0, SEQ_ROWS),)
    dx[0] = grad_out[...].astype(jnp.float32)
    mlp = (dm.at[0], w, g_ref, u_ref, dgu)
    gu_columns = (GATE[0], UP[1])
    spread = None
    for layer in (1, 0):
        if layer == 1:
            collect_out = collector()
            ready("a", "down")
            for piece in range(PIECES):
                rows_partial(0, there_rows(at, piece), a_ref, w, DOWN, part)
                collect_out.other_ready(piece)
            ready("turned")
            keep_grads(layer, turned, a_ref, 0, 1024, DOWN[0])
            behind.append(grads_kept)
            fill(3)
            collect_out.send_over(0)
            collect_out.send_over(1)
            rows_partial(0, here, a_ref, w, DOWN, part)
            collect_out.own_ready()
            fill(len(behind))
            scatter.turn()
            ready("dm", "g", "u")
            hidden_back(every, *mlp)
            ready("n2")
            keep_grads(layer, n2_turned, dgu, 0, 1024, GATE[0])
            behind.append(grads_kept)
            keep_grads(layer, n2_turned, dgu, 1024, 1024, UP[0])
            behind.append(grads_kept)
            fill(2)
            while tables:
                local.wait(tables.pop())
            for piece in range(PIECES):
                total = h_ref[1, window(piece), :] + collect_out.result(piece)
                output[window(piece), :] = total.astype(jnp.bfloat16)
            scatter.turn()
            ready("gu")
            collect = collector()
            for piece in range(PIECES):
                rows_partial(0, there_rows(at, piece), dgu, w, gu_columns, part)
                collect.other_ready(piece)
            fill(1)
            collect.send_over(0)
            collect.send_over(1)
            rows_partial(0, here, dgu, w, gu_columns, part)
            collect.own_ready()
            scatter.turn()
        else:
            spread.near_done()
            ready("down", "g", "u")
            hidden_back(here, *mlp)
            scatter.turn()
            fill(2)
            spread.pass_on(0)
            fill(1)
            collect = collector()
            for piece in range(PIECES):
                spread.far_done(piece)
                hidden_back(there_rows(at, piece), *mlp)
                if piece == 0:
                    ready("gu")
                rows_partial(0, there_rows(at, piece), dgu, w, gu_columns, part)
                collect.other_ready(piece)
                if piece + 1 < PIECES:
                    spread.pass_on(piece + 1)
                    fill(2)
                    scatter.turn()
                collect.send_over(piece)
            rows_partial(0, here, dgu, w, gu_columns, part)
            collect.own_ready()
            fill(len(behind))
            load(0, attn_names)
            ready("a", "n2")
            turn_rows(dm.at[0], turned)
            scatter.turn()
            keep_grads(layer, turned, a_ref, 0, 1024, DOWN[0])
            behind.append(grads_kept)
            keep_grads(layer, n2_turned, dgu, 0, 1024, GATE[0])
            behind.append(grads_kept)
            keep_grads(layer, n2_turned, dgu, 1024, 1024, UP[0])
            behind.append(grads_kept)
        fill(3)
        spread = Spread(wire, at, dm.at[1])
        gain_rows = None
        for piece in range(PIECES):
            normed_grad, gain_row = norm_backward(
                h_ref[layer, window(piece), :],
                gains[pl.ds(2 * layer + 1, 1), :],
                collect.result(piece),
            )
            gain_rows = gain_row if gain_rows is None else gain_rows + gain_row
            dh = dx[0, window(piece), :] + normed_grad
            dx[1, window(piece), :] = dh
            dm[1, own(piece), :] = dh.astype(jnp.bfloat16)
            spread.send(piece)
            if piece + 1 < PIECES:
                fill(2)
        gains_grad[pl.ds(2 * layer + 1, 1), :] = gain_rows
        scatter.turn()
        ready("out")

        def heads_back(rows):
            grad = nn(take(dm.at[1], rows), weight(w, 0, cut(OUT)))
            for head in range(4):
                put(do_ref.at[head], rows, slice(None), head_of(grad, head * HD).astype(jnp.bfloat16))

        spread.near_done()
        heads_back(here)
        fill(4)
        spread.pass_on(0)
        fill(3)
        spread.far_done(0)
        heads_back(there_rows(at, 0))
        scatter.turn()
        spread.pass_on(1)
        fill(len(behind))
        if layer == 1:
            load(0, mlp_names)
        spread.far_done(1)
        heads_back(there_rows(at, 1))
        ready("v", "p", "k", "q")
        attend_back(
            q_ref, k_ref, v_ref, p_ref, do_ref, dk_ref, dv_ref, cosine, sine, dqkv
        )
        collect = collector()
        ready("qkv")
        for piece in range(PIECES):
            rows_partial(0, there_rows(at, piece), dqkv, w, QKV, part)
            collect.other_ready(piece)
        scatter.turn()
        collect.send_over(0)
        collect.send_over(1)
        rows_partial(0, here, dqkv, w, QKV, part)
        collect.own_ready()
        turn_rows(dm.at[1], turned)
        ready("o", "n1")
        keep_grads(layer, turned, o_ref, 0, 384, OUT[0])
        keep_grads(layer, n1_turned, dqkv, 0, 768, QKV[0])
        behind.append(grads_kept)
        fill(2)
        if layer == 0:
            scatter.turn()
        rows_in = tokens if layer == 0 else x_second
        spread = Spread(wire, at, dm.at[0]) if layer == 1 else None
        gain_rows = None
        for piece in range(PIECES):
            normed_grad, gain_row = norm_backward(
                rows_in[window(piece), :].astype(jnp.float32),
                gains[pl.ds(2 * layer, 1), :],
                collect.result(piece),
            )
            gain_rows = gain_row if gain_rows is None else gain_rows + gain_row
            dx_rows = dx[1, window(piece), :] + normed_grad
            if layer == 1:
                dx[0, window(piece), :] = dx_rows
                dm[0, own(piece), :] = dx_rows.astype(jnp.bfloat16)
                spread.send(piece)
                if piece == 0:
                    fill(1)
                    scatter.turn()
            else:
                input_grad[window(piece), :] = dx_rows
        gains_grad[pl.ds(2 * layer, 1), :] = gain_rows
    fill(len(behind))
    rounds = sum_small(wire, at, gains_grad, gains_landing, True)
    for _ in rounds:
        scatter.turn()
    while scatter.done < len(scatter.order):
        scatter.step()
    local.drain()
    wire.drain()


def run_backward(gains, grad_out, tokens, cosine, sine, x_second, h, kept):
    def held(*shape, kind=jnp.bfloat16):
        return pltpu.VMEM(shape, kind)

    vmem = pl.BlockSpec(memory_space=pltpu.VMEM)
    hbm = pl.BlockSpec(memory_space=pl.ANY)
    float32 = jnp.float32
    wires = 8 * 26 + 9 + 3 * 6 + 5 * 5
    return pl.pallas_call(
        backward_kernel,
        out_shape=(
            jax.ShapeDtypeStruct((OWN, MODEL), jnp.bfloat16),
            jax.ShapeDtypeStruct((OWN, MODEL), float32),
            jax.ShapeDtypeStruct((2, 48, WIDTH), float32),
            jax.ShapeDtypeStruct((8, MODEL), float32),
            jax.ShapeDtypeStruct((2, 2, SIDE, SIDE, 48, WIDTH), jnp.bfloat16),
        ),
        in_specs=[vmem] * 3 + [hbm] * (4 + len(kept)),
        out_specs=(vmem, vmem, vmem, vmem, hbm),
        scratch_shapes=[
            held(SEQ_ROWS, 384, kind=float32),
            held(SEQ_ROWS, 384, kind=float32),
            held(OWN, MODEL, kind=float32),
            held(2, OWN, MODEL, kind=float32),
            held(1, 2, 768, WIDTH),
            held(MODEL, SEQ_ROWS),
            held(MODEL, SEQ_ROWS),
            held(4, SEQ_ROWS, 128),
            held(2, SEQ_ROWS, 128),
            held(2, SEQ_ROWS, 128),
            held(4, SEQ_ROWS, SEQ_ROWS),
            held(SEQ_ROWS, 384),
            held(SEQ_ROWS, 1024, kind=KEEP),
            held(SEQ_ROWS, 1024, kind=KEEP),
            held(SEQ_ROWS, 1024),
            held(2, SEQ_ROWS, MODEL),
            held(MODEL, SEQ_ROWS),
            held(SEQ_ROWS, 2048),
            held(4, SEQ_ROWS, 128),
            held(2, 128, SEQ_ROWS, kind=float32),
            held(2, 128, SEQ_ROWS, kind=float32),
            held(SEQ_ROWS, 768),
            held(2, OWN, MODEL, kind=float32),
            held(SEQ_ROWS, MODEL),
            held(2, OWN, MODEL),
            held(2, OWN, MODEL),
            held(2, OWN, MODEL),
            held(2, 2, SIDE, SIDE, 48, 256),
            held(SETS, 2, SIDE, 48, JOB_WIDTH),
            held(SETS, 2, SIDE, 48, JOB_WIDTH),
            held(SETS, 2, SIDE, 48, JOB_WIDTH),
            held(SETS, 2, 48, JOB_WIDTH),
            held(SETS, 2, 48, JOB_WIDTH),
            held(SETS, 2, 48, JOB_WIDTH),
            held(1, 2, SIDE, 48, JOB_WIDTH),
            held(1, 2, SIDE, 48, JOB_WIDTH),
            held(8, 48, JOB_WIDTH),
            held(8, 48, JOB_WIDTH),
            held(9, 8, MODEL, kind=float32),
            pltpu.SemaphoreType.DMA((wires,)),
            pltpu.SemaphoreType.DMA((wires,)),
            pltpu.SemaphoreType.DMA((34 + 40 + 48,)),
            pltpu.SemaphoreType.REGULAR((4,)),
        ],
        compiler_params=pltpu.CompilerParams(
            collective_id=1, has_side_effects=True, vmem_limit_bytes=63 * 2**20
        ),
        name="backward",
    )(gains, grad_out, tokens, cosine, sine, x_second, h, *kept)


def pack_rows(arrays):
    query, key, value, out, gate, up, down = arrays
    turned_out = jnp.swapaxes(out, 1, 2)
    turned_down = jnp.swapaxes(down, 1, 2)
    return jnp.concatenate([query, key, value, turned_out, gate, up, turned_down], axis=2)


def body(
    tokens,
    query_weight,
    key_weight,
    value_weight,
    out_weight,
    gate_weight,
    up_weight,
    down_weight,
    norm_gains,
    grad_out,
):
    packed = pack_rows(
        (query_weight, key_weight, value_weight, out_weight, gate_weight, up_weight, down_weight)
    )
    dp = lax.axis_index("dp")
    gains_placed = lax.dynamic_update_slice(
        jnp.zeros((8, MODEL), jnp.float32),
        norm_gains.reshape(4, -1).astype(jnp.float32),
        (0, dp * 48),
    )
    cosine, sine = rope_tables(4)
    w_kept, gains, *kept, x_second, h = run_forward(
        packed, gains_placed, tokens, grad_out, cosine, sine
    )
    output, input_grad, summed, gains_grad, _ = run_backward(
        gains, grad_out, tokens, cosine, sine, x_second, h, (w_kept, *kept)
    )
    gains_own = lax.dynamic_slice(gains_grad, (0, dp * 48), (4, 48)).reshape(2, 2, 48)
    pieces, start = [], 0
    for width in COLS:
        pieces.append(summed[:, :, start : start + width])
        start += width
    query, key, value, out, gate, up, down = pieces
    return (
        output,
        input_grad,
        query,
        key,
        value,
        jnp.swapaxes(out, 1, 2),
        gate,
        up,
        jnp.swapaxes(down, 1, 2),
        gains_own,
    )


def solution(mesh):
    return jax.shard_map(
        body,
        mesh=mesh,
        in_specs=(
            P(("dp", "tensor"), None),
            P(None, "dp", "tensor"),
            P(None, "dp", "tensor"),
            P(None, "dp", "tensor"),
            P(None, "tensor", "dp"),
            P(None, "dp", "tensor"),
            P(None, "dp", "tensor"),
            P(None, "tensor", "dp"),
            P(None, None, "dp"),
            P(("dp", "tensor"), None),
        ),
        out_specs=(
            P(("dp", "tensor"), None),
            P(("dp", "tensor"), None),
            P(None, "dp", "tensor"),
            P(None, "dp", "tensor"),
            P(None, "dp", "tensor"),
            P(None, "tensor", "dp"),
            P(None, "dp", "tensor"),
            P(None, "dp", "tensor"),
            P(None, "tensor", "dp"),
            P(None, None, "dp"),
        ),
        check_vma=False,
    )
```

```python
import math

import jax
import jax.numpy as jnp
from jax import lax
from jax.experimental import pallas as pl
from jax.experimental.pallas import tpu as pltpu
from jax.sharding import PartitionSpec as P

HD = 96
MESH_IDS = pl.DeviceIdType.MESH
SIDE = 4
MODEL = 1536
SEQ_ROWS = 512
OWN = 128
QKV = (0, 768)
OUT = (768, 1152)
GATE = (1152, 2176)
UP = (2176, 3200)
DOWN = (3200, 4224)
COLS = (384, 192, 192, 384, 1024, 1024, 1024)
WIDTH = 4224
ATTN_PARTS = (((0, 256), (256, 512)), ((512, 768), (768, 1152)))
GU_PARTS = (((1152, 1664), (1664, 2176)), ((2176, 2688), (2688, 3200)))
DOWN_PARTS = (((3200, 3456), (3456, 3712)), ((3712, 3968), (3968, 4224)))

norm_eps = 1e-05
rope_base = 100000.0
SCALING = 1.0 / math.sqrt(HD)


def cut(cols):
    return pl.ds(cols[0], cols[1] - cols[0])


def shift(place, step):
    return lax.rem(place + step + 2 * SIDE, SIDE)


class Place:
    def __init__(self):
        dp = lax.axis_index("dp")
        tensor = lax.axis_index("tensor")
        self.z_hi, self.x, self.y = dp // 16, (dp // 4) % 4, dp % 4
        self.z_lo, self.core = tensor // 2, tensor % 2
        self.dp, self.tensor = dp, tensor

    def device(self, z_hi, x, y, tensor):
        return (z_hi * 16 + x * 4 + y, tensor)

    def beside(self, axis, step):
        if axis == "x":
            return self.device(self.z_hi, shift(self.x, step), self.y, self.tensor)
        return self.device(self.z_hi, self.x, shift(self.y, step), self.tensor)

    def across(self):
        return self.device(1 - self.z_hi, self.x, self.y, self.tensor)

    def twin(self):
        return (self.dp, self.z_lo * 2 + 1 - self.core)

    def above(self):
        return (self.dp, (1 - self.z_lo) * 2 + self.core)

    def greet(self):
        targets = [self.beside(axis, step) for axis in ("x", "y") for step in (1, 2, 3)]
        targets += [self.across(), self.twin(), self.above()]
        barrier = pltpu.get_barrier_semaphore()
        for target in targets:
            pl.semaphore_signal(barrier, inc=1, device_id=target, device_id_type=MESH_IDS)
        pl.semaphore_wait(barrier, len(targets))


class Wire:
    def __init__(self, send_sems, recv_sems):
        self.send_sems, self.recv_sems = send_sems, recv_sems
        self.count = 0
        self.sent = []

    def slot(self):
        self.count += 1
        return self.count - 1

    def send(self, slot, source, target_ref, target):
        copy = pltpu.make_async_remote_copy(
            src_ref=source,
            dst_ref=target_ref,
            send_sem=self.send_sems.at[slot],
            recv_sem=self.recv_sems.at[slot],
            device_id=target,
            device_id_type=MESH_IDS,
        )
        copy.start()
        self.sent.append(copy)
        return copy

    def arrive(self, slot, landed, target):
        pltpu.make_async_remote_copy(
            src_ref=landed,
            dst_ref=landed,
            send_sem=self.send_sems.at[slot],
            recv_sem=self.recv_sems.at[slot],
            device_id=target,
            device_id_type=MESH_IDS,
        ).wait_recv()

    def release(self, copy):
        copy.wait_send()
        self.sent = [other for other in self.sent if other is not copy]

    def drain(self):
        for copy in self.sent:
            copy.wait_send()
        self.sent = []


class Local:
    def __init__(self, sems):
        self.sems, self.count, self.open = sems, 0, []

    def start(self, source, target):
        copy = pltpu.make_async_copy(source, target, self.sems.at[self.count])
        self.count += 1
        copy.start()
        self.open.append(copy)
        return copy

    def wait(self, copy):
        copy.wait()
        self.open = [other for other in self.open if other is not copy]

    def drain(self):
        for copy in self.open:
            copy.wait()
        self.open = []


def sum_small(wire, at, value_ref, landing, whole_group):
    rounds = []
    if whole_group:
        rounds += [[at.twin()], [at.above()]]
    rounds += [[at.across()]]
    rounds += [[at.beside(axis, step) for step in (1, 2, 3)] for axis in ("y", "x")]
    place = 0
    for targets in rounds:
        slots = [wire.slot() for _ in targets]
        copies = []
        for index, target in enumerate(targets):
            copies.append(wire.send(slots[index], value_ref, landing.at[place + index], target))
        yield
        total = value_ref[...]
        for index, target in enumerate(targets):
            wire.arrive(slots[index], landing.at[place + index], target)
            total = total + landing[place + index]
        for copy in copies:
            wire.release(copy)
        value_ref[...] = total
        place += len(targets)
    yield


PIECES = 2
PIECE = OWN // PIECES


class Spread:
    def __init__(self, wire, at, rows_ref):
        self.wire, self.at, self.rows_ref = wire, at, rows_ref
        self.near = [wire.slot() for _ in range(PIECES)]
        self.over = [wire.slot() for _ in range(PIECES)]
        self.passed = [wire.slot() for _ in range(PIECES)]
        self.copies = []

    def rows(self, tensor, piece):
        start = pl.multiple_of(tensor * OWN + piece * PIECE, PIECE)
        return self.rows_ref.at[pl.ds(start, PIECE)]

    def send(self, piece):
        at, wire = self.at, self.wire
        block = self.rows(at.tensor, piece)
        self.copies.append(wire.send(self.over[piece], block, block, at.above()))
        self.copies.append(wire.send(self.near[piece], block, block, at.twin()))

    def near_done(self):
        at = self.at
        for piece in range(PIECES):
            block = self.rows(at.z_lo * 2 + 1 - at.core, piece)
            self.wire.arrive(self.near[piece], block, at.twin())

    def pass_on(self, piece):
        at, wire = self.at, self.wire
        block = self.rows((1 - at.z_lo) * 2 + at.core, piece)
        wire.arrive(self.over[piece], block, at.above())
        self.copies.append(wire.send(self.passed[piece], block, block, at.twin()))

    def far_done(self, piece):
        at = self.at
        block = self.rows((1 - at.z_lo) * 2 + 1 - at.core, piece)
        self.wire.arrive(self.passed[piece], block, at.twin())
        if piece == PIECES - 1:
            for copy in self.copies:
                self.wire.release(copy)


class Collect:
    def __init__(self, wire, at, part, help_ref, near_ref, over_ref):
        self.wire, self.at, self.part = wire, at, part
        self.help_ref, self.near_ref, self.over_ref = help_ref, near_ref, over_ref
        self.help = [wire.slot() for _ in range(PIECES)]
        self.near = wire.slot()
        self.over = [wire.slot() for _ in range(PIECES)]
        self.copies = []

    def rows(self, z_lo, core, piece):
        start = (z_lo * 2 + core) * OWN + piece * PIECE
        return pl.ds(pl.multiple_of(start, PIECE), PIECE)

    def other_ready(self, piece):
        at = self.at
        block = self.part.at[self.rows(1 - at.z_lo, 1 - at.core, piece)]
        landing = self.help_ref.at[pl.ds(piece * PIECE, PIECE)]
        self.copies.append(self.wire.send(self.help[piece], block, landing, at.twin()))

    def own_ready(self):
        at = self.at
        start = pl.multiple_of((at.z_lo * 2 + 1 - at.core) * OWN, OWN)
        block = self.part.at[pl.ds(start, OWN)]
        self.copies.append(self.wire.send(self.near, block, self.near_ref, at.twin()))

    def send_over(self, piece):
        at = self.at
        window = pl.ds(piece * PIECE, PIECE)
        self.wire.arrive(self.help[piece], self.help_ref.at[window], at.twin())
        rows = self.rows(1 - at.z_lo, at.core, piece)
        total = self.part[rows, :].astype(jnp.float32) + self.help_ref[window, :].astype(
            jnp.float32
        )
        self.part[rows, :] = total.astype(jnp.bfloat16)
        self.copies.append(
            self.wire.send(
                self.over[piece], self.part.at[rows], self.over_ref.at[window], at.above()
            )
        )

    def result(self, piece):
        at = self.at
        window = pl.ds(piece * PIECE, PIECE)
        if piece == 0:
            self.wire.arrive(self.near, self.near_ref, at.twin())
        total = self.part[self.rows(at.z_lo, at.core, piece), :].astype(
            jnp.float32
        ) + self.near_ref[window, :].astype(jnp.float32)
        self.wire.arrive(self.over[piece], self.over_ref.at[window], at.above())
        total = total + self.over_ref[window, :].astype(jnp.float32)
        if piece == PIECES - 1:
            for copy in self.copies:
                self.wire.release(copy)
        return total


def here_rows(at):
    return ((at.z_lo * 2 * OWN, 2 * OWN),)


def there_rows(at, piece):
    start = (1 - at.z_lo) * 2 * OWN + piece * PIECE
    return ((start, PIECE), (start + OWN, PIECE))


def windows(rows):
    return [pl.ds(pl.multiple_of(start, size), size) for start, size in rows]


def take(ref, rows, cols=slice(None)):
    pieces = [ref[window, cols] for window in windows(rows)]
    return pieces[0] if len(pieces) == 1 else jnp.concatenate(pieces, axis=0)


def put(ref, rows, cols, value):
    place = 0
    for window, (_, size) in zip(windows(rows), rows):
        ref[window, cols] = value[place : place + size]
        place += size


def nn(left, right):
    return jnp.dot(left, right, preferred_element_type=jnp.float32)


def nt(left, right):
    return lax.dot_general(
        left, right, (((1,), (1,)), ((), ())), preferred_element_type=jnp.float32
    )


def tn(left, right):
    return lax.dot_general(
        left, right, (((0,), (0,)), ((), ())), preferred_element_type=jnp.float32
    )


def rope_tables(heads):
    half = HD // 2
    position = jnp.arange(SEQ_ROWS, dtype=jnp.float32)[:, None]
    exponent = 2.0 * jnp.arange(half, dtype=jnp.float32) / HD
    angles = position * (rope_base ** (-exponent))[None, :]
    cosine, sine = jnp.cos(angles), jnp.sin(angles)
    wide_cosine = jnp.concatenate([cosine, cosine], axis=1)
    wide_sine = jnp.concatenate([-sine, sine], axis=1)
    return jnp.tile(wide_cosine, (1, heads)), jnp.tile(wide_sine, (1, heads))


def swap_halves(values):
    width = values.shape[1]
    lane = lax.broadcasted_iota(jnp.int32, values.shape, 1)
    first = lax.rem(lane, HD) < HD // 2
    return jnp.where(
        first, pltpu.roll(values, width - HD // 2, 1), pltpu.roll(values, HD // 2, 1)
    )


def head_of(values, start):
    width = values.shape[1]
    moved = values if start == 0 else pltpu.roll(values, width - start, 1)
    moved = moved[:, :128]
    lane = lax.broadcasted_iota(jnp.int32, moved.shape, 1)
    return jnp.where(lane < HD, moved, 0.0)


def side_by_side(heads):
    tiles = []
    for tile in range(len(heads) * HD // 128):
        total = None
        lane = lax.broadcasted_iota(jnp.int32, heads[0].shape, 1)
        for index, head in enumerate(heads):
            start = index * HD - tile * 128
            if start <= -HD or start >= 128:
                continue
            moved = pltpu.roll(head, start % 128, 1) if start else head
            if start > 0 or start < 0:
                keep = (lane >= start) if start > 0 else (lane < start + HD)
                moved = jnp.where(keep, moved, 0.0)
            total = moved if total is None else total + moved
        tiles.append(total)
    return jnp.concatenate(tiles, axis=1)


def weight(w_ref, layer, cols):
    value = w_ref[layer, :, :, cols]
    return value.reshape(MODEL, value.shape[-1])


def turn_rows(source, target):
    def tile(index, carry):
        start = pl.multiple_of(index * 256, 256)
        target[pl.ds(start, 256), :] = source[:, pl.ds(start, 256)].T
        return carry

    lax.fori_loop(0, MODEL // 256, tile, 0)


def gather_job(wire, at, full, layer, group):
    parts = []
    for (first, second), (left, right) in zip((("y", "x"), ("x", "y")), group):

        def block(first_step, second_step, cols, first=first):
            x_step, y_step = (
                (first_step, second_step) if first == "x" else (second_step, first_step)
            )
            row = shift(at.x, x_step) * 192 + shift(at.y, y_step) * 48
            return full.at[layer, :, pl.ds(pl.multiple_of(row, 48), 48), cut(cols)]

        parts.append(
            dict(
                first=first,
                second=second,
                left=left,
                right=right,
                whole=(left[0], right[1]),
                block=block,
                one={s: wire.slot() for s in (1, -1)},
                two={s: wire.slot() for s in (1, -1)},
                side={(f, s): wire.slot() for f in (0, -1, 1, 2) for s in (1, -1)},
                far={(f, s): wire.slot() for f in (0, -1, 1, 2) for s in (1, -1)},
            )
        )

    def half(part, step):
        return part["left"] if step == 1 else part["right"]

    def one_start(part, step):
        piece = part["block"](0, 0, part["whole"])
        wire.send(part["one"][step], piece, piece, at.beside(part["first"], step))

    def side_start(part, first_step):
        for step in (1, -1):
            piece = part["block"](first_step, 0, part["whole"])
            wire.send(
                part["side"][first_step, step], piece, piece, at.beside(part["second"], step)
            )

    def one_done(part, step):
        target = at.beside(part["first"], step)
        wire.arrive(part["one"][step], part["block"](-step, 0, part["whole"]), target)
        piece = part["block"](-step, 0, half(part, step))
        wire.send(part["two"][step], piece, piece, target)

    def two_done(part):
        for step in (1, -1):
            piece = part["block"](2, 0, half(part, step))
            wire.arrive(part["two"][step], piece, at.beside(part["first"], step))

    def side_done(part, first_step):
        for step in (1, -1):
            target = at.beside(part["second"], step)
            landed = part["block"](first_step, -step, part["whole"])
            wire.arrive(part["side"][first_step, step], landed, target)
            piece = part["block"](first_step, -step, half(part, step))
            wire.send(part["far"][first_step, step], piece, piece, target)

    def far_done(part, first_step):
        for step in (1, -1):
            piece = part["block"](first_step, 2, half(part, step))
            wire.arrive(part["far"][first_step, step], piece, at.beside(part["second"], step))

    for part in parts:
        for step in (1, -1):
            one_start(part, step)
    for part in parts:
        side_start(part, 0)
    yield
    for step in (1, -1):
        for part in parts:
            one_done(part, step)
    for first_step in (-1, 1):
        for part in parts:
            side_start(part, first_step)
    yield
    for part in parts:
        two_done(part)
    for part in parts:
        side_start(part, 2)
    for part in parts:
        side_done(part, 0)
    yield
    for first_step in (-1, 1):
        for part in parts:
            side_done(part, first_step)
    yield
    for part in parts:
        side_done(part, 2)
    yield
    for first_step in (0, -1, 1, 2):
        for part in parts:
            far_done(part, first_step)
    yield


STEPS = (1, 2, 1, 2)
LAG = 2


class Gather:
    def __init__(self, wire, local, at, shard, full, kept):
        self.wire, self.local, self.at, self.shard = wire, local, at, shard
        self.full, self.kept = full, kept
        self.groups = [
            (layer, group)
            for layer in range(2)
            for group in (ATTN_PARTS, GU_PARTS, DOWN_PARTS)
        ]
        self.jobs = [gather_job(wire, at, full, *pair) for pair in self.groups]
        self.slots = [wire.slot() for _ in self.groups]
        self.own = []
        count = len(self.jobs)
        self.order = [
            (index, turn - LAG * index)
            for turn in range(LAG * count + 6)
            for index in range(count)
            if 0 <= turn - LAG * index < 6
        ]
        self.done = 0

    def columns(self, index):
        group = self.groups[index][1]
        return cut((group[0][0][0], group[1][1][1]))

    def mine(self, z_hi):
        row = self.at.x * 192 + self.at.y * 48
        return (z_hi, pl.ds(pl.multiple_of(row, 48), 48))

    def begin(self):
        at = self.at
        z_own, rows = self.mine(at.z_hi)
        for index, (layer, _) in enumerate(self.groups):
            cols = self.columns(index)
            source = self.shard.at[layer, :, cols]
            target = self.full.at[layer, z_own, rows, cols]
            self.wire.send(self.slots[index], source, target, at.across())
            self.own.append(self.local.start(source, target))

    def step(self, count=1):
        for _ in range(count):
            if self.done == len(self.order):
                return
            index, stage = self.order[self.done]
            self.done += 1
            layer = self.groups[index][0]
            cols = self.columns(index)
            if stage == 0:
                self.local.wait(self.own[index])
                z_other, rows = self.mine(1 - self.at.z_hi)
                landed = self.full.at[layer, z_other, rows, cols]
                self.wire.arrive(self.slots[index], landed, self.at.across())
            next(self.jobs[index])
            if stage == 5:
                self.local.start(
                    self.full.at[layer, :, :, cols], self.kept.at[layer, :, :, cols]
                )

    def until(self, index):
        while (index, 5) in self.order[self.done :]:
            self.step()


def normed(rows_in, gain):
    inverse = lax.rsqrt(jnp.mean(rows_in * rows_in, axis=-1, keepdims=True) + norm_eps)
    return (rows_in * inverse * gain).astype(jnp.bfloat16)


def project_heads(layer, rows, n1, w, cosine, sine, q_ref, k_ref, v_ref):
    left = take(n1.at[layer], rows)
    cosine_rows, sine_rows = take(cosine, rows), take(sine, rows)
    every = slice(None)
    query = nn(left, weight(w, layer, pl.ds(0, 384)))
    turned = query * cosine_rows + swap_halves(query) * sine_rows
    for head in range(4):
        put(q_ref.at[layer, head], rows, every, head_of(turned, head * HD).astype(jnp.bfloat16))
    both = nn(left, weight(w, layer, pl.ds(384, 384)))
    turned = both * cosine_rows + swap_halves(both) * sine_rows
    for head in range(2):
        put(k_ref.at[layer, head], rows, every, head_of(turned, head * HD).astype(jnp.bfloat16))
        value = head_of(both, 192 + head * HD).astype(jnp.bfloat16)
        put(v_ref.at[layer, head], rows, every, value)


def attend(layer, blocks, q_ref, k_ref, v_ref, p_ref, o_ref):
    for block in blocks:
        rows = pl.ds(block * 128, 128)
        keys = (block + 1) * 128
        outputs = []
        for head in range(2):
            pair = jnp.concatenate(
                [q_ref[layer, 2 * head, rows, :], q_ref[layer, 2 * head + 1, rows, :]], axis=0
            )
            scores = nt(pair, k_ref[layer, head, pl.ds(0, keys), :]) * SCALING
            row = lax.broadcasted_iota(jnp.int32, (256, keys), 0) % 128 + block * 128
            key = lax.broadcasted_iota(jnp.int32, (256, keys), 1)
            scores = jnp.where(row >= key, scores, -1e30)
            peak = jnp.max(scores, axis=-1, keepdims=True)
            exponent = jnp.exp(scores - peak)
            inverse = 1.0 / jnp.sum(exponent, axis=-1, keepdims=True)
            shares = (exponent * inverse).astype(jnp.bfloat16)
            p_ref[layer, 2 * head, rows, pl.ds(0, keys)] = shares[:128]
            p_ref[layer, 2 * head + 1, rows, pl.ds(0, keys)] = shares[128:]
            out = nn(shares, v_ref[layer, head, pl.ds(0, keys), :])
            outputs += [out[:128], out[128:]]
        o_ref[layer, rows, :] = side_by_side(outputs).astype(jnp.bfloat16)


def rows_partial(layer, rows, left_ref, w, cols, part):
    left = take(left_ref, rows)
    for half in range(2):

        def tile(index, carry, half=half):
            start = pl.multiple_of(index * 256, 256)
            right = w[layer, half, pl.ds(start, 256), cut(cols)]
            column = pl.ds(pl.multiple_of(half * 768 + start, 256), 256)
            put(part, rows, column, nt(left, right).astype(jnp.bfloat16))
            return carry

        lax.fori_loop(0, 3, tile, 0)


def hidden_rows(layer, rows, n2, w, g_ref, u_ref, a_ref):
    left = take(n2.at[layer], rows)

    def tile(index, carry):
        start = pl.multiple_of(index * 256, 256)
        column = pl.ds(start, 256)
        gate = nn(left, weight(w, layer, pl.ds(GATE[0] + start, 256)))
        up = nn(left, weight(w, layer, pl.ds(UP[0] + start, 256)))
        hidden = gate * up / (1.0 + jnp.exp(-gate))
        put(g_ref.at[layer], rows, column, gate.astype(g_ref.dtype))
        put(u_ref.at[layer], rows, column, up.astype(u_ref.dtype))
        put(a_ref.at[layer], rows, column, hidden.astype(jnp.bfloat16))
        return carry

    lax.fori_loop(0, 4, tile, 0)


def forward_kernel(
    shard,
    gains_placed,
    tokens,
    grad_out,
    cosine_kept,
    sine_kept,
    w_kept,
    gains,
    dm_kept,
    dm_turned_kept,
    n1_kept,
    n2_kept,
    q_kept,
    k_kept,
    v_kept,
    p_kept,
    o_kept,
    g_kept,
    u_kept,
    a_kept,
    x_kept,
    h_kept,
    cosine,
    sine,
    w,
    n1,
    n2,
    q_ref,
    k_ref,
    v_ref,
    p_ref,
    o_ref,
    g_ref,
    u_ref,
    a_ref,
    x_ref,
    h_ref,
    dm,
    n1_turned,
    n2_turned,
    part,
    help_ref,
    near_ref,
    over_ref,
    gains_landing,
    send_sems,
    recv_sems,
    local_sems,
):
    at = Place()
    at.greet()
    wire = Wire(send_sems, recv_sems)
    local = Local(local_sems)
    gather = Gather(wire, local, at, shard, w, w_kept)
    gather.begin()
    tables = [local.start(cosine_kept, cosine), local.start(sine_kept, sine)]
    gather.step()
    gains[...] = gains_placed[...]
    rounds = sum_small(wire, at, gains, gains_landing, False)
    for _ in rounds:
        gather.step()
    turn = 0

    def collector():
        nonlocal turn
        turn += 1
        slot = turn % 2
        return Collect(
            wire, at, part, help_ref.at[slot], near_ref.at[slot], over_ref.at[slot]
        )

    def own(piece):
        return pl.ds(pl.multiple_of(at.tensor * OWN + piece * PIECE, PIECE), PIECE)

    def window(piece):
        return pl.ds(piece * PIECE, PIECE)

    here = here_rows(at)
    turning = [None, None]
    spread = Spread(wire, at, n1.at[0])
    for piece in range(PIECES):
        x_rows = tokens[window(piece), :].astype(jnp.float32)
        x_ref[0, window(piece), :] = x_rows
        n1[0, own(piece), :] = normed(x_rows, gains[pl.ds(0, 1), :])
        spread.send(piece)
    for layer in range(2):
        heads = (n1, w, cosine, sine, q_ref, k_ref, v_ref)
        spread.near_done()
        gather.until(3 * layer)
        while tables:
            local.wait(tables.pop())
        project_heads(layer, here, *heads)
        gather.step(STEPS[0])
        spread.pass_on(0)
        spread.far_done(0)
        project_heads(layer, there_rows(at, 0), *heads)
        spread.pass_on(1)
        spread.far_done(1)
        project_heads(layer, there_rows(at, 1), *heads)
        for source, target in ((q_ref, q_kept), (k_ref, k_kept), (v_ref, v_kept)):
            local.start(source.at[layer], target.at[layer])
        collect = collector()
        around = (q_ref, k_ref, v_ref, p_ref, o_ref)

        def blocks(first, second, layer=layer, around=around):
            @pl.when(at.z_lo == 0)
            def _():
                attend(layer, first, *around)

            @pl.when(at.z_lo == 1)
            def _():
                attend(layer, second, *around)

        blocks((2, 3), (0, 1))
        for piece in range(PIECES):
            rows_partial(layer, there_rows(at, piece), o_ref.at[layer], w, OUT, part)
            collect.other_ready(piece)
        collect.send_over(0)
        collect.send_over(1)
        blocks((0, 1), (2, 3))
        rows_partial(layer, here, o_ref.at[layer], w, OUT, part)
        collect.own_ready()
        for source, target in ((p_ref, p_kept), (o_ref, o_kept)):
            local.start(source.at[layer], target.at[layer])
        gather.step(STEPS[1])
        spread = Spread(wire, at, n2.at[layer])
        for piece in range(PIECES):
            h_rows = x_ref[layer, window(piece), :] + collect.result(piece)
            h_ref[layer, window(piece), :] = h_rows
            n2[layer, own(piece), :] = normed(h_rows, gains[pl.ds(2 * layer + 1, 1), :])
            spread.send(piece)
        if layer == 1:
            spread_back = Spread(wire, at, dm)
            for piece in range(PIECES):
                dm[own(piece), :] = grad_out[window(piece), :]
                spread_back.send(piece)
        if layer == 1:
            local.wait(turning[0])
        turn_rows(n1.at[layer], n1_turned)
        turning[0] = local.start(n1_turned, n1_kept.at[layer])
        spread.near_done()
        gather.until(3 * layer + 1)
        mlp = (n2, w, g_ref, u_ref, a_ref)
        hidden_rows(layer, here, *mlp)
        gather.step(STEPS[2])
        if layer == 1:
            spread.pass_on(0)
            spread_back.pass_on(0)
            spread.far_done(0)
            hidden_rows(layer, there_rows(at, 0), *mlp)
            gather.step()
            spread.pass_on(1)
            spread_back.pass_on(1)
            spread.far_done(1)
            hidden_rows(layer, there_rows(at, 1), *mlp)
            gather.step()
            spread_back.near_done()
            spread_back.far_done(0)
            spread_back.far_done(1)
        else:
            spread.pass_on(0)
            spread.far_done(0)
            hidden_rows(layer, there_rows(at, 0), *mlp)
            spread.pass_on(1)
            spread.far_done(1)
            hidden_rows(layer, there_rows(at, 1), *mlp)
            gather.until(2)
            collect = collector()
            for piece in range(PIECES):
                rows_partial(layer, there_rows(at, piece), a_ref.at[layer], w, DOWN, part)
                collect.other_ready(piece)
            collect.send_over(0)
            rows_partial(layer, here, a_ref.at[layer], w, DOWN, part)
            collect.own_ready()
            collect.send_over(1)
        for source, target in (
            (h_ref, h_kept),
            (g_ref, g_kept),
            (u_ref, u_kept),
            (a_ref, a_kept),
        ):
            local.start(source.at[layer], target.at[layer])
        if layer == 1:
            local.wait(turning[1])
        turn_rows(n2.at[layer], n2_turned)
        turning[1] = local.start(n2_turned, n2_kept.at[layer])
        gather.step(STEPS[3])
        if layer == 1:
            local.start(dm, dm_kept)
            local.wait(turning[0])
            turn_rows(dm, n1_turned)
            local.start(n1_turned, dm_turned_kept)
            break
        spread = Spread(wire, at, n1.at[1])
        for piece in range(PIECES):
            total = h_ref[layer, window(piece), :] + collect.result(piece)
            x_ref[1, window(piece), :] = total
            n1[1, own(piece), :] = normed(total, gains[pl.ds(2, 1), :])
            spread.send(piece)
        local.start(x_ref.at[1], x_kept)
    gather.until(5)
    local.drain()
    wire.drain()


KEEP = jnp.bfloat16


def run_forward(shard, gains_placed, tokens, grad_out, cosine, sine):
    def kept(*shape, kind=jnp.bfloat16):
        return jax.ShapeDtypeStruct(shape, kind)

    def held(*shape, kind=jnp.bfloat16):
        return pltpu.VMEM(shape, kind)

    vmem = pl.BlockSpec(memory_space=pltpu.VMEM)
    hbm = pl.BlockSpec(memory_space=pl.ANY)
    float32 = jnp.float32
    wires = 6 * 41 + 7 + 5 * 6 + 3 * 5
    return pl.pallas_call(
        forward_kernel,
        out_shape=(
            kept(2, 2, 768, WIDTH),
            kept(8, MODEL, kind=float32),
            kept(SEQ_ROWS, MODEL),
            kept(MODEL, SEQ_ROWS),
            kept(2, MODEL, SEQ_ROWS),
            kept(2, MODEL, SEQ_ROWS),
            kept(2, 4, SEQ_ROWS, 128),
            kept(2, 2, SEQ_ROWS, 128),
            kept(2, 2, SEQ_ROWS, 128),
            kept(2, 4, SEQ_ROWS, SEQ_ROWS),
            kept(2, SEQ_ROWS, 384),
            kept(2, SEQ_ROWS, 1024, kind=KEEP),
            kept(2, SEQ_ROWS, 1024, kind=KEEP),
            kept(2, SEQ_ROWS, 1024),
            kept(OWN, MODEL, kind=float32),
            kept(2, OWN, MODEL, kind=float32),
        ),
        in_specs=[hbm] + [vmem] * 3 + [hbm] * 2,
        out_specs=(hbm, vmem) + (hbm,) * 14,
        scratch_shapes=[
            held(SEQ_ROWS, 384, kind=float32),
            held(SEQ_ROWS, 384, kind=float32),
            held(2, 2, 768, WIDTH),
            held(2, SEQ_ROWS, MODEL),
            held(2, SEQ_ROWS, MODEL),
            held(2, 4, SEQ_ROWS, 128),
            held(2, 2, SEQ_ROWS, 128),
            held(2, 2, SEQ_ROWS, 128),
            held(2, 4, SEQ_ROWS, SEQ_ROWS),
            held(2, SEQ_ROWS, 384),
            held(2, SEQ_ROWS, 1024, kind=KEEP),
            held(2, SEQ_ROWS, 1024, kind=KEEP),
            held(2, SEQ_ROWS, 1024),
            held(2, OWN, MODEL, kind=float32),
            held(2, OWN, MODEL, kind=float32),
            held(SEQ_ROWS, MODEL),
            held(MODEL, SEQ_ROWS),
            held(MODEL, SEQ_ROWS),
            held(SEQ_ROWS, MODEL),
            held(2, OWN, MODEL),
            held(2, OWN, MODEL),
            held(2, OWN, MODEL),
            held(7, 8, MODEL, kind=float32),
            pltpu.SemaphoreType.DMA((wires,)),
            pltpu.SemaphoreType.DMA((wires,)),
            pltpu.SemaphoreType.DMA((48,)),
        ],
        compiler_params=pltpu.CompilerParams(
            collective_id=0, has_side_effects=True, vmem_limit_bytes=62 * 2**20
        ),
        name="forward",
    )(shard, gains_placed, tokens, grad_out, cosine, sine)


JOBS = (
    (((3200, 3456), (3456, 3712)), ((3712, 3968), (3968, 4224))),
    (((1152, 1408), (1408, 1664)), ((1664, 1920), (1920, 2176))),
    (((2176, 2432), (2432, 2688)), ((2688, 2944), (2944, 3200))),
    (((0, 256), (256, 512)), ((512, 768), (768, 1152))),
)
JOB_WIDTH = 1152
SETS = 3
LAG_BACK = 2


def add_rows(target, terms):
    lead = target.shape[:-2]

    def step(index, carry):
        window = ()
        if lead:
            window = (index // lead[1], index % lead[1])
        total = None
        for term in terms:
            value = term[window + (slice(None), slice(None))].astype(jnp.float32)
            total = value if total is None else total + value
        target[window + (slice(None), slice(None))] = total.astype(target.dtype)
        return carry

    lax.fori_loop(0, math.prod(lead), step, 0)


def scatter_job(wire, local, at, grads, layer, group, bufs, finish):
    one, two_up, two_down, small_one, small_up, small_down, near_side, near_own = bufs
    base = group[0][0][0]
    parts = []
    for (first, second), (left, right) in zip((("y", "x"), ("x", "y")), group):

        def region(step, cols, second=second):
            if second == "x":
                return grads.at[layer, :, shift(at.x, step), :, :, cut(cols)]
            return grads.at[layer, :, :, shift(at.y, step), :, cut(cols)]

        def mine(step, cols, first=first):
            place = at.y if first == "y" else at.x
            return two_up.at[:, shift(place, step), :, inside(cols)]

        parts.append(
            dict(
                first=first,
                second=second,
                left=left,
                right=right,
                whole=(left[0], right[1]),
                region=region,
                mine=mine,
                **{
                    name: {s: wire.slot() for s in (1, -1)}
                    for name in ("far", "raw", "sum", "far2", "raw2", "sum2")
                },
            )
        )

    def inside(cols):
        return pl.ds(cols[0] - base, cols[1] - cols[0])

    def half(part, step):
        return part["left"] if step == 1 else part["right"]

    def other(part, step):
        return part["right"] if step == 1 else part["left"]

    def big(ref, cols):
        return ref.at[:, :, :, inside(cols)]

    def small(ref, cols):
        return ref.at[:, :, inside(cols)]

    copies = []
    near = {}
    for part in parts:
        for step in (1, -1):
            cols = half(part, step)
            target = at.beside(part["second"], step)
            copies.append(
                wire.send(part["far"][step], part["region"](2, cols), big(one, cols), target)
            )
    for number, part in enumerate(parts):
        for step in (1, -1):
            cols = other(part, step)
            landing = two_up if step == 1 else two_down
            target = at.beside(part["second"], step)
            copies.append(
                wire.send(part["raw"][step], part["region"](step, cols), big(landing, cols), target)
            )
            cols = half(part, step)
            near[number, step] = local.start(part["region"](step, cols), big(near_side, cols))
    yield
    for number, part in enumerate(parts):
        cols = part["whole"]
        near[number, 0] = local.start(part["region"](0, cols), big(near_own, cols))
    for step in (1, -1):
        for number, part in enumerate(parts):
            cols = half(part, step)
            target = at.beside(part["second"], step)
            piece = big(one, cols)
            local.wait(near[number, step])
            wire.arrive(part["far"][step], piece, target)
            add_rows(piece, (piece, big(near_side, cols)))
            landing = two_up if step == 1 else two_down
            copies.append(wire.send(part["sum"][step], piece, big(landing, cols), target))
    yield
    for number, part in enumerate(parts):
        local.wait(near[number, 0])
        for step in (1, -1):
            target = at.beside(part["second"], step)
            landing = two_up if step == 1 else two_down
            for name, cols in (("raw", other(part, step)), ("sum", half(part, step))):
                wire.arrive(part[name][step], big(landing, cols), target)
        cols = part["whole"]
        add_rows(big(two_up, cols), (big(near_own, cols), big(two_up, cols), big(two_down, cols)))
        for step in (1, -1):
            target = at.beside(part["first"], step)
            cols = half(part, step)
            copies.append(
                wire.send(part["far2"][step], part["mine"](2, cols), small(small_one, cols), target)
            )
            cols = other(part, step)
            landing = small_up if step == 1 else small_down
            copies.append(
                wire.send(part["raw2"][step], part["mine"](step, cols), small(landing, cols), target)
            )
    yield
    for step in (1, -1):
        for part in parts:
            cols = half(part, step)
            target = at.beside(part["first"], step)
            piece = small(small_one, cols)
            wire.arrive(part["far2"][step], piece, target)
            own = part["mine"](step, cols)
            for z_hi in range(2):
                add_rows(piece.at[z_hi], (piece.at[z_hi], own.at[z_hi]))
            landing = small_up if step == 1 else small_down
            copies.append(wire.send(part["sum2"][step], piece, small(landing, cols), target))
    yield
    for part in parts:
        for step in (1, -1):
            target = at.beside(part["first"], step)
            landing = small_up if step == 1 else small_down
            for name, cols in (("raw2", other(part, step)), ("sum2", half(part, step))):
                wire.arrive(part[name][step], small(landing, cols), target)
        cols = part["whole"]
        finish(
            cols,
            [
                [
                    ref.at[z_hi]
                    for ref in (part["mine"](0, cols), small(small_up, cols), small(small_down, cols))
                ]
                for z_hi in (1 - at.z_hi, at.z_hi)
            ],
        )
    for copy in copies:
        wire.release(copy)
    yield


class Scatter:
    def __init__(self, wire, local, at, grads, summed, sets, leaving, landed, credits):
        self.wire, self.local, self.at, self.grads = wire, local, at, grads
        self.summed, self.leaving, self.landed, self.credits = summed, leaving, landed, credits
        self.groups = [(layer, group) for layer in (1, 0) for group in JOBS]
        self.last = []
        self.jobs = []
        for index, (layer, group) in enumerate(self.groups):
            bufs = tuple(ref.at[index % ref.shape[0]] for ref in sets)
            self.jobs.append(
                scatter_job(
                    wire, local, at, grads, layer, group, bufs, self.finisher(index, layer, group)
                )
            )
        count = len(self.jobs)
        self.order = [
            (index, turn - LAG_BACK * index)
            for turn in range(LAG_BACK * count + 6)
            for index in range(count)
            if 0 <= turn - LAG_BACK * index < 6
        ]
        self.done = 0
        self.ready = 0

    def finisher(self, index, layer, group):
        wire, at = self.wire, self.at
        base = group[0][0][0]

        def finish(cols, terms):
            theirs, own = terms
            window = pl.ds(cols[0] - base, cols[1] - cols[0])
            piece = self.leaving.at[index, :, window]
            add_rows(piece, theirs)
            slot = wire.slot()
            landing = self.landed.at[index, :, window]
            wire.send(slot, piece, landing, at.across())
            target = self.summed.at[layer, :, cut(cols)]
            add_rows(target, own)
            self.last.append((index, slot, landing, target))

        return finish

    def turn(self):
        if self.done < len(self.order):
            index, stage = self.order[self.done]
            now = LAG_BACK * index + stage
            while self.done < len(self.order):
                index, stage = self.order[self.done]
                if LAG_BACK * index + stage != now or index >= self.ready:
                    return
                self.step()

    def step(self, count=1):
        at = self.at
        for _ in range(count):
            if self.done == len(self.order):
                return
            index, stage = self.order[self.done]
            if index >= self.ready:
                return
            self.done += 1
            ways = [(axis, step) for axis in ("x", "y") for step in (1, -1)]
            if stage == 5:
                for job, slot, landing, target in self.last:
                    if job == index:
                        self.wire.arrive(slot, landing, at.across())
                        add_rows(target, (target, landing))
                continue
            if stage == 0 and index >= SETS:
                for number in range(4):
                    pl.semaphore_wait(self.credits.at[number], 1)
            next(self.jobs[index])
            if stage == 4 and index + SETS < len(self.jobs):
                for number, (axis, step) in enumerate(ways):
                    pl.semaphore_signal(
                        self.credits.at[number],
                        inc=1,
                        device_id=at.beside(axis, step),
                        device_id_type=MESH_IDS,
                    )


def norm_backward(rows_in, gain, grad_normed):
    inverse = lax.rsqrt(jnp.mean(rows_in * rows_in, axis=-1, keepdims=True) + norm_eps)
    scaled = rows_in * inverse
    grad_gain = jnp.sum(grad_normed * scaled, axis=0, keepdims=True)
    grad_scaled = grad_normed * gain
    grad_input = inverse * (
        grad_scaled - scaled * jnp.mean(grad_scaled * scaled, axis=-1, keepdims=True)
    )
    return grad_input, grad_gain


def hidden_back(rows, dm, w, g_ref, u_ref, dgu):
    left = take(dm, rows)

    def tile(index, carry):
        start = pl.multiple_of(index * 256, 256)
        column = pl.ds(start, 256)
        grad = nn(left, weight(w, 0, pl.ds(DOWN[0] + start, 256)))
        gate = take(g_ref, rows, column).astype(jnp.float32)
        up = take(u_ref, rows, column).astype(jnp.float32)
        sigma = 1.0 / (1.0 + jnp.exp(-gate))
        grad_gate = grad * up * sigma * (1.0 + gate * (1.0 - sigma))
        put(dgu, rows, column, grad_gate.astype(jnp.bfloat16))
        column = pl.ds(pl.multiple_of(1024 + start, 256), 256)
        put(dgu, rows, column, (grad * gate * sigma).astype(jnp.bfloat16))
        return carry

    lax.fori_loop(0, 4, tile, 0)


def attend_back(q_ref, k_ref, v_ref, p_ref, do_ref, dk_ref, dv_ref, cosine, sine, dqkv):
    dk_ref[...] = jnp.zeros_like(dk_ref)
    dv_ref[...] = jnp.zeros_like(dv_ref)
    for block in range(4):
        rows = pl.ds(block * 128, 128)
        keys = pl.ds(0, (block + 1) * 128)
        queries = []
        for head in range(2):
            both = (2 * head, 2 * head + 1)
            shares = jnp.concatenate([p_ref[h, rows, keys] for h in both], axis=0)
            pair = jnp.concatenate([q_ref[h, rows, :] for h in both], axis=0)
            grad = jnp.concatenate([do_ref[h, rows, :] for h in both], axis=0)
            wide = shares.astype(jnp.float32)
            grad_shares = nt(grad, v_ref[head, keys, :])
            inner = jnp.sum(grad_shares * wide, axis=-1, keepdims=True)
            grad_scores = (wide * (grad_shares - inner)).astype(jnp.bfloat16)
            grad_pair = nn(grad_scores, k_ref[head, keys, :]) * SCALING
            queries += [grad_pair[:128], grad_pair[128:]]
            dk_ref[head, :, keys] += nn(pair.T, grad_scores)
            dv_ref[head, :, keys] += nn(grad.T, shares)
        grad_rows = side_by_side(queries)
        turned = grad_rows * cosine[rows, :] - swap_halves(grad_rows) * sine[rows, :]
        dqkv[rows, pl.ds(0, 384)] = turned.astype(jnp.bfloat16)
    both = side_by_side(
        [dk_ref[0].T * SCALING, dk_ref[1].T * SCALING, dv_ref[0].T, dv_ref[1].T]
    )
    turned = both * cosine[...] - swap_halves(both) * sine[...]
    lane = lax.broadcasted_iota(jnp.int32, both.shape, 1)
    dqkv[:, pl.ds(384, 384)] = jnp.where(lane < 192, turned, both).astype(jnp.bfloat16)


def backward_kernel(
    gains,
    grad_out,
    tokens,
    cosine_kept,
    sine_kept,
    x_kept,
    h_kept,
    w_kept,
    dm_kept,
    dm_turned_kept,
    n1_kept,
    n2_kept,
    q_kept,
    k_kept,
    v_kept,
    p_kept,
    o_kept,
    g_kept,
    u_kept,
    a_kept,
    output,
    input_grad,
    summed,
    gains_grad,
    grads,
    cosine,
    sine,
    x_second,
    h_ref,
    w,
    n1_turned,
    n2_turned,
    q_ref,
    k_ref,
    v_ref,
    p_ref,
    o_ref,
    g_ref,
    u_ref,
    a_ref,
    dm,
    turned,
    dgu,
    do_ref,
    dk_ref,
    dv_ref,
    dqkv,
    dx,
    part,
    help_ref,
    near_ref,
    over_ref,
    staged,
    one,
    two_up,
    two_down,
    small_one,
    small_up,
    small_down,
    near_side,
    near_own,
    leaving,
    landed,
    gains_landing,
    send_sems,
    recv_sems,
    local_sems,
    credits,
):
    at = Place()
    at.greet()
    wire = Wire(send_sems, recv_sems)
    local = Local(local_sems)
    sets = (one, two_up, two_down, small_one, small_up, small_down, near_side, near_own)
    scatter = Scatter(wire, local, at, grads, summed, sets, leaving, landed, credits)
    turn = 0

    def collector():
        nonlocal turn
        turn += 1
        slot = turn % 2
        return Collect(
            wire, at, part, help_ref.at[slot], near_ref.at[slot], over_ref.at[slot]
        )

    loads = {}

    def load(layer, names):
        pairs = dict(
            n1=(n1_kept, n1_turned),
            n2=(n2_kept, n2_turned),
            q=(q_kept, q_ref),
            k=(k_kept, k_ref),
            v=(v_kept, v_ref),
            p=(p_kept, p_ref),
            o=(o_kept, o_ref),
            g=(g_kept, g_ref),
            u=(u_kept, u_ref),
            a=(a_kept, a_ref),
            dm=(dm_kept, dm.at[0]),
            turned=(dm_turned_kept, turned),
        )
        columns = dict(down=DOWN, gu=(GATE[0], UP[1]), out=OUT, qkv=QKV)
        for name in names:
            if name in columns:
                cols = cut(columns[name])
                loads[name] = local.start(w_kept.at[layer, :, :, cols], w.at[0, :, :, cols])
            else:
                kept, held = pairs[name]
                source = kept if name in ("dm", "turned") else kept.at[layer]
                loads[name] = local.start(source, held)

    def ready(*names):
        for name in names:
            local.wait(loads.pop(name))

    mlp_names = ("down", "g", "u", "gu", "a", "n2")
    attn_names = ("out", "v", "p", "k", "q", "qkv", "o", "n1")
    load(1, ("a", "down", "turned", "dm", "g", "u", "gu", "n2"))
    load(1, attn_names)
    tables = [
        local.start(*pair)
        for pair in (
            (h_kept, h_ref),
            (x_kept, x_second),
            (cosine_kept, cosine),
            (sine_kept, sine),
        )
    ]
    staging = [None, None]
    tiles = 0
    behind = []

    def keep_tile(layer, left, right_ref, start, size, column):
        nonlocal tiles
        slot = tiles % 2
        tiles += 1
        if staging[slot] is not None:
            local.wait(staging[slot])
        product = nn(left[...], right_ref[:, pl.ds(start, size)])
        staged[slot, :, :, :, :, pl.ds(0, size)] = product.astype(jnp.bfloat16).reshape(
            2, SIDE, SIDE, 48, size
        )
        staging[slot] = local.start(
            staged.at[slot, :, :, :, :, pl.ds(0, size)],
            grads.at[layer, :, :, :, :, pl.ds(column, size)],
        )

    def keep_grads(layer, left, right_ref, start, width, column):
        for tile in range(0, width, 256):
            size = min(256, width - tile)
            behind.append(
                lambda tile=tile, size=size: keep_tile(
                    layer, left, right_ref, start + tile, size, column + tile
                )
            )

    def grads_kept():
        for slot in range(2):
            if staging[slot] is not None:
                local.wait(staging[slot])
                staging[slot] = None
        scatter.ready += 1

    def fill(count):
        for _ in range(min(count, len(behind))):
            behind.pop(0)()

    def own(piece):
        return pl.ds(pl.multiple_of(at.tensor * OWN + piece * PIECE, PIECE), PIECE)

    def window(piece):
        return pl.ds(piece * PIECE, PIECE)

    here = here_rows(at)
    gains_grad[...] = jnp.zeros_like(gains_grad)
    every = ((0, SEQ_ROWS),)
    dx[0] = grad_out[...].astype(jnp.float32)
    mlp = (dm.at[0], w, g_ref, u_ref, dgu)
    gu_columns = (GATE[0], UP[1])
    spread = None
    for layer in (1, 0):
        if layer == 1:
            collect_out = collector()
            ready("a", "down")
            for piece in range(PIECES):
                rows_partial(0, there_rows(at, piece), a_ref, w, DOWN, part)
                collect_out.other_ready(piece)
            ready("turned")
            keep_grads(layer, turned, a_ref, 0, 1024, DOWN[0])
            behind.append(grads_kept)
            fill(3)
            collect_out.send_over(0)
            collect_out.send_over(1)
            rows_partial(0, here, a_ref, w, DOWN, part)
            collect_out.own_ready()
            fill(len(behind))
            scatter.turn()
            ready("dm", "g", "u")
            hidden_back(every, *mlp)
            ready("n2")
            keep_grads(layer, n2_turned, dgu, 0, 1024, GATE[0])
            behind.append(grads_kept)
            keep_grads(layer, n2_turned, dgu, 1024, 1024, UP[0])
            behind.append(grads_kept)
            fill(5)
            while tables:
                local.wait(tables.pop())
            for piece in range(PIECES):
                total = h_ref[1, window(piece), :] + collect_out.result(piece)
                output[window(piece), :] = total.astype(jnp.bfloat16)
            scatter.turn()
            ready("gu")
            collect = collector()
            for piece in range(PIECES):
                rows_partial(0, there_rows(at, piece), dgu, w, gu_columns, part)
                collect.other_ready(piece)
            fill(1)
            collect.send_over(0)
            collect.send_over(1)
            rows_partial(0, here, dgu, w, gu_columns, part)
            collect.own_ready()
            scatter.turn()
        else:
            spread.near_done()
            ready("down", "g", "u")
            hidden_back(here, *mlp)
            scatter.turn()
            fill(2)
            spread.pass_on(0)
            fill(1)
            collect = collector()
            for piece in range(PIECES):
                spread.far_done(piece)
                hidden_back(there_rows(at, piece), *mlp)
                if piece == 0:
                    ready("gu")
                rows_partial(0, there_rows(at, piece), dgu, w, gu_columns, part)
                collect.other_ready(piece)
                if piece + 1 < PIECES:
                    spread.pass_on(piece + 1)
                    fill(2)
                    scatter.turn()
                collect.send_over(piece)
            rows_partial(0, here, dgu, w, gu_columns, part)
            collect.own_ready()
            fill(len(behind))
            load(0, attn_names)
            ready("a", "n2")
            turn_rows(dm.at[0], turned)
            scatter.turn()
            keep_grads(layer, turned, a_ref, 0, 1024, DOWN[0])
            behind.append(grads_kept)
            keep_grads(layer, n2_turned, dgu, 0, 1024, GATE[0])
            behind.append(grads_kept)
            keep_grads(layer, n2_turned, dgu, 1024, 1024, UP[0])
            behind.append(grads_kept)
        fill(3)
        spread = Spread(wire, at, dm.at[1])
        gain_rows = None
        for piece in range(PIECES):
            normed_grad, gain_row = norm_backward(
                h_ref[layer, window(piece), :],
                gains[pl.ds(2 * layer + 1, 1), :],
                collect.result(piece),
            )
            gain_rows = gain_row if gain_rows is None else gain_rows + gain_row
            dh = dx[0, window(piece), :] + normed_grad
            dx[1, window(piece), :] = dh
            dm[1, own(piece), :] = dh.astype(jnp.bfloat16)
            spread.send(piece)
            if piece + 1 < PIECES:
                fill(2)
        gains_grad[pl.ds(2 * layer + 1, 1), :] = gain_rows
        scatter.turn()
        ready("out")

        def heads_back(rows):
            grad = nn(take(dm.at[1], rows), weight(w, 0, cut(OUT)))
            for head in range(4):
                put(do_ref.at[head], rows, slice(None), head_of(grad, head * HD).astype(jnp.bfloat16))

        spread.near_done()
        heads_back(here)
        fill(4)
        spread.pass_on(0)
        fill(3)
        spread.far_done(0)
        heads_back(there_rows(at, 0))
        scatter.turn()
        spread.pass_on(1)
        fill(len(behind))
        if layer == 1:
            load(0, mlp_names)
        spread.far_done(1)
        heads_back(there_rows(at, 1))
        ready("v", "p", "k", "q")
        attend_back(
            q_ref, k_ref, v_ref, p_ref, do_ref, dk_ref, dv_ref, cosine, sine, dqkv
        )
        collect = collector()
        ready("qkv")
        for piece in range(PIECES):
            rows_partial(0, there_rows(at, piece), dqkv, w, QKV, part)
            collect.other_ready(piece)
        scatter.turn()
        collect.send_over(0)
        collect.send_over(1)
        rows_partial(0, here, dqkv, w, QKV, part)
        collect.own_ready()
        turn_rows(dm.at[1], turned)
        ready("o", "n1")
        keep_grads(layer, turned, o_ref, 0, 384, OUT[0])
        keep_grads(layer, n1_turned, dqkv, 0, 768, QKV[0])
        behind.append(grads_kept)
        fill(6 if layer == 1 else 2)
        if layer == 0:
            scatter.turn()
        rows_in = tokens if layer == 0 else x_second
        spread = Spread(wire, at, dm.at[0]) if layer == 1 else None
        gain_rows = None
        for piece in range(PIECES):
            normed_grad, gain_row = norm_backward(
                rows_in[window(piece), :].astype(jnp.float32),
                gains[pl.ds(2 * layer, 1), :],
                collect.result(piece),
            )
            gain_rows = gain_row if gain_rows is None else gain_rows + gain_row
            dx_rows = dx[1, window(piece), :] + normed_grad
            if layer == 1:
                dx[0, window(piece), :] = dx_rows
                dm[0, own(piece), :] = dx_rows.astype(jnp.bfloat16)
                spread.send(piece)
                if piece == 0:
                    fill(1)
                    scatter.turn()
            else:
                input_grad[window(piece), :] = dx_rows
        gains_grad[pl.ds(2 * layer, 1), :] = gain_rows
    fill(len(behind))
    rounds = sum_small(wire, at, gains_grad, gains_landing, True)
    for _ in rounds:
        scatter.turn()
    while scatter.done < len(scatter.order):
        scatter.step()
    local.drain()
    wire.drain()


def run_backward(gains, grad_out, tokens, cosine, sine, x_second, h, kept):
    def held(*shape, kind=jnp.bfloat16):
        return pltpu.VMEM(shape, kind)

    vmem = pl.BlockSpec(memory_space=pltpu.VMEM)
    hbm = pl.BlockSpec(memory_space=pl.ANY)
    float32 = jnp.float32
    wires = 8 * 26 + 9 + 3 * 6 + 5 * 5
    return pl.pallas_call(
        backward_kernel,
        out_shape=(
            jax.ShapeDtypeStruct((OWN, MODEL), jnp.bfloat16),
            jax.ShapeDtypeStruct((OWN, MODEL), float32),
            jax.ShapeDtypeStruct((2, 48, WIDTH), float32),
            jax.ShapeDtypeStruct((8, MODEL), float32),
            jax.ShapeDtypeStruct((2, 2, SIDE, SIDE, 48, WIDTH), jnp.bfloat16),
        ),
        in_specs=[vmem] * 3 + [hbm] * (4 + len(kept)),
        out_specs=(vmem, vmem, vmem, vmem, hbm),
        scratch_shapes=[
            held(SEQ_ROWS, 384, kind=float32),
            held(SEQ_ROWS, 384, kind=float32),
            held(OWN, MODEL, kind=float32),
            held(2, OWN, MODEL, kind=float32),
            held(1, 2, 768, WIDTH),
            held(MODEL, SEQ_ROWS),
            held(MODEL, SEQ_ROWS),
            held(4, SEQ_ROWS, 128),
            held(2, SEQ_ROWS, 128),
            held(2, SEQ_ROWS, 128),
            held(4, SEQ_ROWS, SEQ_ROWS),
            held(SEQ_ROWS, 384),
            held(SEQ_ROWS, 1024, kind=KEEP),
            held(SEQ_ROWS, 1024, kind=KEEP),
            held(SEQ_ROWS, 1024),
            held(2, SEQ_ROWS, MODEL),
            held(MODEL, SEQ_ROWS),
            held(SEQ_ROWS, 2048),
            held(4, SEQ_ROWS, 128),
            held(2, 128, SEQ_ROWS, kind=float32),
            held(2, 128, SEQ_ROWS, kind=float32),
            held(SEQ_ROWS, 768),
            held(2, OWN, MODEL, kind=float32),
            held(SEQ_ROWS, MODEL),
            held(2, OWN, MODEL),
            held(2, OWN, MODEL),
            held(2, OWN, MODEL),
            held(2, 2, SIDE, SIDE, 48, 256),
            held(SETS, 2, SIDE, 48, JOB_WIDTH),
            held(SETS, 2, SIDE, 48, JOB_WIDTH),
            held(SETS, 2, SIDE, 48, JOB_WIDTH),
            held(SETS, 2, 48, JOB_WIDTH),
            held(SETS, 2, 48, JOB_WIDTH),
            held(SETS, 2, 48, JOB_WIDTH),
            held(1, 2, SIDE, 48, JOB_WIDTH),
            held(1, 2, SIDE, 48, JOB_WIDTH),
            held(8, 48, JOB_WIDTH),
            held(8, 48, JOB_WIDTH),
            held(9, 8, MODEL, kind=float32),
            pltpu.SemaphoreType.DMA((wires,)),
            pltpu.SemaphoreType.DMA((wires,)),
            pltpu.SemaphoreType.DMA((34 + 40 + 48,)),
            pltpu.SemaphoreType.REGULAR((4,)),
        ],
        compiler_params=pltpu.CompilerParams(
            collective_id=1, has_side_effects=True, vmem_limit_bytes=63 * 2**20
        ),
        name="backward",
    )(gains, grad_out, tokens, cosine, sine, x_second, h, *kept)


def pack_rows(arrays):
    query, key, value, out, gate, up, down = arrays
    turned_out = jnp.swapaxes(out, 1, 2)
    turned_down = jnp.swapaxes(down, 1, 2)
    return jnp.concatenate([query, key, value, turned_out, gate, up, turned_down], axis=2)


def body(
    tokens,
    query_weight,
    key_weight,
    value_weight,
    out_weight,
    gate_weight,
    up_weight,
    down_weight,
    norm_gains,
    grad_out,
):
    packed = pack_rows(
        (query_weight, key_weight, value_weight, out_weight, gate_weight, up_weight, down_weight)
    )
    dp = lax.axis_index("dp")
    gains_placed = lax.dynamic_update_slice(
        jnp.zeros((8, MODEL), jnp.float32),
        norm_gains.reshape(4, -1).astype(jnp.float32),
        (0, dp * 48),
    )
    cosine, sine = rope_tables(4)
    w_kept, gains, *kept, x_second, h = run_forward(
        packed, gains_placed, tokens, grad_out, cosine, sine
    )
    output, input_grad, summed, gains_grad, _ = run_backward(
        gains, grad_out, tokens, cosine, sine, x_second, h, (w_kept, *kept)
    )
    gains_own = lax.dynamic_slice(gains_grad, (0, dp * 48), (4, 48)).reshape(2, 2, 48)
    pieces, start = [], 0
    for width in COLS:
        pieces.append(summed[:, :, start : start + width])
        start += width
    query, key, value, out, gate, up, down = pieces
    return (
        output,
        input_grad,
        query,
        key,
        value,
        jnp.swapaxes(out, 1, 2),
        gate,
        up,
        jnp.swapaxes(down, 1, 2),
        gains_own,
    )


def solution(mesh):
    return jax.shard_map(
        body,
        mesh=mesh,
        in_specs=(
            P(("dp", "tensor"), None),
            P(None, "dp", "tensor"),
            P(None, "dp", "tensor"),
            P(None, "dp", "tensor"),
            P(None, "tensor", "dp"),
            P(None, "dp", "tensor"),
            P(None, "dp", "tensor"),
            P(None, "tensor", "dp"),
            P(None, None, "dp"),
            P(("dp", "tensor"), None),
        ),
        out_specs=(
            P(("dp", "tensor"), None),
            P(("dp", "tensor"), None),
            P(None, "dp", "tensor"),
            P(None, "dp", "tensor"),
            P(None, "dp", "tensor"),
            P(None, "tensor", "dp"),
            P(None, "dp", "tensor"),
            P(None, "dp", "tensor"),
            P(None, "tensor", "dp"),
            P(None, None, "dp"),
        ),
        check_vma=False,
    )
```
